32 devices in a mesh: parts: 2 (over x), rep: 8 (over z, y), tp: 2 (over core).
Axes of the slice: x: 2, y: 2, z: 4, core: 2. Of those that a mesh axis runs over, the one named last changes fastest.
Arguments:
- tokens: bfloat16 [4096, 8192], P(('parts', 'rep'), 'tp'), parts along dimension 0, may hold values from -6 to 6
- base_weight: bfloat16 [8192, 1024], P('tp'), may hold values from -0.0625 to 0.0625
- shrink_panels: bfloat16 [32, 8192, 64], P('rep', 'tp'), may hold values from -0.0625 to 0.0625
- expand_panels: bfloat16 [32, 64, 1024], P('rep'), may hold values from -0.75 to 0.75
- adapter_home: int32 [32], replicated, may hold values from 0 to 31, as said below
- fetch_list: int32 [8, 8], replicated, may hold values from 0 to 31, as said below
- seg_len: int32 [16, 8], P(('parts', 'rep')), parts along dimension 0, may hold values from 1 to 64, 256 in all within a row
Outputs:
- projected: bfloat16 [4096, 1024], P(('parts', 'rep'), 'tp'), parts along dimension 0
The draws below stay inside these ranges and needn't reach their ends.
There are 2 independent parts, one for each index of `parts`. The reference program is written for one: setup_inputs(seed, part) draws one part's arguments, and reference() takes and returns one part's arrays. A program takes and returns all parts, laid end to end along the dimension named above; an argument that names none is the same for every part. Nothing has to cross between parts.
Inputs may be any that keep to these rules, and one draw needn't show every extreme that they name: `adapter_home`: a permutation: every adapter has its own storage position. `fetch_list`: each row names 8 different adapters; at most 1 adapters of one row have storage positions with the same value of position // 4, and every row has such a group of exactly 1. `seg_len`: each row sums to 256 and holds one entry of exactly 64.
All inputs are finite; a program needn't handle non-finite values.
Results may differ from the reference program's by a relative error of at most 0.001.
Values may be sent and summed in bfloat16 or wider, within the bound.
No kernel may reach another device: no remote copies, remote signals or barrier semaphores. Data moves between devices by JAX's collectives and lax.ppermute only.
A program may use at most 128 MiB of HBM per device.

```python
import math
import jax
import jax.numpy as jnp
import numpy as np
from jax import lax

D = 8192
RANK = 64
ADP_DEV = 4
TOK_DEV = 256
FETCH = 8
SEGMOST = 64
VALUE_WIDTH = 1024
ADAPTERS = 32
CAP = 1
DECODE_ROWS = 2048
N_REP = 8


def shared_home(key):
    return jax.random.permutation(key, ADAPTERS).astype(jnp.int32)


def draw_adapter_home(key, part):
    placed = shared_home(key)
    return placed


def draw_fetch_list(key, part):
    placed = shared_home(key)
    key = jax.random.fold_in(key, 23)
    inverse = jnp.argsort(placed).astype(jnp.int32)
    order_key, offset_key = jax.random.split(key)
    row_keys = jax.random.split(order_key, N_REP)

    def shuffled(row_key):
        return jax.random.permutation(row_key, N_REP * CAP)
    ordering = jax.vmap(shuffled)(row_keys)[:, :FETCH].astype(jnp.int32)
    owners = ordering % N_REP
    copy_index = ordering // N_REP
    offsets = jax.random.randint(offset_key, (N_REP, N_REP), 0, ADP_DEV).astype(jnp.int32)
    base_offset = jnp.take_along_axis(offsets, owners, axis=1)
    slot_pick = (base_offset + copy_index) % ADP_DEV
    return jnp.take(inverse, owners * ADP_DEV + slot_pick, axis=0).astype(jnp.int32)


def block_levels(own_key, extent, shards, least, largest):
    def one(axis_at, blocks):
        draws = jax.random.uniform(jax.random.fold_in(jax.random.fold_in(own_key, 6), axis_at), (blocks,), jnp.float32, least / len(shards), largest / len(shards))
        return jnp.repeat(jnp.exp(draws), extent[axis_at] // blocks).reshape((-1,) + (1,) * (len(extent) - axis_at - 1))

    loudness = one(*shards[0])
    for cut in shards[1:]:
        loudness = loudness * one(*cut)
    return loudness


def profile(count, total, reach, lean):
    loads = [(1 << 20) // math.isqrt(grade ** lean) + 1 for grade in range(2, count + 1)]
    spare, given = total - reach - (count - 1), [1] * (count - 1)
    while spare > 0:
        movable = [i for i in range(count - 1) if given[i] < reach]
        mass, budget = sum([loads[i] for i in movable]), spare
        for i in movable:
            more = min(reach - given[i], max(1, budget * loads[i] // mass), spare)
            given[i] = given[i] + more
            spare = spare - more
    return np.array([reach] + given)


def uneven_parts(key, amount, total, reach, slope):
    if amount == 2:
        one = jax.random.randint(key, (), max(1, total - reach), min(reach, total - 1) + 1)
        return jnp.stack([one, total - one])
    sizes = jnp.asarray(profile(amount, total, reach, slope), jnp.int32)
    couples = (amount - 1) // 2
    donor, taker = sizes[1:1 + 2 * couples:2], sizes[2:2 + 2 * couples:2]
    margin = jnp.minimum(donor - 1, reach - taker)
    passed = jax.random.randint(jax.random.fold_in(key, 1), (couples,), 0, 1 << 20) % (margin + 1)
    sizes = sizes.at[1:1 + 2 * couples:2].set(donor - passed).at[2:2 + 2 * couples:2].set(taker + passed)
    return sizes[jax.random.permutation(jax.random.fold_in(key, 2), amount)]


def gaussian(own_key, extent, deviation, reach, cuts=(), held_as=jnp.bfloat16):
    level = block_levels(own_key, extent, cuts, -0.22, 0.18) if cuts else 1.0
    entries = jax.random.normal(own_key, extent, jnp.float32) * deviation * level
    return jnp.minimum(jnp.maximum(entries, -reach), reach).astype(held_as)


def setup_inputs(seed: int = 0, part: int = 0) -> dict:
    key_list = jax.random.split(jax.random.key(seed), 8)
    part_splits = jax.random.split(jax.random.fold_in(key_list[7], part), 8)
    tokens = gaussian(part_splits[0], (DECODE_ROWS, D), 1.0, 6.0, ((0, 8), (1, 2)))
    base_weight = gaussian(key_list[1], (D, VALUE_WIDTH), D ** -0.5, 0.0625, ((0, 2),))
    shrink_panels = gaussian(key_list[2], (ADAPTERS, D, RANK), D ** -0.5, 0.0625, ((0, 8), (1, 2)))
    expand_panels = gaussian(key_list[3], (ADAPTERS, RANK, VALUE_WIDTH), RANK ** -0.5, 0.75, ((0, 8),))
    adapter_home = draw_adapter_home(jax.random.fold_in(key_list[7], 71), part)
    fetch_list = draw_fetch_list(jax.random.fold_in(key_list[7], 71), part)
    seg_len = jax.vmap(lambda own: uneven_parts(own, FETCH, TOK_DEV, SEGMOST, 1))(jax.random.split(part_splits[6], N_REP)).reshape((N_REP, FETCH)).astype(jnp.int32)
    return dict(tokens=tokens, base_weight=base_weight, shrink_panels=shrink_panels, expand_panels=expand_panels, adapter_home=adapter_home, fetch_list=fetch_list, seg_len=seg_len)


adapter_scale = 2.0


def reference(tokens, base_weight, shrink_panels, expand_panels, adapter_home, fetch_list, seg_len):
    base_output = jnp.dot(tokens, base_weight, preferred_element_type=jnp.float32)
    stored = jnp.take(adapter_home, fetch_list, axis=0).astype(jnp.int32)
    grouped = tokens.reshape(N_REP, TOK_DEV, D)
    positions = jnp.arange(TOK_DEV, dtype=jnp.int32)

    def replica_term(replica_items):
        rows_block, stored_row, lengths = replica_items
        shrink = jnp.take(shrink_panels, stored_row, axis=0).astype(jnp.float32)
        expand = jnp.take(expand_panels, stored_row, axis=0).astype(jnp.float32)
        seg_ends = jnp.cumsum(lengths).astype(jnp.int32)
        starts = (seg_ends - lengths).astype(jnp.int32)
        member = ((positions[:, None] >= starts[None, :]) & (positions[:, None] < seg_ends[None, :])).astype(jnp.float32)
        scores = jnp.einsum("td,fdr->tfr", rows_block.astype(jnp.float32), shrink, precision=lax.Precision.HIGHEST)
        reduced = jnp.sum(scores * member[:, :, None], axis=1)
        spread = member[:, :, None] * reduced[:, None, :]
        return jnp.einsum("tfr,frc->tc", spread, expand, precision=lax.Precision.HIGHEST)

    adapter_output = lax.map(replica_term, (grouped, stored, seg_len))
    return (base_output + adapter_scale * adapter_output.reshape(DECODE_ROWS, VALUE_WIDTH)).astype(jnp.bfloat16)
```

```python
import functools
import jax
import jax.numpy as jnp
from jax import lax
from jax.experimental import pallas as pl
from jax.experimental.pallas import tpu as pltpu
from jax.sharding import PartitionSpec as P

adapter_scale = 2.0


def pack_kernel(steps, rows, home_ref, fetch_ref, shrink_ref, expand_ref, *refs):
    outs, sems = refs[: len(steps)], refs[len(steps)]
    me, part, half = lax.axis_index("rep"), lax.axis_index("parts"), lax.axis_index("tp")
    per_home, rank, depth = shrink_ref.shape
    listed = fetch_ref.shape[1]
    columns = outs[0].shape[1] - depth
    first = 0 if rows == rank else pl.multiple_of(part * rows, 16)
    left = pl.multiple_of(half * columns, 128)
    copies = []
    for at, step in enumerate(steps):
        peer = me ^ step

        def look(j, slot):
            position = home_ref[fetch_ref[peer, j]]
            return jnp.where(position // per_home == me, position % per_home, slot)

        slot = lax.fori_loop(0, listed, look, jnp.int32(0), unroll=listed <= 8)
        for n, (source, target) in enumerate(
            (
                (shrink_ref.at[slot, pl.ds(first, rows), :], outs[at].at[:, pl.ds(0, depth)]),
                (
                    expand_ref.at[slot, pl.ds(first, rows), pl.ds(left, columns)],
                    outs[at].at[:, pl.ds(depth, columns)],
                ),
            )
        ):
            copy = pltpu.make_async_copy(source, target, sems.at[at, n])
            copy.start()
            copies.append(copy)
    for copy in copies:
        copy.wait()


def pack(steps, rows, columns, adapter_home, fetch_list, panels, expand_panels):
    width = panels.shape[2] + columns
    return pl.pallas_call(
        functools.partial(pack_kernel, steps, rows),
        out_shape=[jax.ShapeDtypeStruct((rows, width), panels.dtype)] * len(steps),
        in_specs=[pl.BlockSpec(memory_space=pltpu.SMEM)] * 2 + [pl.BlockSpec(memory_space=pl.ANY)] * 2,
        out_specs=[pl.BlockSpec(memory_space=pl.ANY)] * len(steps),
        scratch_shapes=[pltpu.SemaphoreType.DMA((len(steps), 2))],
        cost_estimate=pl.CostEstimate(
            flops=0, bytes_accessed=4 * len(steps) * rows * width, transcendentals=0
        ),
    )(adapter_home, fetch_list, panels, expand_panels)


def on_device(tokens, base_weight, shrink_panels, expand_panels, adapter_home, fetch_list, seg_len):
    per_home, depth, rank = shrink_panels.shape
    replicas, parts, cores = lax.axis_size("rep"), lax.axis_size("parts"), lax.axis_size("tp")
    me = lax.axis_index("rep")
    tok_count = tokens.shape[0]
    columns = expand_panels.shape[2] // cores
    panels = jnp.swapaxes(shrink_panels, 1, 2)
    far = tuple(range(replicas // 2, replicas))
    near = tuple(range(1, replicas // 2))
    share = rank // parts

    args = (columns, adapter_home, fetch_list, panels, expand_panels)
    far_send = pack(far, share, *args)
    near_send = pack(near, rank, *args)
    own = pack((0,), rank, *args)[0]

    tokens, far_send, near_send, own = lax.optimization_barrier((tokens, far_send, near_send, own))

    def hop(x, step):
        return lax.ppermute(x, "rep", [(i, i ^ step) for i in range(replicas)])

    def across(x, shift):
        return lax.ppermute(x, "parts", [(i, (i + shift) % parts) for i in range(parts)])

    far_recv = [hop(x, step) for x, step in zip(far_send, far)]
    near_recv = [hop(x, step) for x, step in zip(near_send, near)]
    passed = [[across(x, shift) for x in far_recv] for shift in range(1, parts)]

    stored = jnp.take(adapter_home, lax.dynamic_index_in_dim(fetch_list, me, 0, keepdims=False))
    owners = stored // per_home
    lengths = seg_len[0]
    ordinal = jnp.arange(lengths.shape[0])
    starts = jnp.sum(jnp.where(ordinal[None, :] < ordinal[:, None], lengths[None, :], 0), axis=1)
    rows = jnp.arange(tok_count, dtype=jnp.int32)
    member = (rows[:, None] >= starts[None, :]) & (rows[:, None] < (starts + lengths)[None, :])
    row_owner = jnp.sum(jnp.where(member, owners[None, :], 0), axis=1)

    base_part = jnp.dot(tokens, base_weight, preferred_element_type=jnp.float32)
    base = lax.psum_scatter(base_part, "tp", scatter_dimension=1, tiled=True)

    def low_rank(blocks, steps):
        scores = [
            jnp.where(
                (row_owner == (me ^ step))[:, None],
                lax.dot_general(
                    tokens,
                    block[:, :depth],
                    (((1,), (1,)), ((), ())),
                    preferred_element_type=jnp.float32,
                ),
                0.0,
            )
            for block, step in zip(blocks, steps)
        ]
        scores = jnp.concatenate(scores, axis=1)
        for shift in range(1, cores):
            scores = scores + lax.ppermute(
                scores, "tp", [(i, (i + shift) % cores) for i in range(cores)]
            )
        expand = jnp.concatenate([block[:, depth:] for block in blocks], axis=0)
        return jnp.dot(
            scores,
            expand.astype(jnp.float32),
            precision=lax.Precision.HIGHEST,
            preferred_element_type=jnp.float32,
        )

    lora = low_rank([own] + near_recv, (0,) + near)
    lora = lora + low_rank(far_recv, far)
    for group in passed:
        lora = lora + low_rank(group, far)
    return (base + adapter_scale * lora).astype(jnp.bfloat16)


def solution(mesh):
    return jax.shard_map(
        on_device,
        mesh=mesh,
        in_specs=(
            P(("parts", "rep"), "tp"),
            P("tp", None),
            P("rep", "tp", None),
            P("rep", None, None),
            P(),
            P(),
            P(("parts", "rep"), None),
        ),
        out_specs=P(("parts", "rep"), "tp"),
        check_vma=False,
    )
```

```python
import functools
import jax
import jax.numpy as jnp
from jax import lax
from jax.experimental import pallas as pl
from jax.experimental.pallas import tpu as pltpu
from jax.sharding import PartitionSpec as P

adapter_scale = 2.0


def pack_kernel(plan, home_ref, fetch_ref, shrink_ref, expand_ref, *refs):
    outs, sems = refs[:-1], refs[-1]
    me, part, half = lax.axis_index("rep"), lax.axis_index("parts"), lax.axis_index("tp")
    per_home, rank, depth = shrink_ref.shape
    listed = fetch_ref.shape[1]
    columns = outs[0].shape[1] - depth
    left = pl.multiple_of(half * columns, 128)
    copies, slots = [], {}
    for at, (step, first, rows, share) in enumerate(plan):
        peer = me ^ step

        def look(j, slot):
            position = home_ref[fetch_ref[peer, j]]
            return jnp.where(position // per_home == me, position % per_home, slot)

        if step not in slots:
            slots[step] = lax.fori_loop(0, listed, look, jnp.int32(0), unroll=listed <= 8)
        slot = slots[step]
        start = pl.multiple_of(part * share + first, 16)
        for n, (source, target) in enumerate(
            (
                (shrink_ref.at[slot, pl.ds(start, rows), :], outs[at].at[:, pl.ds(0, depth)]),
                (
                    expand_ref.at[slot, pl.ds(start, rows), pl.ds(left, columns)],
                    outs[at].at[:, pl.ds(depth, columns)],
                ),
            )
        ):
            copy = pltpu.make_async_copy(source, target, sems.at[at, n])
            copy.start()
            copies.append(copy)
    for copy in copies:
        copy.wait()


def pack(plan, columns, adapter_home, fetch_list, panels, expand_panels):
    width = panels.shape[2] + columns
    size = 2 * width * sum(rows for _, _, rows, _ in plan)
    return pl.pallas_call(
        functools.partial(pack_kernel, plan),
        out_shape=[jax.ShapeDtypeStruct((rows, width), panels.dtype) for _, _, rows, _ in plan],
        in_specs=[pl.BlockSpec(memory_space=pltpu.SMEM)] * 2 + [pl.BlockSpec(memory_space=pl.ANY)] * 2,
        out_specs=[pl.BlockSpec(memory_space=pltpu.VMEM)] * len(plan),
        scratch_shapes=[pltpu.SemaphoreType.DMA((len(plan), 2))],
        compiler_params=pltpu.CompilerParams(vmem_limit_bytes=2 * size + (1 << 20)),
        cost_estimate=pl.CostEstimate(flops=0, bytes_accessed=2 * size, transcendentals=0),
    )(adapter_home, fetch_list, panels, expand_panels)


def on_device(tokens, base_weight, shrink_panels, expand_panels, adapter_home, fetch_list, seg_len):
    per_home, depth, rank = shrink_panels.shape
    replicas, parts, cores = lax.axis_size("rep"), lax.axis_size("parts"), lax.axis_size("tp")
    me = lax.axis_index("rep")
    tok_count = tokens.shape[0]
    columns = expand_panels.shape[2] // cores
    panels = jnp.swapaxes(shrink_panels, 1, 2)
    share = rank // parts

    shared = [step for step in range(replicas // 2, replicas)]
    shared += [step for step in range(2, replicas // 2)]
    order = shared[: replicas // 2 - 1] + shared[replicas // 2 :] + shared[replicas // 2 - 1 : replicas // 2]
    cut = max(16, share // 2)
    plan = [(step, 0, share, share) for step in order[:-1]]
    plan += [(order[-1], first, cut, share) for first in range(0, share, cut)]
    window = 2

    args = (columns, adapter_home, fetch_list, panels, expand_panels)
    first_send = pack(plan[:window], *args)
    panels, first_send = lax.optimization_barrier((panels, first_send))
    args = (columns, adapter_home, fetch_list, panels, expand_panels)
    *rest_send, whole_send, own = pack(plan[window:] + [(1, 0, rank, 0), (0, 0, rank, 0)], *args)
    tokens, rest_send, whole_send, own = lax.optimization_barrier(
        (tokens, rest_send, whole_send, own)
    )
    send = list(first_send) + list(rest_send)

    def hop(x, step):
        return lax.ppermute(x, "rep", [(i, i ^ step) for i in range(replicas)])

    def across(x, shift):
        return lax.ppermute(x, "parts", [(i, (i + shift) % parts) for i in range(parts)])

    received = []
    whole = hop(whole_send, 1)
    for at, (step, *_) in enumerate(plan):
        block = send[at]
        if at >= window:
            block, received[at - window] = lax.optimization_barrier((block, received[at - window]))
        if at == len(plan) // 2:
            block, whole = lax.optimization_barrier((block, whole))
        received.append(hop(block, step))
    passed = [[across(x, shift) for shift in range(1, parts)] for x in received]

    stored = jnp.take(adapter_home, lax.dynamic_index_in_dim(fetch_list, me, 0, keepdims=False))
    owners = stored // per_home
    lengths = seg_len[0]
    ordinal = jnp.arange(lengths.shape[0])
    starts = jnp.sum(jnp.where(ordinal[None, :] < ordinal[:, None], lengths[None, :], 0), axis=1)
    rows = jnp.arange(tok_count, dtype=jnp.int32)
    member = (rows[:, None] >= starts[None, :]) & (rows[:, None] < (starts + lengths)[None, :])
    row_owner = jnp.sum(jnp.where(member, owners[None, :], 0), axis=1)

    base_part = jnp.dot(tokens, base_weight, preferred_element_type=jnp.float32)
    base = lax.psum_scatter(base_part, "tp", scatter_dimension=1, tiled=True)

    def low_rank(blocks):
        scores = [
            jnp.where(
                (row_owner == (me ^ step))[:, None],
                lax.dot_general(
                    tokens,
                    block[:, :depth],
                    (((1,), (1,)), ((), ())),
                    preferred_element_type=jnp.float32,
                ),
                0.0,
            )
            for step, block in blocks
        ]
        scores = jnp.concatenate(scores, axis=1)
        for shift in range(1, cores):
            scores = scores + lax.ppermute(
                scores, "tp", [(i, (i + shift) % cores) for i in range(cores)]
            )
        expand = jnp.concatenate([block[:, depth:] for _, block in blocks], axis=0)
        return jnp.dot(
            scores,
            expand.astype(jnp.float32),
            precision=lax.Precision.HIGHEST,
            preferred_element_type=jnp.float32,
        )

    steps = [step for step, *_ in plan]
    late = len(plan) - 2
    lora = low_rank([(0, own), (1, whole)] + list(zip(steps[:late], received[:late])))
    lora = lora + low_rank(
        [(step, x) for step, group in zip(steps[:late], passed[:late]) for x in group]
    )
    lora = lora + low_rank(
        list(zip(steps[late:], received[late:]))
        + [(step, x) for step, group in zip(steps[late:], passed[late:]) for x in group]
    )
    return (base + adapter_scale * lora).astype(jnp.bfloat16)


def solution(mesh):
    return jax.shard_map(
        on_device,
        mesh=mesh,
        in_specs=(
            P(("parts", "rep"), "tp"),
            P("tp", None),
            P("rep", "tp", None),
            P("rep", None, None),
            P(),
            P(),
            P(("parts", "rep"), None),
        ),
        out_specs=P(("parts", "rep"), "tp"),
        check_vma=False,
    )
```

```python
import functools
import jax
import jax.numpy as jnp
from jax import lax
from jax.experimental import pallas as pl
from jax.experimental.pallas import tpu as pltpu
from jax.sharding import PartitionSpec as P

adapter_scale = 2.0


def pack_kernel(plan, home_ref, fetch_ref, shrink_ref, expand_ref, *refs):
    outs, sems = refs[:-1], refs[-1]
    me, part, half = lax.axis_index("rep"), lax.axis_index("parts"), lax.axis_index("tp")
    per_home, rank, depth = shrink_ref.shape
    listed = fetch_ref.shape[1]
    columns = outs[0].shape[1] - depth
    left = pl.multiple_of(half * columns, 128)
    copies, slots = [], {}
    for at, (step, first, rows, share) in enumerate(plan):
        peer = me ^ step

        def look(j, slot):
            position = home_ref[fetch_ref[peer, j]]
            return jnp.where(position // per_home == me, position % per_home, slot)

        if step not in slots:
            slots[step] = lax.fori_loop(0, listed, look, jnp.int32(0), unroll=listed <= 8)
        slot = slots[step]
        start = pl.multiple_of(part * share + first, 16)
        for n, (source, target) in enumerate(
            (
                (shrink_ref.at[slot, pl.ds(start, rows), :], outs[at].at[:, pl.ds(0, depth)]),
                (
                    expand_ref.at[slot, pl.ds(start, rows), pl.ds(left, columns)],
                    outs[at].at[:, pl.ds(depth, columns)],
                ),
            )
        ):
            copy = pltpu.make_async_copy(source, target, sems.at[at, n])
            copy.start()
            copies.append(copy)
    for copy in copies:
        copy.wait()


def pack(plan, columns, adapter_home, fetch_list, panels, expand_panels):
    width = panels.shape[2] + columns
    size = 2 * width * sum(rows for _, _, rows, _ in plan)
    return pl.pallas_call(
        functools.partial(pack_kernel, plan),
        out_shape=[jax.ShapeDtypeStruct((rows, width), panels.dtype) for _, _, rows, _ in plan],
        in_specs=[pl.BlockSpec(memory_space=pltpu.SMEM)] * 2 + [pl.BlockSpec(memory_space=pl.ANY)] * 2,
        out_specs=[pl.BlockSpec(memory_space=pltpu.VMEM)] * len(plan),
        scratch_shapes=[pltpu.SemaphoreType.DMA((len(plan), 2))],
        compiler_params=pltpu.CompilerParams(vmem_limit_bytes=56 << 20),
        cost_estimate=pl.CostEstimate(flops=0, bytes_accessed=2 * size, transcendentals=0),
    )(adapter_home, fetch_list, panels, expand_panels)


def on_device(tokens, base_weight, shrink_panels, expand_panels, adapter_home, fetch_list, seg_len):
    per_home, depth, rank = shrink_panels.shape
    replicas, parts, cores = lax.axis_size("rep"), lax.axis_size("parts"), lax.axis_size("tp")
    me = lax.axis_index("rep")
    tok_count = tokens.shape[0]
    columns = expand_panels.shape[2] // cores
    panels = jnp.swapaxes(shrink_panels, 1, 2)
    share = rank // parts

    half = replicas // 2
    cut = max(16, share // 2)
    far = [(step, 0, share, share) for step in range(half, replicas - 1)]
    far += [(replicas - 1, first, cut, share) for first in range(0, share, cut)]
    near = [(step, 0, share, share) for step in range(2, half)]
    plan = far + near + [(1, 0, rank, 0), (0, 0, rank, 0)]
    send = pack(plan, columns, adapter_home, fetch_list, panels, expand_panels)
    tokens, send = lax.optimization_barrier((tokens, list(send)))
    far_send, near_send = send[: len(far)], send[len(far) : -2]
    whole_send, own = send[-2:]

    def hop(x, step):
        return lax.ppermute(x, "rep", [(i, i ^ step) for i in range(replicas)])

    def across(x):
        return [
            lax.ppermute(x, "parts", [(i, (i + shift) % parts) for i in range(parts)])
            for shift in range(1, parts)
        ]

    def trade(x):
        for shift in range(1, cores):
            x = x + lax.ppermute(x, "tp", [(i, (i + shift) % cores) for i in range(cores)])
        return x

    stored = jnp.take(adapter_home, lax.dynamic_index_in_dim(fetch_list, me, 0, keepdims=False))
    owners = stored // per_home
    lengths = seg_len[0]
    ordinal = jnp.arange(lengths.shape[0])
    starts = jnp.sum(jnp.where(ordinal[None, :] < ordinal[:, None], lengths[None, :], 0), axis=1)
    rows = jnp.arange(tok_count, dtype=jnp.int32)
    member = (rows[:, None] >= starts[None, :]) & (rows[:, None] < (starts + lengths)[None, :])
    row_owner = jnp.sum(jnp.where(member, owners[None, :], 0), axis=1)

    def score(block, step, tokens):
        product = lax.dot_general(
            tokens, block[:, :depth], (((1,), (1,)), ((), ())), preferred_element_type=jnp.float32
        )
        return jnp.where((row_owner == (me ^ step))[:, None], product, 0.0)

    def spread(scores, blocks):
        return jnp.dot(
            trade(jnp.concatenate(scores, axis=1)),
            jnp.concatenate([block[:, depth:] for block in blocks], axis=0).astype(jnp.float32),
            precision=lax.Precision.HIGHEST,
            preferred_element_type=jnp.float32,
        )

    tie = lax.optimization_barrier
    window = 2
    far_recv = [hop(far_send[at], far[at][0]) for at in range(window)]
    near_recv = [hop(near_send[0], near[0][0])]
    for at in range(window, len(far)):
        block = far_send[at]
        before = at - window
        if before < len(near):
            block, near_recv[before] = tie((block, near_recv[before]))
        if at == len(far) - 1:
            block, far_recv[before:] = tie((block, far_recv[before:]))
        else:
            block, far_recv[before] = tie((block, far_recv[before]))
        far_recv.append(hop(block, far[at][0]))
        if before + 1 < len(near):
            block, near_recv[before] = tie((near_send[before + 1], near_recv[before]))
            near_recv.append(hop(block, near[before + 1][0]))
    whole_send, near_recv[-1] = tie((whole_send, near_recv[-1]))
    whole = hop(whole_send, 1)

    arrived = [(x, step) for x, (step, *_) in zip(far_recv, far)]
    arrived_near = [(x, step) for x, (step, *_) in zip(near_recv, near)]
    arrived = arrived_near[:1] + arrived[:window] + arrived_near[1:] + arrived[window:]
    base_part = jnp.dot(tokens, base_weight, preferred_element_type=jnp.float32)
    base = lax.psum_scatter(base_part, "tp", scatter_dimension=1, tiled=True)

    done_scores, done_blocks, passed = [], [], []

    def multiply(blocks, step):
        for block in blocks:
            done_scores.append(score(block, step, tokens))
            done_blocks.append(block)

    multiply([own], 0)
    for at, (block, step) in enumerate(arrived):
        if at >= window:
            block, passed[at - window] = tie((block, passed[at - window]))
        block, done_scores = tie((block, done_scores))
        passed.append(across(block))
        multiply([block], step)
        if at >= window:
            multiply(passed[at - window], arrived[at - window][1])
        if at == len(arrived) - 2:
            multiply([whole], 1)
    for at in range(len(arrived) - window, len(arrived) - 1):
        multiply(passed[at], arrived[at][1])
    done_scores = tie(done_scores)
    total = base + adapter_scale * spread(done_scores, done_blocks)
    tokens, total = tie((tokens, total))
    last = [score(block, arrived[-1][1], tokens) for block in passed[-1]]
    total = total + adapter_scale * spread(last, passed[-1])
    return total.astype(jnp.bfloat16)


def solution(mesh):
    return jax.shard_map(
        on_device,
        mesh=mesh,
        in_specs=(
            P(("parts", "rep"), "tp"),
            P("tp", None),
            P("rep", "tp", None),
            P("rep", None, None),
            P(),
            P(),
            P(("parts", "rep"), None),
        ),
        out_specs=P(("parts", "rep"), "tp"),
        check_vma=False,
    )
```

```python
import functools
import jax
import jax.numpy as jnp
from jax import lax
from jax.experimental import pallas as pl
from jax.experimental.pallas import tpu as pltpu
from jax.sharding import PartitionSpec as P

adapter_scale = 2.0


def pack_kernel(groups, home_ref, fetch_ref, shrink_ref, expand_ref, *refs):
    outs, sems = refs[:-1], refs[-1]
    me, part, half = lax.axis_index("rep"), lax.axis_index("parts"), lax.axis_index("tp")
    per_home = shrink_ref.shape[0]
    listed = fetch_ref.shape[1]
    copies = []
    for at, (group, kind) in enumerate(groups):
        step = jnp.int32(group[0])
        for p, other in enumerate(group):
            step = jnp.where(part == p, other, step)
        peer = me ^ step

        def look(j, slot):
            position = home_ref[fetch_ref[peer, j]]
            return jnp.where(position // per_home == me, position % per_home, slot)

        slot = lax.fori_loop(0, listed, look, jnp.int32(0), unroll=listed <= 8)
        if kind == "shrink":
            source = shrink_ref.at[slot]
        else:
            columns = outs[at].shape[1]
            source = expand_ref.at[slot, :, pl.ds(pl.multiple_of(half * columns, 128), columns)]
        copy = pltpu.make_async_copy(source, outs[at], sems.at[at])
        copy.start()
        copies.append(copy)
    for copy in copies:
        copy.wait()


def pack(groups, columns, adapter_home, fetch_list, panels, expand_panels):
    rank, depth = panels.shape[1:]
    widths = [depth if kind == "shrink" else columns for _, kind in groups]
    return list(
        pl.pallas_call(
            functools.partial(pack_kernel, groups),
            out_shape=[jax.ShapeDtypeStruct((rank, width), panels.dtype) for width in widths],
            in_specs=[pl.BlockSpec(memory_space=pltpu.SMEM)] * 2 + [pl.BlockSpec(memory_space=pl.ANY)] * 2,
            out_specs=[pl.BlockSpec(memory_space=pltpu.VMEM)] * len(groups),
            scratch_shapes=[pltpu.SemaphoreType.DMA((len(groups),))],
            compiler_params=pltpu.CompilerParams(vmem_limit_bytes=56 << 20),
            cost_estimate=pl.CostEstimate(
                flops=0, bytes_accessed=4 * rank * sum(widths), transcendentals=0
            ),
        )(adapter_home, fetch_list, panels, expand_panels)
    )


def on_device(tokens, base_weight, shrink_panels, expand_panels, adapter_home, fetch_list, seg_len):
    per_home = shrink_panels.shape[0]
    replicas, parts, cores = lax.axis_size("rep"), lax.axis_size("parts"), lax.axis_size("tp")
    me, part = lax.axis_index("rep"), lax.axis_index("parts")
    tok_count = tokens.shape[0]
    columns = expand_panels.shape[2] // cores
    panels = jnp.swapaxes(shrink_panels, 1, 2)
    tie = lax.optimization_barrier

    alone, half = max(2, parts), replicas // 2

    def grouped(steps):
        size = len(steps) // parts
        return [tuple(steps[p * size + g] for p in range(parts)) for g in range(size)]

    far = grouped(list(range(half, replicas)))
    near = grouped(list(range(alone, half)))
    groups = far + near
    solo = [(step,) * parts for step in range(1, alone)]

    def hop(x, group):
        pairs = [
            (p * replicas + i, p * replicas + (i ^ group[p]))
            for p in range(parts)
            for i in range(replicas)
        ]
        return lax.ppermute(x, ("parts", "rep"), pairs)

    def shift_parts(x, shift, turn=0):
        pairs = [
            (p * cores + t, ((p + shift) % parts) * cores + (t + turn) % cores)
            for p in range(parts)
            for t in range(cores)
        ]
        return lax.ppermute(x, ("parts", "tp"), pairs)

    def packed(kind, groups, panels):
        kinds = [(group, kind) for group in groups]
        return pack(kinds, columns, adapter_home, fetch_list, panels, expand_panels)

    others = near + solo
    own_group = (0,) * parts
    far_send = packed("shrink", far, panels)
    panels, far_send = tie((panels, far_send))
    near_send = packed("shrink", others, panels)
    tokens, far_send, near_send = tie((tokens, far_send, near_send))

    far_recv = [hop(x, group) for x, group in zip(far_send, far)]
    tokens_of = [tokens] + [shift_parts(tokens, shift) for shift in range(1, parts)]
    near_recv = [hop(x, group) for x, group in zip(near_send, others)]
    panels, seg_len, near_recv = tie((panels, seg_len, near_recv))
    own, *expand_send = pack(
        [(own_group, "shrink")] + [(group, "expand") for group in far + others + [own_group]],
        columns,
        adapter_home,
        fetch_list,
        panels,
        expand_panels,
    )
    own_expand = expand_send.pop()
    expand_recv = [hop(x, group) for x, group in zip(expand_send, far)]
    seg_len, expand_send, expand_recv = tie((seg_len, expand_send, expand_recv))
    lengths_of = [seg_len[0]] + [shift_parts(seg_len, shift)[0] for shift in range(1, parts)]
    expand_recv += [hop(x, group) for x, group in zip(expand_send[len(far) :], others)]

    stored = jnp.take(adapter_home, lax.dynamic_index_in_dim(fetch_list, me, 0, keepdims=False))
    steps = (stored // per_home) ^ me
    rows = jnp.arange(tok_count, dtype=jnp.int32)

    def steps_of_rows(lengths):
        ordinal = jnp.arange(lengths.shape[0])
        starts = jnp.sum(jnp.where(ordinal[None, :] < ordinal[:, None], lengths[None, :], 0), axis=1)
        member = (rows[:, None] >= starts[None, :]) & (rows[:, None] < (starts + lengths)[None, :])
        return jnp.sum(jnp.where(member, steps[None, :], 0), axis=1)[:, None]

    row_steps = [steps_of_rows(lengths) for lengths in lengths_of]

    def step_of(group, shift=0):
        step = jnp.int32(0)
        for p in range(parts):
            step = jnp.where(part == p, group[(p - shift) % parts], step)
        return step

    def score(block, step, shift):
        product = lax.dot_general(
            tokens_of[shift], block, (((1,), (1,)), ((), ())), preferred_element_type=jnp.float32
        )
        return jnp.where(row_steps[shift] == step, product, 0.0)

    base_part = jnp.dot(tokens, base_weight, preferred_element_type=jnp.float32)
    base = lax.psum_scatter(base_part, "tp", scatter_dimension=1, tiled=True)

    count = len(far) + len(near)
    expands = [own_expand] + expand_recv
    expand_steps = [0] + [step_of(group) for group in far + others]
    mine = jnp.concatenate(expand_recv[:count], axis=0)
    for shift in range(1, parts):
        expands.append(shift_parts(mine, shift))
        expand_steps += [step_of(group, shift) for group in far + near]
    expand = jnp.concatenate(expands, axis=0).astype(jnp.float32)

    scores = [score(own, 0, 0)] + [None] * (parts - 1)
    for block, group in zip(near_recv[len(near) :], solo):
        scores[0] = scores[0] + score(block, group[0], 0)
    for at, (block, group) in enumerate(zip(near_recv[: len(near)] + far_recv, near + far)):
        if at == len(near):
            tokens_of, expand, scores = tie((tokens_of, expand, scores))
        for shift in range(parts):
            term = score(block, step_of(group), shift)
            scores[shift] = term if scores[shift] is None else scores[shift] + term
    shrink = scores[0]
    for turn in range(cores):
        for shift in range(parts):
            if shift or turn:
                shrink = shrink + shift_parts(scores[shift], -shift, turn)
    wide = jnp.concatenate(
        [jnp.where(row_steps[0] == step, shrink, 0.0) for step in expand_steps], axis=1
    )
    lora = jnp.dot(
        wide, expand, precision=lax.Precision.HIGHEST, preferred_element_type=jnp.float32
    )
    return (base + adapter_scale * lora).astype(jnp.bfloat16)


def solution(mesh):
    return jax.shard_map(
        on_device,
        mesh=mesh,
        in_specs=(
            P(("parts", "rep"), "tp"),
            P("tp", None),
            P("rep", "tp", None),
            P("rep", None, None),
            P(),
            P(),
            P(("parts", "rep"), None),
        ),
        out_specs=P(("parts", "rep"), "tp"),
        check_vma=False,
    )
```

```python
import functools
import jax
import jax.numpy as jnp
from jax import lax
from jax.experimental import pallas as pl
from jax.experimental.pallas import tpu as pltpu
from jax.sharding import PartitionSpec as P

adapter_scale = 2.0


def pack_kernel(blocks, home_ref, fetch_ref, shrink_ref, expand_ref, *refs):
    outs, sems = refs[:-1], refs[-1]
    me, part, half = lax.axis_index("rep"), lax.axis_index("parts"), lax.axis_index("tp")
    per_home, _, depth = shrink_ref.shape
    columns = expand_ref.shape[2] // lax.axis_size("tp")
    listed = fetch_ref.shape[1]
    copies, slots = [], {}
    for at, (group, shrink, expand) in enumerate(blocks):
        if group not in slots:
            step = jnp.int32(group[0])
            for p, other in enumerate(group):
                step = jnp.where(part == p, other, step)
            peer = me ^ step

            def look(j, slot):
                position = home_ref[fetch_ref[peer, j]]
                return jnp.where(position // per_home == me, position % per_home, slot)

            slots[group] = lax.fori_loop(0, listed, look, jnp.int32(0), unroll=listed <= 8)
        slot = slots[group]
        pieces = []
        if shrink:
            pieces.append((shrink_ref.at[slot], outs[at].at[:, pl.ds(0, depth)]))
        if expand:
            left = pl.multiple_of(half * columns, 128)
            pieces.append(
                (
                    expand_ref.at[slot, :, pl.ds(left, columns)],
                    outs[at].at[:, pl.ds(depth * shrink, columns)],
                )
            )
        for n, (source, target) in enumerate(pieces):
            copy = pltpu.make_async_copy(source, target, sems.at[at, n])
            copy.start()
            copies.append(copy)
    for copy in copies:
        copy.wait()


def pack(blocks, columns, adapter_home, fetch_list, panels, expand_panels):
    rank, depth = panels.shape[1:]
    shapes = [(rank, depth * shrink + columns * expand) for _, shrink, expand in blocks]
    return list(
        pl.pallas_call(
            functools.partial(pack_kernel, blocks),
            out_shape=[jax.ShapeDtypeStruct(shape, panels.dtype) for shape in shapes],
            in_specs=[pl.BlockSpec(memory_space=pltpu.SMEM)] * 2 + [pl.BlockSpec(memory_space=pl.ANY)] * 2,
            out_specs=[pl.BlockSpec(memory_space=pltpu.VMEM)] * len(blocks),
            scratch_shapes=[pltpu.SemaphoreType.DMA((len(blocks), 2))],
            compiler_params=pltpu.CompilerParams(vmem_limit_bytes=56 << 20),
            cost_estimate=pl.CostEstimate(
                flops=0, bytes_accessed=4 * sum(r * w for r, w in shapes), transcendentals=0
            ),
        )(adapter_home, fetch_list, panels, expand_panels)
    )


def on_device(tokens, base_weight, shrink_panels, expand_panels, adapter_home, fetch_list, seg_len):
    per_home, depth, _ = shrink_panels.shape
    replicas, parts, cores = lax.axis_size("rep"), lax.axis_size("parts"), lax.axis_size("tp")
    me, part = lax.axis_index("rep"), lax.axis_index("parts")
    tok_count = tokens.shape[0]
    columns = expand_panels.shape[2] // cores
    panels = jnp.swapaxes(shrink_panels, 1, 2)
    tie = lax.optimization_barrier

    alone, half = max(2, parts), replicas // 2

    def grouped(steps):
        size = len(steps) // parts
        return [tuple(steps[p * size + g] for p in range(parts)) for g in range(size)]

    far = grouped(list(range(half, replicas)))
    near = grouped(list(range(alone, half)))
    groups = far + near
    solo = [(step,) * parts for step in range(1, alone)]

    def hop(x, group):
        pairs = [
            (p * replicas + i, p * replicas + (i ^ group[p]))
            for p in range(parts)
            for i in range(replicas)
        ]
        return lax.ppermute(x, ("parts", "rep"), pairs)

    def shift_parts(x, shift, turn=0):
        pairs = [
            (p * cores + t, ((p + shift) % parts) * cores + (t + turn) % cores)
            for p in range(parts)
            for t in range(cores)
        ]
        return lax.ppermute(x, ("parts", "tp"), pairs)

    rank = panels.shape[1]
    others, own_group = near + solo, (0,) * parts
    tables = (columns, adapter_home, fetch_list, panels, expand_panels)
    blocks = [(group, True, True) for group in others + far[:-1]]
    blocks += [(far[-1], True, False), (far[-1], False, True)]
    send = pack(blocks, *tables)
    tokens, send = tie((tokens, send))
    last_expand = hop(send.pop(), far[-1])
    recv = [hop(x, group) for x, group in zip(send[:-1], others + far[:-1])]
    last_send, last_expand = tie((send[-1], last_expand))
    recv.append(hop(last_send, far[-1]))
    every_tokens = lax.all_gather(tokens, "parts", axis=0, tiled=True)
    every_seg_len = lax.all_gather(seg_len, "parts", axis=0, tiled=True)
    base_part = jnp.dot(tokens, base_weight, preferred_element_type=jnp.float32)
    base = lax.psum_scatter(base_part, "tp", scatter_dimension=1, tiled=True)
    panels, base_part = tie((panels, base_part))
    tables = (columns, adapter_home, fetch_list, panels, expand_panels)
    (own,) = pack([(own_group, True, True)], *tables)

    stored = jnp.take(adapter_home, lax.dynamic_index_in_dim(fetch_list, me, 0, keepdims=False))
    steps = (stored // per_home) ^ me
    rows = jnp.arange(tok_count, dtype=jnp.int32)

    def steps_of_rows(lengths):
        ends = jnp.cumsum(lengths, axis=1)[:, None, :]
        starts = ends - lengths[:, None, :]
        member = (rows[None, :, None] >= starts) & (rows[None, :, None] < ends)
        return jnp.sum(jnp.where(member, steps[None, None, :], 0), axis=2).reshape(-1, 1)

    row_steps, every_row_steps = steps_of_rows(seg_len), steps_of_rows(every_seg_len)

    def step_of(group, shift=0):
        step = jnp.int32(0)
        for p in range(parts):
            step = jnp.where(part == p, group[(p - shift) % parts], step)
        return step

    def score(block, step, tokens, row_steps):
        product = lax.dot_general(
            tokens,
            block[:, :depth],
            (((1,), (1,)), ((), ())),
            preferred_element_type=jnp.float32,
        )
        return jnp.where(row_steps == step, product, 0.0)

    def total(scores, solo_scores=None):
        shrink = solo_scores
        for shift in range(parts):
            at = ((part + shift) % parts) * tok_count
            piece = lax.dynamic_slice_in_dim(scores, at, tok_count, 0)
            if shift == 0 and solo_scores is not None:
                piece = piece + solo_scores
            for turn in range(cores):
                term = shift_parts(piece, shift, turn) if shift or turn else piece
                shrink = term if shift == 0 and turn == 0 else shrink + term
        return shrink

    def spread(shrink, steps, expands):
        wide = jnp.concatenate([jnp.where(row_steps == step, shrink, 0.0) for step in steps], axis=1)
        return adapter_scale * jnp.dot(
            wide,
            jnp.concatenate(expands, axis=0).astype(jnp.float32),
            precision=lax.Precision.HIGHEST,
            preferred_element_type=jnp.float32,
        )

    shared = recv[: len(near)] + recv[len(others) :]
    shared_groups = near + far
    mine = [x[:, depth:] for x in shared[:-1]] + [last_expand]
    alone_blocks = [own] + recv[len(near) : len(others)]
    alone_steps = [0] + [group[0] for group in solo]
    expands = [x[:, depth:] for x in alone_blocks] + mine[:-1]
    expand_steps = alone_steps + [step_of(group) for group in shared_groups[:-1]]
    last_expands, last_steps = mine[-1:], [step_of(far[-1])]
    sent = jnp.concatenate(mine, axis=0)
    for shift in range(1, parts):
        came = shift_parts(sent, shift)
        expands.append(came[:-rank])
        expand_steps += [step_of(group, shift) for group in shared_groups[:-1]]
        last_expands.append(came[-rank:])
        last_steps.append(step_of(far[-1], shift))

    solo_scores = sum(
        score(block, step, tokens, row_steps) for block, step in zip(alone_blocks, alone_steps)
    )
    scores = sum(
        score(block, step_of(group), every_tokens, every_row_steps)
        for block, group in zip(shared[:-1], shared_groups)
    )
    result = base + spread(total(scores, solo_scores), expand_steps, expands)

    every_tokens, result, last_expands = tie((every_tokens, result, last_expands))
    scores = score(shared[-1], step_of(far[-1]), every_tokens, every_row_steps)
    result = result + spread(total(scores), last_steps, last_expands)
    return result.astype(jnp.bfloat16)


def solution(mesh):
    return jax.shard_map(
        on_device,
        mesh=mesh,
        in_specs=(
            P(("parts", "rep"), "tp"),
            P("tp", None),
            P("rep", "tp", None),
            P("rep", None, None),
            P(),
            P(),
            P(("parts", "rep"), None),
        ),
        out_specs=P(("parts", "rep"), "tp"),
        check_vma=False,
    )
```

```python
import functools
import jax
import jax.numpy as jnp
from jax import lax
from jax.experimental import pallas as pl
from jax.experimental.pallas import tpu as pltpu
from jax.sharding import PartitionSpec as P

adapter_scale = 2.0


def pack_kernel(blocks, home_ref, fetch_ref, shrink_ref, expand_ref, *refs):
    outs, sems = refs[:-1], refs[-1]
    me, part, half = lax.axis_index("rep"), lax.axis_index("parts"), lax.axis_index("tp")
    per_home, _, depth = shrink_ref.shape
    columns = expand_ref.shape[2] // lax.axis_size("tp")
    listed = fetch_ref.shape[1]
    copies, slots = [], {}
    for at, (group, first, rows) in enumerate(blocks):
        if group not in slots:
            step = jnp.int32(group[0])
            for p, other in enumerate(group):
                step = jnp.where(part == p, other, step)
            peer = me ^ step

            def look(j, slot):
                position = home_ref[fetch_ref[peer, j]]
                return jnp.where(position // per_home == me, position % per_home, slot)

            slots[group] = lax.fori_loop(0, listed, look, jnp.int32(0), unroll=listed <= 8)
        slot = slots[group]
        left = pl.multiple_of(half * columns, 128)
        pieces = (
            (shrink_ref.at[slot, pl.ds(first, rows)], outs[at].at[:, pl.ds(0, depth)]),
            (
                expand_ref.at[slot, pl.ds(first, rows), pl.ds(left, columns)],
                outs[at].at[:, pl.ds(depth, columns)],
            ),
        )
        for n, (source, target) in enumerate(pieces):
            copy = pltpu.make_async_copy(source, target, sems.at[at, n])
            copy.start()
            copies.append(copy)
    for copy in copies:
        copy.wait()


def pack(blocks, columns, adapter_home, fetch_list, panels, expand_panels):
    shapes = [(rows, panels.shape[2] + columns) for _, _, rows in blocks]
    return list(
        pl.pallas_call(
            functools.partial(pack_kernel, blocks),
            out_shape=[jax.ShapeDtypeStruct(shape, panels.dtype) for shape in shapes],
            in_specs=[pl.BlockSpec(memory_space=pltpu.SMEM)] * 2 + [pl.BlockSpec(memory_space=pl.ANY)] * 2,
            out_specs=[pl.BlockSpec(memory_space=pltpu.VMEM)] * len(blocks),
            scratch_shapes=[pltpu.SemaphoreType.DMA((len(blocks), 2))],
            compiler_params=pltpu.CompilerParams(vmem_limit_bytes=56 << 20),
            cost_estimate=pl.CostEstimate(
                flops=0, bytes_accessed=4 * sum(r * w for r, w in shapes), transcendentals=0
            ),
        )(adapter_home, fetch_list, panels, expand_panels)
    )


def on_device(tokens, base_weight, shrink_panels, expand_panels, adapter_home, fetch_list, seg_len):
    per_home, depth, _ = shrink_panels.shape
    replicas, parts, cores = lax.axis_size("rep"), lax.axis_size("parts"), lax.axis_size("tp")
    me, part = lax.axis_index("rep"), lax.axis_index("parts")
    tok_count = tokens.shape[0]
    columns = expand_panels.shape[2] // cores
    panels = jnp.swapaxes(shrink_panels, 1, 2)
    tie = lax.optimization_barrier

    alone, half = max(2, parts), replicas // 2

    def grouped(steps):
        size = len(steps) // parts
        return [tuple(steps[p * size + g] for p in range(parts)) for g in range(size)]

    far = grouped(list(range(half, replicas)))
    near = grouped(list(range(alone, half)))
    groups = far + near
    solo = [(step,) * parts for step in range(1, alone)]

    def hop(x, group):
        pairs = [
            (p * replicas + i, p * replicas + (i ^ group[p]))
            for p in range(parts)
            for i in range(replicas)
        ]
        return lax.ppermute(x, ("parts", "rep"), pairs)

    def across(x):
        return [
            lax.ppermute(x, "parts", [(i, (i + shift) % parts) for i in range(parts)])
            for shift in range(1, parts)
        ]

    def trade(x):
        for shift in range(1, cores):
            x = x + lax.ppermute(x, "tp", [(i, (i + shift) % cores) for i in range(cores)])
        return x

    rank = panels.shape[1]
    cut = rank - 16
    early = near + solo + far[:-1]
    tables = (columns, adapter_home, fetch_list, panels, expand_panels)
    send = pack([(group, 0, rank) for group in early], *tables)
    tokens, send = tie((tokens, send))
    recv = [hop(x, group) for x, group in zip(send, early)]
    base_part = jnp.dot(tokens, base_weight, preferred_element_type=jnp.float32)
    base = lax.psum_scatter(base_part, "tp", scatter_dimension=1, tiled=True)
    panels, base_part = tie((panels, base_part))
    tables = (columns, adapter_home, fetch_list, panels, expand_panels)
    last_low, last_high, own = pack(
        [(far[-1], 0, cut), (far[-1], cut, rank - cut), ((0,) * parts, 0, rank)], *tables
    )
    last_low, recv[: len(near)] = tie((last_low, recv[: len(near)]))
    last_low = hop(last_low, far[-1])
    passed = [across(x) for x in recv[: len(near)]]
    last_high, recv[len(near) :] = tie((last_high, recv[len(near) :]))
    last_high = hop(last_high, far[-1])
    passed += [across(x) for x in recv[len(near) + len(solo) :] + [last_low]]
    last_passed = across(last_high)

    stored = jnp.take(adapter_home, lax.dynamic_index_in_dim(fetch_list, me, 0, keepdims=False))
    steps = (stored // per_home) ^ me
    lengths = seg_len[0]
    ordinal = jnp.arange(lengths.shape[0])
    starts = jnp.sum(jnp.where(ordinal[None, :] < ordinal[:, None], lengths[None, :], 0), axis=1)
    rows = jnp.arange(tok_count, dtype=jnp.int32)
    member = (rows[:, None] >= starts[None, :]) & (rows[:, None] < (starts + lengths)[None, :])
    row_steps = jnp.sum(jnp.where(member, steps[None, :], 0), axis=1)[:, None]

    def step_of(group, shift=0):
        step = jnp.int32(0)
        for p in range(parts):
            step = jnp.where(part == p, group[(p - shift) % parts], step)
        return step

    def score(block, step, tokens):
        product = lax.dot_general(
            tokens,
            block[:, :depth],
            (((1,), (1,)), ((), ())),
            preferred_element_type=jnp.float32,
        )
        return jnp.where(row_steps == step, product, 0.0)

    def spread(scores, blocks):
        return adapter_scale * jnp.dot(
            trade(jnp.concatenate(scores, axis=1)),
            jnp.concatenate([block[:, depth:] for block in blocks], axis=0).astype(jnp.float32),
            precision=lax.Precision.HIGHEST,
            preferred_element_type=jnp.float32,
        )

    blocks = [(own, 0)] + [(x, step_of(group)) for x, group in zip(recv, early)]
    blocks += [(last_low, step_of(far[-1])), (last_high, step_of(far[-1]))]
    for group, came in zip(near + far, passed):
        blocks += [(x, step_of(group, shift + 1)) for shift, x in enumerate(came)]
    scores = tie([score(block, step, tokens) for block, step in blocks])
    result = base + spread(scores, [block for block, _ in blocks])
    tokens, result = tie((tokens, result))
    scores = [score(x, step_of(far[-1], shift + 1), tokens) for shift, x in enumerate(last_passed)]
    result = result + spread(scores, last_passed)
    return result.astype(jnp.bfloat16)


def solution(mesh):
    return jax.shard_map(
        on_device,
        mesh=mesh,
        in_specs=(
            P(("parts", "rep"), "tp"),
            P("tp", None),
            P("rep", "tp", None),
            P("rep", None, None),
            P(),
            P(),
            P(("parts", "rep"), None),
        ),
        out_specs=P(("parts", "rep"), "tp"),
        check_vma=False,
    )
```

```python
import functools
import jax
import jax.numpy as jnp
from jax import lax
from jax.experimental import pallas as pl
from jax.experimental.pallas import tpu as pltpu
from jax.sharding import PartitionSpec as P

adapter_scale = 2.0


def pack_kernel(blocks, home_ref, fetch_ref, shrink_ref, expand_ref, *refs):
    outs, sems = refs[:-1], refs[-1]
    me, part, half = lax.axis_index("rep"), lax.axis_index("parts"), lax.axis_index("tp")
    per_home, _, depth = shrink_ref.shape
    columns = expand_ref.shape[2] // lax.axis_size("tp")
    listed = fetch_ref.shape[1]
    copies, slots = [], {}
    for at, (group, first, rows) in enumerate(blocks):
        if group not in slots:
            step = jnp.int32(group[0])
            for p, other in enumerate(group):
                step = jnp.where(part == p, other, step)
            peer = me ^ step

            def look(j, slot):
                position = home_ref[fetch_ref[peer, j]]
                return jnp.where(position // per_home == me, position % per_home, slot)

            slots[group] = lax.fori_loop(0, listed, look, jnp.int32(0), unroll=listed <= 8)
        slot = slots[group]
        left = pl.multiple_of(half * columns, 128)
        pieces = (
            (shrink_ref.at[slot, pl.ds(first, rows)], outs[at].at[:, pl.ds(0, depth)]),
            (
                expand_ref.at[slot, pl.ds(first, rows), pl.ds(left, columns)],
                outs[at].at[:, pl.ds(depth, columns)],
            ),
        )
        for n, (source, target) in enumerate(pieces):
            copy = pltpu.make_async_copy(source, target, sems.at[at, n])
            copy.start()
            copies.append(copy)
    for copy in copies:
        copy.wait()


def pack(blocks, columns, adapter_home, fetch_list, panels, expand_panels):
    shapes = [(rows, panels.shape[2] + columns) for _, _, rows in blocks]
    return list(
        pl.pallas_call(
            functools.partial(pack_kernel, blocks),
            out_shape=[jax.ShapeDtypeStruct(shape, panels.dtype) for shape in shapes],
            in_specs=[pl.BlockSpec(memory_space=pltpu.SMEM)] * 2 + [pl.BlockSpec(memory_space=pl.ANY)] * 2,
            out_specs=[pl.BlockSpec(memory_space=pltpu.VMEM)] * len(blocks),
            scratch_shapes=[pltpu.SemaphoreType.DMA((len(blocks), 2))],
            compiler_params=pltpu.CompilerParams(vmem_limit_bytes=56 << 20),
            cost_estimate=pl.CostEstimate(
                flops=0, bytes_accessed=4 * sum(r * w for r, w in shapes), transcendentals=0
            ),
        )(adapter_home, fetch_list, panels, expand_panels)
    )


def on_device(tokens, base_weight, shrink_panels, expand_panels, adapter_home, fetch_list, seg_len):
    per_home, depth, _ = shrink_panels.shape
    replicas, parts, cores = lax.axis_size("rep"), lax.axis_size("parts"), lax.axis_size("tp")
    me, part = lax.axis_index("rep"), lax.axis_index("parts")
    tok_count = tokens.shape[0]
    columns = expand_panels.shape[2] // cores
    panels = jnp.swapaxes(shrink_panels, 1, 2)
    tie = lax.optimization_barrier

    alone, half = max(2, parts), replicas // 2

    def grouped(steps):
        size = len(steps) // parts
        return [tuple(steps[p * size + g] for p in range(parts)) for g in range(size)]

    far = grouped(list(range(half, replicas)))
    near = grouped(list(range(alone, half)))
    groups = far + near
    solo = [(step,) * parts for step in range(1, alone)]

    def hop(x, group):
        pairs = [
            (p * replicas + i, p * replicas + (i ^ group[p]))
            for p in range(parts)
            for i in range(replicas)
        ]
        return lax.ppermute(x, ("parts", "rep"), pairs)

    def across(x):
        return [
            lax.ppermute(x, "parts", [(i, (i + shift) % parts) for i in range(parts)])
            for shift in range(1, parts)
        ]

    def trade(x):
        for shift in range(1, cores):
            x = x + lax.ppermute(x, "tp", [(i, (i + shift) % cores) for i in range(cores)])
        return x

    rank = panels.shape[1]
    cut = rank - 16
    early = near + far[:-1] + solo
    tables = (columns, adapter_home, fetch_list, panels, expand_panels)
    send = pack([(group, 0, rank) for group in early], *tables)
    tokens, send = tie((tokens, send))
    recv = [hop(x, group) for x, group in zip(send[: -len(solo)], early)]
    near_recv, far_recv = recv[: len(near)], recv[len(near) :]
    base_part = jnp.dot(tokens, base_weight, preferred_element_type=jnp.float32)
    base = lax.psum_scatter(base_part, "tp", scatter_dimension=1, tiled=True)
    panels, base_part = tie((panels, base_part))
    tables = (columns, adapter_home, fetch_list, panels, expand_panels)
    last_low, last_high, own = pack(
        [(far[-1], 0, cut), (far[-1], cut, rank - cut), ((0,) * parts, 0, rank)], *tables
    )
    last_low, solo_send, near_recv = tie((last_low, send[-len(solo) :], near_recv))
    last_low = hop(last_low, far[-1])
    solo_recv = [hop(x, group) for x, group in zip(solo_send, solo)]
    passed = [across(x) for x in near_recv]
    last_high, passed = tie((last_high, passed))
    last_high = hop(last_high, far[-1])
    passed += [across(x) for x in far_recv + [last_low]]
    last_passed = across(last_high)

    stored = jnp.take(adapter_home, lax.dynamic_index_in_dim(fetch_list, me, 0, keepdims=False))
    steps = (stored // per_home) ^ me
    lengths = seg_len[0]
    ordinal = jnp.arange(lengths.shape[0])
    starts = jnp.sum(jnp.where(ordinal[None, :] < ordinal[:, None], lengths[None, :], 0), axis=1)
    rows = jnp.arange(tok_count, dtype=jnp.int32)
    member = (rows[:, None] >= starts[None, :]) & (rows[:, None] < (starts + lengths)[None, :])
    row_steps = jnp.sum(jnp.where(member, steps[None, :], 0), axis=1)[:, None]

    def step_of(group, shift=0):
        step = jnp.int32(0)
        for p in range(parts):
            step = jnp.where(part == p, group[(p - shift) % parts], step)
        return step

    def score(block, step, tokens):
        product = lax.dot_general(
            tokens,
            block[:, :depth],
            (((1,), (1,)), ((), ())),
            preferred_element_type=jnp.float32,
        )
        return jnp.where(row_steps == step, product, 0.0)

    def spread(scores, blocks):
        return adapter_scale * jnp.dot(
            trade(jnp.concatenate(scores, axis=1)),
            jnp.concatenate([block[:, depth:] for block in blocks], axis=0).astype(jnp.float32),
            precision=lax.Precision.HIGHEST,
            preferred_element_type=jnp.float32,
        )

    blocks = [(own, 0)] + [(x, step_of(group)) for x, group in zip(near_recv + far_recv + solo_recv, early)]
    blocks += [(last_low, step_of(far[-1])), (last_high, step_of(far[-1]))]
    for group, came in zip(near + far, passed):
        blocks += [(x, step_of(group, shift + 1)) for shift, x in enumerate(came)]
    scores = tie([score(block, step, tokens) for block, step in blocks])
    result = base + spread(scores, [block for block, _ in blocks])
    tokens, result = tie((tokens, result))
    scores = [score(x, step_of(far[-1], shift + 1), tokens) for shift, x in enumerate(last_passed)]
    result = result + spread(scores, last_passed)
    return result.astype(jnp.bfloat16)


def solution(mesh):
    return jax.shard_map(
        on_device,
        mesh=mesh,
        in_specs=(
            P(("parts", "rep"), "tp"),
            P("tp", None),
            P("rep", "tp", None),
            P("rep", None, None),
            P(),
            P(),
            P(("parts", "rep"), None),
        ),
        out_specs=P(("parts", "rep"), "tp"),
        check_vma=False,
    )
```

```python
import functools
import jax
import jax.numpy as jnp
from jax import lax
from jax.experimental import pallas as pl
from jax.experimental.pallas import tpu as pltpu
from jax.sharding import PartitionSpec as P

adapter_scale = 2.0


def pack_kernel(blocks, home_ref, fetch_ref, shrink_ref, expand_ref, *refs):
    outs, sems = refs[:-1], refs[-1]
    me, part, half = lax.axis_index("rep"), lax.axis_index("parts"), lax.axis_index("tp")
    per_home, _, depth = shrink_ref.shape
    columns = expand_ref.shape[2] // lax.axis_size("tp")
    left = pl.multiple_of(half * columns, 128)
    listed = fetch_ref.shape[1]
    copies, slots = [], {}
    for at, (group, shrink, expand) in enumerate(blocks):
        if group not in slots:
            step = jnp.int32(group[0])
            for p, other in enumerate(group):
                step = jnp.where(part == p, other, step)
            peer = me ^ step

            def look(j, slot):
                position = home_ref[fetch_ref[peer, j]]
                return jnp.where(position // per_home == me, position % per_home, slot)

            slots[group] = lax.fori_loop(0, listed, look, jnp.int32(0), unroll=listed <= 8)
        slot = slots[group]
        pieces = []
        if shrink:
            pieces.append((shrink_ref.at[slot], outs[at].at[:, pl.ds(0, depth)]))
        if expand:
            target = outs[at].at[:, pl.ds(depth * shrink, columns)]
            pieces.append((expand_ref.at[slot, :, pl.ds(left, columns)], target))
        for n, (source, target) in enumerate(pieces):
            copies.append(pltpu.make_async_copy(source, target, sems.at[at, n]))
            copies[-1].start()
    for copy in copies:
        copy.wait()


def pack(blocks, columns, adapter_home, fetch_list, panels, expand_panels):
    rank, depth = panels.shape[1:]
    shapes = [(rank, depth * shrink + columns * expand) for _, shrink, expand in blocks]
    return list(
        pl.pallas_call(
            functools.partial(pack_kernel, blocks),
            out_shape=[jax.ShapeDtypeStruct(shape, panels.dtype) for shape in shapes],
            in_specs=[pl.BlockSpec(memory_space=pltpu.SMEM)] * 2 + [pl.BlockSpec(memory_space=pl.ANY)] * 2,
            out_specs=[pl.BlockSpec(memory_space=pltpu.VMEM)] * len(blocks),
            scratch_shapes=[pltpu.SemaphoreType.DMA((len(blocks), 2))],
            compiler_params=pltpu.CompilerParams(vmem_limit_bytes=56 << 20),
            cost_estimate=pl.CostEstimate(
                flops=0, bytes_accessed=4 * sum(r * w for r, w in shapes), transcendentals=0
            ),
        )(adapter_home, fetch_list, panels, expand_panels)
    )


def on_device(tokens, base_weight, shrink_panels, expand_panels, adapter_home, fetch_list, seg_len):
    per_home, depth, _ = shrink_panels.shape
    replicas, parts, cores = lax.axis_size("rep"), lax.axis_size("parts"), lax.axis_size("tp")
    me, part = lax.axis_index("rep"), lax.axis_index("parts")
    tok_count = tokens.shape[0]
    columns = expand_panels.shape[2] // cores
    panels = jnp.swapaxes(shrink_panels, 1, 2)
    tie = lax.optimization_barrier

    alone, half = max(2, parts), replicas // 2

    def grouped(steps):
        size = len(steps) // parts
        return [tuple(steps[p * size + g] for p in range(parts)) for g in range(size)]

    far = grouped(list(range(half, replicas)))
    near = grouped(list(range(alone, half)))
    groups = far + near
    solo = [(step,) * parts for step in range(1, alone)]

    def hop(x, group):
        pairs = [
            (p * replicas + i, p * replicas + (i ^ group[p]))
            for p in range(parts)
            for i in range(replicas)
        ]
        return lax.ppermute(x, ("parts", "rep"), pairs)

    def shift_parts(x, shift, turn=0):
        pairs = [
            (p * cores + t, ((p + shift) % parts) * cores + (t + turn) % cores)
            for p in range(parts)
            for t in range(cores)
        ]
        return lax.ppermute(x, ("parts", "tp"), pairs)

    rank = panels.shape[1]
    others = near + solo
    blocks = [(group, False, True) for group in far] + [(group, True, False) for group in far]
    blocks += [(group, True, True) for group in others]
    send = pack(blocks, columns, adapter_home, fetch_list, panels, expand_panels)
    tokens, send = tie((tokens, send))
    count = len(far)
    far_expand = [hop(x, group) for x, group in zip(send, far)]
    far_recv = [hop(x, group) for x, group in zip(send[count:], far)]
    tokens_of = [tokens] + [shift_parts(tokens, shift) for shift in range(1, parts)]
    other_send, far_expand = tie((send[2 * count :], far_expand))
    recv = [hop(x, group) for x, group in zip(other_send, others)]
    base_part = jnp.dot(tokens, base_weight, preferred_element_type=jnp.float32)
    base = lax.psum_scatter(base_part, "tp", scatter_dimension=1, tiled=True)
    panels, base_part = tie((panels, base_part))
    tables = (columns, adapter_home, fetch_list, panels, expand_panels)
    (own,) = pack([((0,) * parts, True, True)], *tables)

    def step_of(group, shift=0):
        step = jnp.int32(0)
        for p in range(parts):
            step = jnp.where(part == p, group[(p - shift) % parts], step)
        return step

    mine = [x[:, depth:] for x in recv[: len(near)]] + far_expand
    expands = [own[:, depth:]] + [x[:, depth:] for x in recv[len(near) :]] + mine
    expand_steps = [0] + [group[0] for group in solo] + [step_of(group) for group in near + far]
    sent = jnp.concatenate(mine, axis=0)
    for shift in range(1, parts):
        expands.append(shift_parts(sent, shift))
        expand_steps += [step_of(group, shift) for group in near + far]
    expand = jnp.concatenate(expands, axis=0)
    lengths_of = [seg_len[0]]
    for shift in range(1, parts):
        seg_len, tokens_of[shift] = tie((seg_len, tokens_of[shift]))
        lengths_of.append(shift_parts(seg_len, shift)[0])

    stored = jnp.take(adapter_home, lax.dynamic_index_in_dim(fetch_list, me, 0, keepdims=False))
    steps = (stored // per_home) ^ me
    rows = jnp.arange(tok_count, dtype=jnp.int32)

    def steps_of_rows(lengths):
        ordinal = jnp.arange(lengths.shape[0])
        starts = jnp.sum(jnp.where(ordinal[None, :] < ordinal[:, None], lengths[None, :], 0), axis=1)
        member = (rows[:, None] >= starts[None, :]) & (rows[:, None] < (starts + lengths)[None, :])
        return jnp.sum(jnp.where(member, steps[None, :], 0), axis=1)[:, None]

    row_steps = [steps_of_rows(lengths) for lengths in lengths_of]

    def score(block, step, shift):
        product = lax.dot_general(
            tokens_of[shift],
            block[:, :depth],
            (((1,), (1,)), ((), ())),
            preferred_element_type=jnp.float32,
        )
        return jnp.where(row_steps[shift] == step, product, 0.0)

    scores = [score(own, 0, 0)] + [0.0] * (parts - 1)
    for block, group in zip(recv[len(near) :], solo):
        scores[0] = scores[0] + score(block, group[0], 0)
    for block, group in zip(recv, near):
        for shift in range(parts):
            scores[shift] = scores[shift] + score(block, step_of(group), shift)
    tokens_of, scores, expand, base = tie((tokens_of, scores, expand, base))
    for block, group in zip(far_recv, far):
        for shift in range(parts):
            scores[shift] = scores[shift] + score(block, step_of(group), shift)
    shrink = scores[0]
    for turn in range(cores):
        for shift in range(parts):
            if shift or turn:
                shrink = shrink + shift_parts(scores[shift], -shift, turn)
    wide = jnp.concatenate(
        [jnp.where(row_steps[0] == step, shrink, 0.0) for step in expand_steps], axis=1
    )
    lora = jnp.dot(
        wide,
        expand.astype(jnp.float32),
        precision=lax.Precision.HIGHEST,
        preferred_element_type=jnp.float32,
    )
    return (base + adapter_scale * lora).astype(jnp.bfloat16)


def solution(mesh):
    return jax.shard_map(
        on_device,
        mesh=mesh,
        in_specs=(
            P(("parts", "rep"), "tp"),
            P("tp", None),
            P("rep", "tp", None),
            P("rep", None, None),
            P(),
            P(),
            P(("parts", "rep"), None),
        ),
        out_specs=P(("parts", "rep"), "tp"),
        check_vma=False,
    )
```

```python
import functools
import jax
import jax.numpy as jnp
from jax import lax
from jax.experimental import pallas as pl
from jax.experimental.pallas import tpu as pltpu
from jax.sharding import PartitionSpec as P

adapter_scale = 2.0


def pack_kernel(blocks, home_ref, fetch_ref, shrink_ref, expand_ref, *refs):
    outs, sems = refs[:-1], refs[-1]
    me, part, half = lax.axis_index("rep"), lax.axis_index("parts"), lax.axis_index("tp")
    per_home, _, depth = shrink_ref.shape
    columns = expand_ref.shape[2] // lax.axis_size("tp")
    left = pl.multiple_of(half * columns, 128)
    listed = fetch_ref.shape[1]
    copies, slots = [], {}
    for at, (group, shrink, expand) in enumerate(blocks):
        if group not in slots:
            step = jnp.int32(group[0])
            for p, other in enumerate(group):
                step = jnp.where(part == p, other, step)
            peer = me ^ step

            def look(j, slot):
                position = home_ref[fetch_ref[peer, j]]
                return jnp.where(position // per_home == me, position % per_home, slot)

            slots[group] = lax.fori_loop(0, listed, look, jnp.int32(0), unroll=listed <= 8)
        slot = slots[group]
        pieces = []
        if shrink:
            pieces.append((shrink_ref.at[slot], outs[at].at[:, pl.ds(0, depth)]))
        if expand:
            target = outs[at].at[:, pl.ds(depth * shrink, columns)]
            pieces.append((expand_ref.at[slot, :, pl.ds(left, columns)], target))
        for n, (source, target) in enumerate(pieces):
            copies.append(pltpu.make_async_copy(source, target, sems.at[at, n]))
            copies[-1].start()
    for copy in copies:
        copy.wait()


def pack(blocks, columns, adapter_home, fetch_list, panels, expand_panels):
    rank, depth = panels.shape[1:]
    shapes = [(rank, depth * shrink + columns * expand) for _, shrink, expand in blocks]
    return list(
        pl.pallas_call(
            functools.partial(pack_kernel, blocks),
            out_shape=[jax.ShapeDtypeStruct(shape, panels.dtype) for shape in shapes],
            in_specs=[pl.BlockSpec(memory_space=pltpu.SMEM)] * 2 + [pl.BlockSpec(memory_space=pl.ANY)] * 2,
            out_specs=[pl.BlockSpec(memory_space=pltpu.VMEM)] * len(blocks),
            scratch_shapes=[pltpu.SemaphoreType.DMA((len(blocks), 2))],
            compiler_params=pltpu.CompilerParams(vmem_limit_bytes=56 << 20),
            cost_estimate=pl.CostEstimate(
                flops=0, bytes_accessed=4 * sum(r * w for r, w in shapes), transcendentals=0
            ),
        )(adapter_home, fetch_list, panels, expand_panels)
    )


def on_device(tokens, base_weight, shrink_panels, expand_panels, adapter_home, fetch_list, seg_len):
    per_home, depth, _ = shrink_panels.shape
    replicas, parts, cores = lax.axis_size("rep"), lax.axis_size("parts"), lax.axis_size("tp")
    me, part = lax.axis_index("rep"), lax.axis_index("parts")
    tok_count = tokens.shape[0]
    columns = expand_panels.shape[2] // cores
    panels = jnp.swapaxes(shrink_panels, 1, 2)
    tie = lax.optimization_barrier

    alone, half = max(2, parts), replicas // 2

    def grouped(steps):
        size = len(steps) // parts
        return [tuple(steps[p * size + g] for p in range(parts)) for g in range(size)]

    far = grouped(list(range(half, replicas)))
    near = grouped(list(range(alone, half)))
    groups = far + near
    solo = [(step,) * parts for step in range(1, alone)]

    def hop(x, group):
        pairs = [
            (p * replicas + i, p * replicas + (i ^ group[p]))
            for p in range(parts)
            for i in range(replicas)
        ]
        return lax.ppermute(x, ("parts", "rep"), pairs)

    def shift_parts(x, shift):
        return lax.ppermute(x, "parts", [(i, (i + shift) % parts) for i in range(parts)])

    def trade(x):
        for shift in range(1, cores):
            x = x + lax.ppermute(x, "tp", [(i, (i + shift) % cores) for i in range(cores)])
        return x

    rank = panels.shape[1]
    groups = far + near + solo
    blocks = [(group, True, True) for group in groups]
    send = pack(blocks, columns, adapter_home, fetch_list, panels, expand_panels)
    tokens, send = tie((tokens, send))
    recv = [hop(x, group) for x, group in zip(send, groups)]
    tokens_of = [tokens] + [shift_parts(tokens, shift) for shift in range(1, parts)]
    base_part = jnp.dot(tokens, base_weight, preferred_element_type=jnp.float32)
    base = lax.psum_scatter(base_part, "tp", scatter_dimension=1, tiled=True)

    stored = jnp.take(adapter_home, lax.dynamic_index_in_dim(fetch_list, me, 0, keepdims=False))
    steps = (stored // per_home) ^ me
    slot = jnp.sum(jnp.where(steps == 0, stored % per_home, 0))
    own = lax.dynamic_index_in_dim(panels, slot, 0, keepdims=False)
    left = lax.axis_index("tp") * columns
    own_expand = lax.dynamic_slice(expand_panels, (slot, 0, left), (1, rank, columns))[0]
    far_recv, near_recv = recv[: len(far)], recv[len(far) : len(far) + len(near)]
    solo_recv = recv[len(far) + len(near) :]
    early, early_groups = near_recv + far_recv[:-1], near + far[:-1]

    def step_of(group, shift=0):
        step = jnp.int32(0)
        for p in range(parts):
            step = jnp.where(part == p, group[(p - shift) % parts], step)
        return step

    expands = [own_expand] + [x[:, depth:] for x in solo_recv + early]
    expand_steps = [0] + [group[0] for group in solo] + [step_of(group) for group in early_groups]
    sent = jnp.concatenate([x[:, depth:] for x in early], axis=0)
    for shift in range(1, parts):
        expands.append(shift_parts(sent, shift))
        expand_steps += [step_of(group, shift) for group in early_groups]
    expand = jnp.concatenate(expands, axis=0)

    lengths_of = [seg_len[0]]
    for shift in range(1, parts):
        seg_len, tokens_of[shift] = tie((seg_len, tokens_of[shift]))
        lengths_of.append(shift_parts(seg_len, shift)[0])
    rows = jnp.arange(tok_count, dtype=jnp.int32)

    def steps_of_rows(lengths):
        ordinal = jnp.arange(lengths.shape[0])
        starts = jnp.sum(jnp.where(ordinal[None, :] < ordinal[:, None], lengths[None, :], 0), axis=1)
        member = (rows[:, None] >= starts[None, :]) & (rows[:, None] < (starts + lengths)[None, :])
        return jnp.sum(jnp.where(member, steps[None, :], 0), axis=1)[None, :]

    row_steps = [steps_of_rows(lengths) for lengths in lengths_of]

    def score(block, step, shift):
        product = lax.dot_general(
            block[:, :depth],
            tokens_of[shift],
            (((1,), (1,)), ((), ())),
            preferred_element_type=jnp.float32,
        )
        return jnp.where(row_steps[shift] == step, product, 0.0)

    scores = [score(own, 0, 0)] + [0.0] * (parts - 1)
    for block, group in zip(solo_recv, solo):
        scores[0] = scores[0] + score(block, group[0], 0)
    for block, group in zip(early, early_groups):
        for shift in range(parts):
            scores[shift] = scores[shift] + score(block, step_of(group), shift)
    tokens_of, scores, expand, base, far_recv[-1] = tie(
        (tokens_of, scores, expand, base, far_recv[-1])
    )
    last_expand = far_recv[-1][:, depth:]
    expands = [expand, last_expand] + [shift_parts(last_expand, shift) for shift in range(1, parts)]
    expand_steps += [step_of(far[-1], shift) for shift in range(parts)]
    for shift in range(parts):
        scores[shift] = scores[shift] + score(far_recv[-1], step_of(far[-1]), shift)
    scores, expands = tie((scores, expands))
    scores = trade(jnp.concatenate(scores, axis=1))
    shrink = scores[:, :tok_count]
    for shift in range(1, parts):
        shrink = shrink + shift_parts(scores[:, shift * tok_count : (shift + 1) * tok_count], -shift)
    wide = jnp.concatenate(
        [jnp.where(row_steps[0] == step, shrink, 0.0) for step in expand_steps], axis=0
    )
    lora = lax.dot_general(
        wide,
        jnp.concatenate(expands, axis=0).astype(jnp.float32),
        (((0,), (0,)), ((), ())),
        precision=lax.Precision.HIGHEST,
        preferred_element_type=jnp.float32,
    )
    return (base + adapter_scale * lora).astype(jnp.bfloat16)


def solution(mesh):
    return jax.shard_map(
        on_device,
        mesh=mesh,
        in_specs=(
            P(("parts", "rep"), "tp"),
            P("tp", None),
            P("rep", "tp", None),
            P("rep", None, None),
            P(),
            P(),
            P(("parts", "rep"), None),
        ),
        out_specs=P(("parts", "rep"), "tp"),
        check_vma=False,
    )
```

```python
import functools
import jax
import jax.numpy as jnp
from jax import lax
from jax.experimental import pallas as pl
from jax.experimental.pallas import tpu as pltpu
from jax.sharding import PartitionSpec as P

adapter_scale = 2.0


def pack_kernel(blocks, home_ref, fetch_ref, shrink_ref, expand_ref, *refs):
    outs, sems = refs[:-1], refs[-1]
    me, part, half = lax.axis_index("rep"), lax.axis_index("parts"), lax.axis_index("tp")
    per_home, _, depth = shrink_ref.shape
    columns = expand_ref.shape[2] // lax.axis_size("tp")
    left = pl.multiple_of(half * columns, 128)
    listed = fetch_ref.shape[1]
    copies, slots = [], {}
    for at, (group, shrink, expand) in enumerate(blocks):
        if group not in slots:
            step = jnp.int32(group[0])
            for p, other in enumerate(group):
                step = jnp.where(part == p, other, step)
            peer = me ^ step

            def look(j, slot):
                position = home_ref[fetch_ref[peer, j]]
                return jnp.where(position // per_home == me, position % per_home, slot)

            slots[group] = lax.fori_loop(0, listed, look, jnp.int32(0), unroll=listed <= 8)
        slot = slots[group]
        pieces = []
        if shrink:
            pieces.append((shrink_ref.at[slot], outs[at].at[:, pl.ds(0, depth)]))
        if expand:
            target = outs[at].at[:, pl.ds(depth * shrink, columns)]
            pieces.append((expand_ref.at[slot, :, pl.ds(left, columns)], target))
        for n, (source, target) in enumerate(pieces):
            copies.append(pltpu.make_async_copy(source, target, sems.at[at, n]))
            copies[-1].start()
    for copy in copies:
        copy.wait()


def pack(blocks, columns, adapter_home, fetch_list, panels, expand_panels):
    rank, depth = panels.shape[1:]
    shapes = [(rank, depth * shrink + columns * expand) for _, shrink, expand in blocks]
    return list(
        pl.pallas_call(
            functools.partial(pack_kernel, blocks),
            out_shape=[jax.ShapeDtypeStruct(shape, panels.dtype) for shape in shapes],
            in_specs=[pl.BlockSpec(memory_space=pltpu.SMEM)] * 2 + [pl.BlockSpec(memory_space=pl.ANY)] * 2,
            out_specs=[pl.BlockSpec(memory_space=pltpu.VMEM)] * len(blocks),
            scratch_shapes=[pltpu.SemaphoreType.DMA((len(blocks), 2))],
            compiler_params=pltpu.CompilerParams(vmem_limit_bytes=56 << 20),
            cost_estimate=pl.CostEstimate(
                flops=0, bytes_accessed=4 * sum(r * w for r, w in shapes), transcendentals=0
            ),
        )(adapter_home, fetch_list, panels, expand_panels)
    )


def score_kernel(parts, shared, alone, scalars, *refs):
    row_steps = refs[0]
    tokens, panels = refs[1 : 1 + parts], refs[1 + parts : 1 + parts + shared + alone]
    out, sums = refs[1 + parts + shared + alone], refs[2 + parts + shared + alone :]
    at = pl.program_id(0)
    blocks = [x[...] if len(x.shape) == 2 else x[0] for x in panels]
    stack = jnp.concatenate(blocks, axis=0)
    rank, count = blocks[0].shape[0], out.shape[1] // parts
    for shift in range(parts):
        left = stack if shift == 0 else stack[: shared * rank]
        product = lax.dot_general(
            left, tokens[shift][...], (((1,), (1,)), ((), ())), preferred_element_type=jnp.float32
        )

        @pl.when(at == 0)
        def _(shift=shift, product=product):
            sums[shift][...] = product

        @pl.when(at > 0)
        def _(shift=shift, product=product):
            sums[shift][...] += product

    @pl.when(at == pl.num_programs(0) - 1)
    def _():
        for shift in range(parts):
            used = row_steps[pl.ds(shift, 1), :]
            total = jnp.zeros((rank, count), jnp.float32)
            for n in range(shared + (alone if shift == 0 else 0)):
                term = sums[shift][pl.ds(n * rank, rank), :]
                total = total + jnp.where(used == scalars[1 + n], term, 0.0)
            out[:, pl.ds(shift * count, count)] = total


def score(tokens_of, shared, solo, panels, slot, steps, row_steps):
    parts, count = len(tokens_of), tokens_of[0].shape[0]
    _, rank, depth = panels.shape
    chunk = 1024
    alone = len(solo) + 1
    panel_spec = pl.BlockSpec((rank, chunk), lambda k, scalars: (0, k))
    heights = [(len(shared) + (alone if shift == 0 else 0)) * rank for shift in range(parts)]
    return pl.pallas_call(
        functools.partial(score_kernel, parts, len(shared), alone),
        grid_spec=pltpu.PrefetchScalarGridSpec(
            num_scalar_prefetch=1,
            grid=(depth // chunk,),
            in_specs=[pl.BlockSpec(row_steps.shape, lambda k, scalars: (0, 0))]
            + [pl.BlockSpec((count, chunk), lambda k, scalars: (0, k))] * parts
            + [panel_spec] * (len(shared) + len(solo))
            + [pl.BlockSpec((1, rank, chunk), lambda k, scalars: (scalars[0], 0, k))],
            out_specs=pl.BlockSpec((rank, parts * count), lambda k, scalars: (0, 0)),
            scratch_shapes=[pltpu.VMEM((height, count), jnp.float32) for height in heights],
        ),
        out_shape=jax.ShapeDtypeStruct((rank, parts * count), jnp.float32),
        compiler_params=pltpu.CompilerParams(
            dimension_semantics=("arbitrary",), vmem_limit_bytes=32 << 20
        ),
        cost_estimate=pl.CostEstimate(
            flops=2 * depth * count * sum(heights),
            bytes_accessed=2 * depth * (parts * count + heights[0]),
            transcendentals=0,
        ),
    )(jnp.stack([slot] + steps), row_steps, *tokens_of, *shared, *solo, panels)


def on_device(tokens, base_weight, shrink_panels, expand_panels, adapter_home, fetch_list, seg_len):
    per_home, depth, _ = shrink_panels.shape
    replicas, parts, cores = lax.axis_size("rep"), lax.axis_size("parts"), lax.axis_size("tp")
    me, part = lax.axis_index("rep"), lax.axis_index("parts")
    tok_count = tokens.shape[0]
    columns = expand_panels.shape[2] // cores
    panels = jnp.swapaxes(shrink_panels, 1, 2)
    tie = lax.optimization_barrier

    alone, half = max(2, parts), replicas // 2

    def grouped(steps):
        size = len(steps) // parts
        return [tuple(steps[p * size + g] for p in range(parts)) for g in range(size)]

    far = grouped(list(range(half, replicas)))
    near = grouped(list(range(alone, half)))
    groups = far + near
    solo = [(step,) * parts for step in range(1, alone)]

    def hop(x, group):
        pairs = [
            (p * replicas + i, p * replicas + (i ^ group[p]))
            for p in range(parts)
            for i in range(replicas)
        ]
        return lax.ppermute(x, ("parts", "rep"), pairs)

    def shift_parts(x, shift):
        return lax.ppermute(x, "parts", [(i, (i + shift) % parts) for i in range(parts)])

    def trade(x):
        for shift in range(1, cores):
            x = x + lax.ppermute(x, "tp", [(i, (i + shift) % cores) for i in range(cores)])
        return x

    rank = panels.shape[1]
    groups = far + near + solo
    blocks = [(group, True, True) for group in groups]
    send = pack(blocks, columns, adapter_home, fetch_list, panels, expand_panels)
    tokens, send = tie((tokens, send))
    recv = [hop(x, group) for x, group in zip(send, groups)]
    tokens_of = [tokens] + [shift_parts(tokens, shift) for shift in range(1, parts)]
    base_part = jnp.dot(tokens, base_weight, preferred_element_type=jnp.float32)
    base = lax.psum_scatter(base_part, "tp", scatter_dimension=1, tiled=True)

    stored = jnp.take(adapter_home, lax.dynamic_index_in_dim(fetch_list, me, 0, keepdims=False))
    steps = (stored // per_home) ^ me
    slot = jnp.sum(jnp.where(steps == 0, stored % per_home, 0))
    left = lax.axis_index("tp") * columns
    own_expand = lax.dynamic_slice(expand_panels, (slot, 0, left), (1, rank, columns))[0]
    far_recv, near_recv = recv[: len(far)], recv[len(far) : len(far) + len(near)]
    solo_recv = recv[len(far) + len(near) :]
    early, early_groups = near_recv + far_recv[:-1], near + far[:-1]

    def step_of(group, shift=0):
        step = jnp.int32(0)
        for p in range(parts):
            step = jnp.where(part == p, group[(p - shift) % parts], step)
        return step

    expands = [own_expand] + [x[:, depth:] for x in solo_recv + early]
    expand_steps = [0] + [group[0] for group in solo] + [step_of(group) for group in early_groups]
    sent = jnp.concatenate([x[:, depth:] for x in early], axis=0)
    for shift in range(1, parts):
        expands.append(shift_parts(sent, shift))
        expand_steps += [step_of(group, shift) for group in early_groups]
    expand = jnp.concatenate(expands, axis=0)

    lengths_of = [seg_len[0]]
    seg_len, solo_recv = tie((seg_len, solo_recv))
    for shift in range(1, parts):
        lengths_of.append(shift_parts(seg_len, shift)[0])
    rows = jnp.arange(tok_count, dtype=jnp.int32)

    def steps_of_rows(lengths):
        ordinal = jnp.arange(lengths.shape[0])
        starts = jnp.sum(jnp.where(ordinal[None, :] < ordinal[:, None], lengths[None, :], 0), axis=1)
        member = (rows[:, None] >= starts[None, :]) & (rows[:, None] < (starts + lengths)[None, :])
        return jnp.sum(jnp.where(member, steps[None, :], 0), axis=1)[None, :]

    row_steps = jnp.concatenate([steps_of_rows(lengths) for lengths in lengths_of], axis=0)

    row_steps, expand, base, far_recv[-1] = tie((row_steps, expand, base, far_recv[-1]))
    last_expand = far_recv[-1][:, depth:]
    expands = [expand, last_expand] + [shift_parts(last_expand, shift) for shift in range(1, parts)]
    expand_steps += [step_of(far[-1], shift) for shift in range(parts)]
    shared_steps = [step_of(group) for group in far + near]
    alone_steps = [jnp.int32(group[0]) for group in solo] + [jnp.int32(0)]
    scores = score(
        tokens_of, far_recv + near_recv, solo_recv, panels, slot, shared_steps + alone_steps, row_steps
    )
    scores, expands = tie((scores, expands))
    scores = trade(scores)
    shrink = scores[:, :tok_count]
    for shift in range(1, parts):
        shrink = shrink + shift_parts(scores[:, shift * tok_count : (shift + 1) * tok_count], -shift)
    wide = jnp.concatenate(
        [jnp.where(row_steps[:1] == step, shrink, 0.0) for step in expand_steps], axis=0
    )
    lora = lax.dot_general(
        wide,
        jnp.concatenate(expands, axis=0).astype(jnp.float32),
        (((0,), (0,)), ((), ())),
        precision=lax.Precision.HIGHEST,
        preferred_element_type=jnp.float32,
    )
    return (base + adapter_scale * lora).astype(jnp.bfloat16)


def solution(mesh):
    return jax.shard_map(
        on_device,
        mesh=mesh,
        in_specs=(
            P(("parts", "rep"), "tp"),
            P("tp", None),
            P("rep", "tp", None),
            P("rep", None, None),
            P(),
            P(),
            P(("parts", "rep"), None),
        ),
        out_specs=P(("parts", "rep"), "tp"),
        check_vma=False,
    )
```

```python
import functools
import jax
import jax.numpy as jnp
from jax import lax
from jax.experimental import pallas as pl
from jax.experimental.pallas import tpu as pltpu
from jax.sharding import PartitionSpec as P

adapter_scale = 2.0


def pack_kernel(blocks, home_ref, fetch_ref, shrink_ref, expand_ref, *refs):
    outs, sems = refs[:-1], refs[-1]
    me, part, half = lax.axis_index("rep"), lax.axis_index("parts"), lax.axis_index("tp")
    per_home, _, depth = shrink_ref.shape
    columns = expand_ref.shape[2] // lax.axis_size("tp")
    left = pl.multiple_of(half * columns, 128)
    listed = fetch_ref.shape[1]
    copies, slots = [], {}
    for at, (group, shrink, expand) in enumerate(blocks):
        if group not in slots:
            step = jnp.int32(group[0])
            for p, other in enumerate(group):
                step = jnp.where(part == p, other, step)
            peer = me ^ step

            def look(j, slot):
                position = home_ref[fetch_ref[peer, j]]
                return jnp.where(position // per_home == me, position % per_home, slot)

            slots[group] = lax.fori_loop(0, listed, look, jnp.int32(0), unroll=listed <= 8)
        slot = slots[group]
        pieces = []
        if shrink:
            pieces.append((shrink_ref.at[slot], outs[at].at[:, pl.ds(0, depth)]))
        if expand:
            target = outs[at].at[:, pl.ds(depth * shrink, columns)]
            pieces.append((expand_ref.at[slot, :, pl.ds(left, columns)], target))
        for n, (source, target) in enumerate(pieces):
            copies.append(pltpu.make_async_copy(source, target, sems.at[at, n]))
            copies[-1].start()
    for copy in copies:
        copy.wait()


def pack(blocks, columns, adapter_home, fetch_list, panels, expand_panels):
    rank, depth = panels.shape[1:]
    shapes = [(rank, depth * shrink + columns * expand) for _, shrink, expand in blocks]
    return list(
        pl.pallas_call(
            functools.partial(pack_kernel, blocks),
            out_shape=[jax.ShapeDtypeStruct(shape, panels.dtype) for shape in shapes],
            in_specs=[pl.BlockSpec(memory_space=pltpu.SMEM)] * 2 + [pl.BlockSpec(memory_space=pl.ANY)] * 2,
            out_specs=[pl.BlockSpec(memory_space=pltpu.VMEM)] * len(blocks),
            scratch_shapes=[pltpu.SemaphoreType.DMA((len(blocks), 2))],
            compiler_params=pltpu.CompilerParams(vmem_limit_bytes=56 << 20),
            cost_estimate=pl.CostEstimate(
                flops=0, bytes_accessed=4 * sum(r * w for r, w in shapes), transcendentals=0
            ),
        )(adapter_home, fetch_list, panels, expand_panels)
    )


def score_kernel(plan, rows_of, chunks, has_prior, scalars, row_steps, *refs):
    prior = refs[0] if has_prior else None
    refs = refs[1:] if has_prior else refs
    sets = len(plan)
    count_panels = len(refs) - sets - 4
    tokens, panels = refs[:sets], refs[sets : sets + count_panels]
    out, held_tokens, held_panels, sems = refs[sets + count_panels :]
    rank, count = out.shape[0], held_tokens.shape[1]
    width = held_tokens.shape[2] // chunks
    copies = []
    for c in range(chunks):
        cols = pl.ds(c * width, width)
        pairs = []
        for n, ref in enumerate(panels):
            source = ref.at[:, cols] if len(ref.shape) == 2 else ref.at[scalars[0], :, cols]
            pairs.append((source, held_panels.at[pl.ds(n * rank, rank), cols]))
        pairs += [(ref.at[:, cols], held_tokens.at[n, :, cols]) for n, ref in enumerate(tokens)]
        copies.append([])
        for n, (source, target) in enumerate(pairs):
            copies[-1].append(pltpu.make_async_copy(source, target, sems.at[c, n]))
            copies[-1][-1].start()
    sums = [None] * sets
    for c in range(chunks):
        for copy in copies[c]:
            copy.wait()
        cols = pl.ds(c * width, width)
        for t, used in enumerate(plan):
            product = lax.dot_general(
                held_panels[pl.ds(used[0] * rank, len(used) * rank), cols],
                held_tokens[t, :, cols],
                (((1,), (1,)), ((), ())),
                preferred_element_type=jnp.float32,
            )
            sums[t] = product if c == 0 else sums[t] + product
    for t, used in enumerate(plan):
        mine = row_steps[pl.ds(rows_of[t], 1), :]
        total = prior[...] if has_prior and t == 0 else jnp.zeros((rank, count), jnp.float32)
        for n, panel in enumerate(used):
            term = sums[t][n * rank : (n + 1) * rank]
            total = total + jnp.where(mine == scalars[1 + panel], term, 0.0)
        out[:, pl.ds(t * count, count)] = total


def score(plan, rows_of, tokens_of, panels, scalars, row_steps, prior=None):
    count, depth = tokens_of[0].shape
    rank = panels[0].shape[0]
    chunks = 4
    shape = (rank, len(plan) * count)
    prior = [] if prior is None else [prior]
    whole = pl.BlockSpec(memory_space=pltpu.VMEM)
    copied = len(tokens_of) + len(panels)
    return pl.pallas_call(
        functools.partial(score_kernel, plan, rows_of, chunks, bool(prior)),
        out_shape=jax.ShapeDtypeStruct(shape, jnp.float32),
        in_specs=[pl.BlockSpec(memory_space=pltpu.SMEM)]
        + [whole] * (1 + len(prior))
        + [pl.BlockSpec(memory_space=pl.ANY)] * copied,
        out_specs=whole,
        scratch_shapes=[
            pltpu.VMEM((len(tokens_of), count, depth), tokens_of[0].dtype),
            pltpu.VMEM((len(panels) * rank, depth), tokens_of[0].dtype),
            pltpu.SemaphoreType.DMA((chunks, copied)),
        ],
        compiler_params=pltpu.CompilerParams(vmem_limit_bytes=40 << 20),
        cost_estimate=pl.CostEstimate(
            flops=2 * depth * count * rank * sum(len(used) for used in plan),
            bytes_accessed=2 * depth * (len(plan) * count + len(panels) * rank),
            transcendentals=0,
        ),
    )(scalars, row_steps, *prior, *tokens_of, *panels)


def on_device(tokens, base_weight, shrink_panels, expand_panels, adapter_home, fetch_list, seg_len):
    per_home, depth, _ = shrink_panels.shape
    replicas, parts, cores = lax.axis_size("rep"), lax.axis_size("parts"), lax.axis_size("tp")
    me, part = lax.axis_index("rep"), lax.axis_index("parts")
    tok_count = tokens.shape[0]
    columns = expand_panels.shape[2] // cores
    panels = jnp.swapaxes(shrink_panels, 1, 2)
    tie = lax.optimization_barrier

    alone, half = max(2, parts), replicas // 2

    def grouped(steps):
        size = len(steps) // parts
        return [tuple(steps[p * size + g] for p in range(parts)) for g in range(size)]

    far = grouped(list(range(half, replicas)))
    near = grouped(list(range(alone, half)))
    groups = far + near
    solo = [(step,) * parts for step in range(1, alone)]

    def hop(x, group):
        pairs = [
            (p * replicas + i, p * replicas + (i ^ group[p]))
            for p in range(parts)
            for i in range(replicas)
        ]
        return lax.ppermute(x, ("parts", "rep"), pairs)

    def shift_parts(x, shift):
        return lax.ppermute(x, "parts", [(i, (i + shift) % parts) for i in range(parts)])

    def trade(x):
        for shift in range(1, cores):
            x = x + lax.ppermute(x, "tp", [(i, (i + shift) % cores) for i in range(cores)])
        return x

    rank = panels.shape[1]
    groups = far + near + solo
    blocks = [(group, True, True) for group in groups]
    send = pack(blocks, columns, adapter_home, fetch_list, panels, expand_panels)
    tokens, send = tie((tokens, send))
    recv = [hop(x, group) for x, group in zip(send, groups)]
    tokens_of = [tokens] + [shift_parts(tokens, shift) for shift in range(1, parts)]
    solo_recv = recv[len(far) + len(near) :]
    base_weight, fetch_list, seg_len, solo_recv = tie((base_weight, fetch_list, seg_len, solo_recv))
    base_part = jnp.dot(tokens, base_weight, preferred_element_type=jnp.float32)
    base_part, recv[: len(far) - 1] = tie((base_part, recv[: len(far) - 1]))
    base = lax.psum_scatter(base_part, "tp", scatter_dimension=1, tiled=True)

    stored = jnp.take(adapter_home, lax.dynamic_index_in_dim(fetch_list, me, 0, keepdims=False))
    steps = (stored // per_home) ^ me
    slot = jnp.sum(jnp.where(steps == 0, stored % per_home, 0))
    left = lax.axis_index("tp") * columns
    own_expand = lax.dynamic_slice(expand_panels, (slot, 0, left), (1, rank, columns))[0]
    far_recv, near_recv = recv[: len(far)], recv[len(far) : len(far) + len(near)]
    early, early_groups = near_recv + far_recv[:-1], near + far[:-1]

    def step_of(group, shift=0):
        step = jnp.int32(0)
        for p in range(parts):
            step = jnp.where(part == p, group[(p - shift) % parts], step)
        return step

    expands = [own_expand] + [x[:, depth:] for x in solo_recv + early]
    expand_steps = [0] + [group[0] for group in solo] + [step_of(group) for group in early_groups]
    sent = jnp.concatenate([x[:, depth:] for x in early], axis=0)
    for shift in range(1, parts):
        expands.append(shift_parts(sent, shift))
        expand_steps += [step_of(group, shift) for group in early_groups]
    expand = jnp.concatenate(expands, axis=0)

    lengths_of = [seg_len[0]]
    for shift in range(1, parts):
        lengths_of.append(shift_parts(seg_len, shift)[0])
    rows = jnp.arange(tok_count, dtype=jnp.int32)

    def steps_of_rows(lengths):
        ordinal = jnp.arange(lengths.shape[0])
        starts = jnp.sum(jnp.where(ordinal[None, :] < ordinal[:, None], lengths[None, :], 0), axis=1)
        member = (rows[:, None] >= starts[None, :]) & (rows[:, None] < (starts + lengths)[None, :])
        return jnp.sum(jnp.where(member, steps[None, :], 0), axis=1)[None, :]

    row_steps = jnp.concatenate([steps_of_rows(lengths) for lengths in lengths_of], axis=0)

    slot_and = lambda values: jnp.stack([slot] + [jnp.int32(value) for value in values])
    early_steps = [step_of(group) for group in early_groups]
    alone_steps = [group[0] for group in solo] + [0]
    first = score(
        [tuple(range(len(early) + len(solo) + 1))],
        [0],
        [tokens],
        early + solo_recv + [panels],
        slot_and(early_steps + alone_steps),
        row_steps[:1],
    )
    row_steps, expand, base, first, tokens_of[1:], far_recv[-1] = tie(
        (row_steps, expand, base, first, tokens_of[1:], far_recv[-1])
    )
    scores = score(
        [(0,)] + [tuple(range(len(early) + 1))] * (parts - 1),
        list(range(parts)),
        tokens_of,
        [far_recv[-1]] + early,
        slot_and([step_of(far[-1])] + early_steps),
        row_steps,
        first,
    )
    scores, far_recv[-1] = tie((scores, far_recv[-1]))
    last_expand = far_recv[-1][:, depth:]
    expands = [expand, last_expand] + [shift_parts(last_expand, shift) for shift in range(1, parts)]
    expand_steps += [step_of(far[-1], shift) for shift in range(parts)]
    scores = trade(scores)
    shrink = scores[:, :tok_count]
    for shift in range(1, parts):
        shrink = shrink + shift_parts(scores[:, shift * tok_count : (shift + 1) * tok_count], -shift)
    high = lax.reduce_precision(shrink, 8, 7)
    terms = [high.astype(jnp.bfloat16), (shrink - high).astype(jnp.bfloat16)]
    wide = jnp.concatenate(
        [
            jnp.where(row_steps[:1] == step, term, jnp.zeros((), jnp.bfloat16))
            for term in terms
            for step in expand_steps
        ],
        axis=0,
    )
    expand = jnp.concatenate(expands * 2, axis=0)
    lora = lax.dot_general(
        wide, expand, (((0,), (0,)), ((), ())), preferred_element_type=jnp.float32
    )
    return (base + adapter_scale * lora).astype(jnp.bfloat16)


def solution(mesh):
    return jax.shard_map(
        on_device,
        mesh=mesh,
        in_specs=(
            P(("parts", "rep"), "tp"),
            P("tp", None),
            P("rep", "tp", None),
            P("rep", None, None),
            P(),
            P(),
            P(("parts", "rep"), None),
        ),
        out_specs=P(("parts", "rep"), "tp"),
        check_vma=False,
    )
```

```python
import functools
import jax
import jax.numpy as jnp
from jax import lax
from jax.experimental import pallas as pl
from jax.experimental.pallas import tpu as pltpu
from jax.sharding import PartitionSpec as P

adapter_scale = 2.0


def by_part(values):
    part = lax.axis_index("parts")
    chosen = jnp.int32(values[0])
    for p, value in enumerate(values):
        chosen = jnp.where(part == p, value, chosen)
    return chosen


def turned(group, shift):
    return tuple(group[(p - shift) % len(group)] for p in range(len(group)))


def slot_for(peer, me, per_home, home_ref, fetch_ref):
    first = me * per_home

    def look(j, slot):
        local = home_ref[fetch_ref[peer, j]] - first
        return jnp.where((local >= 0) & (local < per_home), local, slot)

    listed = fetch_ref.shape[1]
    return lax.fori_loop(0, listed, look, jnp.int32(0), unroll=listed <= 8)


def steps_of_rows(lengths_ref, count, me, per_home, home_ref, fetch_ref):
    rows = lax.broadcasted_iota(jnp.int32, (1, count), 1)
    result = jnp.zeros((1, count), jnp.int32)
    start = jnp.int32(0)
    for j in range(fetch_ref.shape[1]):
        step = lax.div(home_ref[fetch_ref[me, j]], jnp.int32(per_home)) ^ me
        result = jnp.where(rows >= start, step, result)
        start = start + lengths_ref[0, j]
    return result


def pack_kernel(groups, home_ref, fetch_ref, shrink_ref, expand_ref, *refs):
    outs, sems = refs[:-1], refs[-1]
    me = lax.axis_index("rep")
    per_home, _, depth = shrink_ref.shape
    columns = expand_ref.shape[2] // lax.axis_size("tp")
    left = pl.multiple_of(lax.axis_index("tp") * columns, 128)
    copies = []
    for at, group in enumerate(groups):
        slot = slot_for(me ^ by_part(group), me, per_home, home_ref, fetch_ref)
        pieces = (
            (shrink_ref.at[slot], outs[at].at[:, pl.ds(0, depth)]),
            (expand_ref.at[slot, :, pl.ds(left, columns)], outs[at].at[:, pl.ds(depth, columns)]),
        )
        for n, (source, target) in enumerate(pieces):
            copies.append(pltpu.make_async_copy(source, target, sems.at[at, n]))
            copies[-1].start()
    for copy in copies:
        copy.wait()


def pack(groups, columns, adapter_home, fetch_list, panels, expand_panels):
    rank, depth = panels.shape[1:]
    shape = (rank, depth + columns)
    return list(
        pl.pallas_call(
            functools.partial(pack_kernel, groups),
            out_shape=[jax.ShapeDtypeStruct(shape, panels.dtype)] * len(groups),
            in_specs=[pl.BlockSpec(memory_space=pltpu.SMEM)] * 2 + [pl.BlockSpec(memory_space=pl.ANY)] * 2,
            out_specs=[pl.BlockSpec(memory_space=pltpu.VMEM)] * len(groups),
            scratch_shapes=[pltpu.SemaphoreType.DMA((len(groups), 2))],
            compiler_params=pltpu.CompilerParams(vmem_limit_bytes=56 << 20),
            cost_estimate=pl.CostEstimate(
                flops=0, bytes_accessed=4 * len(groups) * shape[0] * shape[1], transcendentals=0
            ),
        )(adapter_home, fetch_list, panels, expand_panels)
    )


def score_kernel(plan, groups, kept, chunks, has_prior, per_home, home_ref, fetch_ref, *refs):
    sets, many = len(plan), len(groups)
    lengths, refs = refs[:sets], refs[sets:]
    prior, refs = (refs[0], refs[1:]) if has_prior else (None, refs)
    tokens, panels = refs[:sets], refs[sets : sets + many]
    out, out_expand, held_tokens, held_panels, sems = refs[sets + many :]
    me = lax.axis_index("rep")
    rank, count, depth = out.shape[0], held_tokens.shape[1], held_tokens.shape[2]
    width = depth // chunks
    slot = slot_for(me, me, per_home, home_ref, fetch_ref)
    copies = []
    for c in range(chunks):
        cols = pl.ds(c * width, width)
        pairs = []
        for n, ref in enumerate(panels):
            source = ref.at[:, cols] if len(ref.shape) == 2 else ref.at[slot, :, cols]
            pairs.append((source, held_panels.at[pl.ds(n * rank, rank), cols]))
        pairs += [(ref.at[:, cols], held_tokens.at[n, :, cols]) for n, ref in enumerate(tokens)]
        if c == chunks - 1:
            pairs += [
                (panels[n].at[:, pl.ds(depth, out_expand.shape[1])], out_expand.at[pl.ds(i * rank, rank)])
                for i, n in enumerate(kept)
            ]
        copies.append([])
        for n, (source, target) in enumerate(pairs):
            copies[-1].append(pltpu.make_async_copy(source, target, sems.at[c, n]))
            copies[-1][-1].start()
    row_steps = [steps_of_rows(x, count, me, per_home, home_ref, fetch_ref) for x in lengths]
    sums = [None] * sets
    for c in range(chunks):
        for copy in copies[c]:
            copy.wait()
        cols = pl.ds(c * width, width)
        for t, used in enumerate(plan):
            product = lax.dot_general(
                held_panels[pl.ds(used[0] * rank, len(used) * rank), cols],
                held_tokens[t, :, cols],
                (((1,), (1,)), ((), ())),
                preferred_element_type=jnp.float32,
            )
            sums[t] = product if c == 0 else sums[t] + product
    for t, used in enumerate(plan):
        total = prior[...] if has_prior and t == 0 else jnp.zeros((rank, count), jnp.float32)
        for n, panel in enumerate(used):
            term = sums[t][n * rank : (n + 1) * rank]
            total = total + jnp.where(row_steps[t] == by_part(groups[panel]), term, 0.0)
        out[:, pl.ds(t * count, count)] = total


def score(plan, groups, kept, tables, columns, lengths_of, tokens_of, panels, prior=None):
    count, depth = tokens_of[0].shape
    per_home, rank, _ = tables[2].shape
    chunks = 4
    prior = [] if prior is None else [prior]
    smem, vmem = pl.BlockSpec(memory_space=pltpu.SMEM), pl.BlockSpec(memory_space=pltpu.VMEM)
    copied = len(tokens_of) + len(panels)
    return pl.pallas_call(
        functools.partial(score_kernel, plan, groups, kept, chunks, bool(prior), per_home),
        out_shape=[
            jax.ShapeDtypeStruct((rank, len(plan) * count), jnp.float32),
            jax.ShapeDtypeStruct((len(kept) * rank, columns), panels[0].dtype),
        ],
        in_specs=[smem] * (2 + len(lengths_of))
        + [vmem] * len(prior)
        + [pl.BlockSpec(memory_space=pl.ANY)] * copied,
        out_specs=[vmem, vmem],
        scratch_shapes=[
            pltpu.VMEM((len(tokens_of), count, depth), tokens_of[0].dtype),
            pltpu.VMEM((len(panels) * rank, depth), tokens_of[0].dtype),
            pltpu.SemaphoreType.DMA((chunks, copied + len(kept))),
        ],
        compiler_params=pltpu.CompilerParams(vmem_limit_bytes=40 << 20),
        cost_estimate=pl.CostEstimate(flops=0, bytes_accessed=0, transcendentals=0),
    )(tables[0], tables[1], *lengths_of, *prior, *tokens_of, *panels)


def base_kernel(chunks, tokens_ref, weight_ref, *refs):
    outs, (held_tokens, held_weight, sems) = refs[:-3], refs[-3:]
    cores, half = len(outs), lax.axis_index("tp")
    columns = outs[0].shape[1]
    height = tokens_ref.shape[1] // chunks
    copies = []
    for c in range(chunks):
        rows = pl.ds(c * height, height)
        pairs = [(tokens_ref.at[:, rows], held_tokens.at[:, rows])]
        for shift in range(cores):
            left = pl.multiple_of(lax.rem(half + shift, cores) * columns, 128)
            pairs.append((weight_ref.at[rows, pl.ds(left, columns)], held_weight.at[shift, rows, :]))
        copies.append([])
        for n, (source, target) in enumerate(pairs):
            copies[-1].append(pltpu.make_async_copy(source, target, sems.at[c, n]))
            copies[-1][-1].start()
    for c in range(chunks):
        for copy in copies[c]:
            copy.wait()
        rows = pl.ds(c * height, height)
        for shift, out in enumerate(outs):
            product = jnp.dot(
                held_tokens[:, rows], held_weight[shift, rows, :], preferred_element_type=jnp.float32
            )
            if c == 0:
                out[...] = product
            else:
                out[...] += product


def base_terms(tokens, weight, cores):
    count, depth = tokens.shape
    columns = weight.shape[1] // cores
    chunks = 4
    return list(
        pl.pallas_call(
            functools.partial(base_kernel, chunks),
            out_shape=[jax.ShapeDtypeStruct((count, columns), jnp.float32)] * cores,
            in_specs=[pl.BlockSpec(memory_space=pl.ANY)] * 2,
            out_specs=[pl.BlockSpec(memory_space=pltpu.VMEM)] * cores,
            scratch_shapes=[
                pltpu.VMEM((count, depth), tokens.dtype),
                pltpu.VMEM((cores, depth, columns), weight.dtype),
                pltpu.SemaphoreType.DMA((chunks, 1 + cores)),
            ],
            compiler_params=pltpu.CompilerParams(vmem_limit_bytes=40 << 20),
            cost_estimate=pl.CostEstimate(flops=0, bytes_accessed=0, transcendentals=0),
        )(tokens, weight)
    )


def finish_kernel(pieces, added, came, bases, per_home, home_ref, fetch_ref, lengths_ref, *refs):
    scores, others = refs[:added], refs[added : added + came]
    base, refs = refs[added + came : added + came + bases], refs[added + came + bases :]
    expand_ref, arrays, (out, held, sems) = refs[0], refs[1:-3], refs[-3:]
    me = lax.axis_index("rep")
    count, columns = out.shape
    rank = scores[0].shape[0]
    left = pl.multiple_of(lax.axis_index("tp") * columns, 128)
    slot = slot_for(me, me, per_home, home_ref, fetch_ref)
    copies = []
    for n, (at, row, _) in enumerate(pieces):
        if at is None:
            source = expand_ref.at[slot, :, pl.ds(left, columns)]
        else:
            source = arrays[at].at[pl.ds(row, rank), pl.ds(arrays[at].shape[1] - columns, columns)]
        copies.append(pltpu.make_async_copy(source, held.at[pl.ds(n * rank, rank)], sems.at[n]))
        copies[-1].start()
    row_steps = steps_of_rows(lengths_ref, count, me, per_home, home_ref, fetch_ref)
    shrink = scores[0][:, pl.ds(0, count)]
    for x in scores[1:]:
        shrink = shrink + x[:, pl.ds(0, count)]
    for x in others:
        shrink = shrink + x[...]
    shrink = adapter_scale * shrink
    high = shrink.astype(jnp.bfloat16).astype(jnp.float32)
    terms = [high, shrink - high]
    masks = [row_steps == by_part(group) for _, _, group in pieces]
    for copy in copies:
        copy.wait()
    total = base[0][...]
    for x in base[1:]:
        total = total + x[...]
    for term in terms:
        wide = jnp.concatenate([jnp.where(mask, term, 0.0) for mask in masks], axis=0)
        total = total + lax.dot_general(
            wide.astype(jnp.bfloat16),
            held[...],
            (((0,), (0,)), ((), ())),
            preferred_element_type=jnp.float32,
        )
    out[...] = total.astype(out.dtype)


def finish(pieces, tables, lengths, scores, others, base, arrays):
    count, columns = base[0].shape
    per_home, rank, _ = tables[2].shape
    smem, vmem = pl.BlockSpec(memory_space=pltpu.SMEM), pl.BlockSpec(memory_space=pltpu.VMEM)
    height = len(pieces) * rank
    return pl.pallas_call(
        functools.partial(finish_kernel, pieces, len(scores), len(others), len(base), per_home),
        out_shape=jax.ShapeDtypeStruct((count, columns), jnp.bfloat16),
        in_specs=[smem] * 3
        + [vmem] * (len(scores) + len(others) + len(base))
        + [pl.BlockSpec(memory_space=pl.ANY)] * (1 + len(arrays)),
        out_specs=vmem,
        scratch_shapes=[
            pltpu.VMEM((height, columns), jnp.bfloat16),
            pltpu.SemaphoreType.DMA((len(pieces),)),
        ],
        compiler_params=pltpu.CompilerParams(vmem_limit_bytes=24 << 20),
        cost_estimate=pl.CostEstimate(
            flops=4 * count * columns * height,
            bytes_accessed=2 * columns * height + 6 * count * columns,
            transcendentals=0,
        ),
    )(tables[0], tables[1], lengths, *scores, *others, *base, tables[3], *arrays)


def on_device(tokens, base_weight, shrink_panels, expand_panels, adapter_home, fetch_list, seg_len):
    replicas, parts, cores = lax.axis_size("rep"), lax.axis_size("parts"), lax.axis_size("tp")
    tok_count = tokens.shape[0]
    columns = expand_panels.shape[2] // cores
    panels = jnp.swapaxes(shrink_panels, 1, 2)
    rank = panels.shape[1]
    tie = lax.optimization_barrier

    alone, half = max(2, parts), replicas // 2

    def grouped(steps):
        size = len(steps) // parts
        return [tuple(steps[p * size + g] for p in range(parts)) for g in range(size)]

    far = grouped(list(range(half, replicas)))
    near = grouped(list(range(alone, half)))
    groups = far + near
    solo = [(step,) * parts for step in range(1, alone)]

    def hop(x, group):
        pairs = [
            (p * replicas + i, p * replicas + (i ^ group[p]))
            for p in range(parts)
            for i in range(replicas)
        ]
        return lax.ppermute(x, ("parts", "rep"), pairs)

    def shift_parts(x, shift):
        return lax.ppermute(x, "parts", [(i, (i + shift) % parts) for i in range(parts)])

    def shift_cores(x, shift):
        return lax.ppermute(x, "tp", [(i, (i + shift) % cores) for i in range(cores)])

    tables = (adapter_home, fetch_list, panels, expand_panels)
    groups = far + near + solo
    send = pack(groups, columns, *tables)
    tokens, send = tie((tokens, send))
    recv = [hop(x, group) for x, group in zip(send, groups)]
    tokens_of = [tokens] + [shift_parts(tokens, shift) for shift in range(1, parts)]
    solo_recv = recv[len(far) + len(near) :]
    base_weight, seg_len, solo_recv = tie((base_weight, seg_len, solo_recv))
    base = base_terms(tokens, base_weight, cores)
    base, recv[: len(far) - 1] = tie((base, recv[: len(far) - 1]))
    base = base[:1] + [shift_cores(x, shift + 1) for shift, x in enumerate(base[1:])]
    lengths_of = [seg_len] + [shift_parts(seg_len, shift) for shift in range(1, parts)]
    early, early_groups = recv[len(far) : len(far) + len(near)] + recv[: len(far) - 1], near + far[:-1]
    last, last_group, own_group = recv[len(far) - 1], far[-1], (0,) * parts

    count = len(early)
    first, sent = score(
        [tuple(range(count + len(solo) + 1))],
        early_groups + solo + [own_group],
        tuple(range(count)),
        tables,
        columns,
        lengths_of[:1],
        [tokens],
        early + solo_recv + [panels],
    )
    passed = [shift_parts(sent, shift) for shift in range(1, parts)]
    base, first, tokens_of[1:], last = tie((base, first, tokens_of[1:], last))
    scores, sent = score(
        [(0,)] + [tuple(range(count + 1))] * (parts - 1),
        [last_group] + early_groups,
        (0,),
        tables,
        columns,
        lengths_of,
        tokens_of,
        [last] + early,
        first,
    )
    last_passed = [shift_parts(sent, shift) for shift in range(1, parts)]
    halves = [scores] + [shift_cores(scores, shift) for shift in range(1, cores)]
    whole = halves[0]
    for x in halves[1:]:
        whole = whole + x
    came = [
        shift_parts(whole[:, shift * tok_count : (shift + 1) * tok_count], -shift)
        for shift in range(1, parts)
    ]
    arrays = early + solo_recv + [last] + passed + last_passed
    pieces = [(None, 0, own_group)]
    pieces += [(n, 0, group) for n, group in enumerate(early_groups + solo + [last_group])]
    at = len(pieces) - 1
    for shift in range(1, parts):
        pieces += [(at, n * rank, turned(group, shift)) for n, group in enumerate(early_groups)]
        pieces.append((at + parts - 1, 0, turned(last_group, shift)))
        at += 1
    return finish(pieces, tables, seg_len, halves, came, base, arrays)


def solution(mesh):
    return jax.shard_map(
        on_device,
        mesh=mesh,
        in_specs=(
            P(("parts", "rep"), "tp"),
            P("tp", None),
            P("rep", "tp", None),
            P("rep", None, None),
            P(),
            P(),
            P(("parts", "rep"), None),
        ),
        out_specs=P(("parts", "rep"), "tp"),
        check_vma=False,
    )
```

```python
import functools
import jax
import jax.numpy as jnp
from jax import lax
from jax.experimental import pallas as pl
from jax.experimental.pallas import tpu as pltpu
from jax.sharding import PartitionSpec as P

adapter_scale = 2.0


def by_part(values):
    part = lax.axis_index("parts")
    chosen = jnp.int32(values[0])
    for p, value in enumerate(values):
        chosen = jnp.where(part == p, value, chosen)
    return chosen


def turned(group, shift):
    return tuple(group[(p - shift) % len(group)] for p in range(len(group)))


def slot_for(peer, me, per_home, home_ref, fetch_ref):
    first = me * per_home

    def look(j, slot):
        local = home_ref[fetch_ref[peer, j]] - first
        return jnp.where((local >= 0) & (local < per_home), local, slot)

    listed = fetch_ref.shape[1]
    return lax.fori_loop(0, listed, look, jnp.int32(0), unroll=listed <= 8)


def steps_of_rows(lengths_ref, count, me, per_home, home_ref, fetch_ref):
    rows = lax.broadcasted_iota(jnp.int32, (1, count), 1)
    result = jnp.zeros((1, count), jnp.int32)
    start = jnp.int32(0)
    for j in range(fetch_ref.shape[1]):
        step = lax.div(home_ref[fetch_ref[me, j]], jnp.int32(per_home)) ^ me
        result = jnp.where(rows >= start, step, result)
        start = start + lengths_ref[0, j]
    return result


def pack_kernel(groups, home_ref, fetch_ref, shrink_ref, expand_ref, *refs):
    count = len(groups)
    outs, held, in_sems, out_sems = refs[:count], refs[count], refs[count + 1], refs[count + 2]
    me = lax.axis_index("rep")
    per_home, _, depth = shrink_ref.shape
    columns = expand_ref.shape[2] // lax.axis_size("tp")
    left = pl.multiple_of(lax.axis_index("tp") * columns, 128)
    cuts = in_sems.shape[1] - 1
    width = depth // cuts
    arriving = []
    for at, group in enumerate(groups):
        slot = slot_for(me ^ by_part(group), me, per_home, home_ref, fetch_ref)
        pieces = [(shrink_ref.at[slot, :, pl.ds(n * width, width)], n * width, width) for n in range(cuts)]
        pieces.append((expand_ref.at[slot, :, pl.ds(left, columns)], depth, columns))
        for n, (source, start, size) in enumerate(pieces):
            target = held.at[at, :, pl.ds(start, size)]
            copy = pltpu.make_async_copy(source, target, in_sems.at[at, n])
            copy.start()
            leave = pltpu.make_async_copy(target, outs[at].at[:, pl.ds(start, size)], out_sems.at[at, n])
            arriving.append((copy, leave))
    for copy, leave in arriving:
        copy.wait()
        leave.start()
    for _, leave in arriving:
        leave.wait()


def pack(groups, columns, adapter_home, fetch_list, panels, expand_panels):
    rank, depth = panels.shape[1:]
    shape = (rank, depth + columns)
    cuts = 2
    return list(
        pl.pallas_call(
            functools.partial(pack_kernel, groups),
            out_shape=[jax.ShapeDtypeStruct(shape, panels.dtype)] * len(groups),
            in_specs=[pl.BlockSpec(memory_space=pltpu.SMEM)] * 2 + [pl.BlockSpec(memory_space=pl.ANY)] * 2,
            out_specs=[pl.BlockSpec(memory_space=pl.ANY)] * len(groups),
            scratch_shapes=[pltpu.VMEM((len(groups),) + shape, panels.dtype)]
            + [pltpu.SemaphoreType.DMA((len(groups), cuts + 1))] * 2,
            compiler_params=pltpu.CompilerParams(vmem_limit_bytes=56 << 20),
            cost_estimate=pl.CostEstimate(flops=0, bytes_accessed=0, transcendentals=0),
        )(adapter_home, fetch_list, panels, expand_panels)
    )


def score_kernel(plan, groups, kept, chunks, has_prior, per_home, home_ref, fetch_ref, *refs):
    sets, many = len(plan), len(groups)
    lengths, refs = refs[:sets], refs[sets:]
    prior, refs = (refs[0], refs[1:]) if has_prior else (None, refs)
    tokens, panels = refs[:sets], refs[sets : sets + many]
    out, out_expand, held_tokens, held_panels, sems = refs[sets + many :]
    me = lax.axis_index("rep")
    rank, count, depth = out.shape[0], held_tokens.shape[1], held_tokens.shape[2]
    width = depth // chunks
    slot = slot_for(me, me, per_home, home_ref, fetch_ref)
    copies = []
    for c in range(chunks):
        cols = pl.ds(c * width, width)
        pairs = []
        for n, ref in enumerate(panels):
            source = ref.at[:, cols] if len(ref.shape) == 2 else ref.at[slot, :, cols]
            pairs.append((source, held_panels.at[pl.ds(n * rank, rank), cols]))
        pairs += [(ref.at[:, cols], held_tokens.at[n, :, cols]) for n, ref in enumerate(tokens)]
        if c == chunks - 1:
            pairs += [
                (panels[n].at[:, pl.ds(depth, out_expand.shape[1])], out_expand.at[pl.ds(i * rank, rank)])
                for i, n in enumerate(kept)
            ]
        copies.append([])
        for n, (source, target) in enumerate(pairs):
            copies[-1].append(pltpu.make_async_copy(source, target, sems.at[c, n]))
            copies[-1][-1].start()
    row_steps = [steps_of_rows(x, count, me, per_home, home_ref, fetch_ref) for x in lengths]
    sums = [None] * sets
    for c in range(chunks):
        for copy in copies[c]:
            copy.wait()
        cols = pl.ds(c * width, width)
        for t, used in enumerate(plan):
            product = lax.dot_general(
                held_panels[pl.ds(used[0] * rank, len(used) * rank), cols],
                held_tokens[t, :, cols],
                (((1,), (1,)), ((), ())),
                preferred_element_type=jnp.float32,
            )
            sums[t] = product if c == 0 else sums[t] + product
    for t, used in enumerate(plan):
        total = prior[...] if has_prior and t == 0 else jnp.zeros((rank, count), jnp.float32)
        for n, panel in enumerate(used):
            term = sums[t][n * rank : (n + 1) * rank]
            total = total + jnp.where(row_steps[t] == by_part(groups[panel]), term, 0.0)
        out[:, pl.ds(t * count, count)] = total


def score(plan, groups, kept, tables, columns, lengths_of, tokens_of, panels, prior=None):
    count, depth = tokens_of[0].shape
    per_home, rank, _ = tables[2].shape
    chunks = 4
    prior = [] if prior is None else [prior]
    smem, vmem = pl.BlockSpec(memory_space=pltpu.SMEM), pl.BlockSpec(memory_space=pltpu.VMEM)
    copied = len(tokens_of) + len(panels)
    return pl.pallas_call(
        functools.partial(score_kernel, plan, groups, kept, chunks, bool(prior), per_home),
        out_shape=[
            jax.ShapeDtypeStruct((rank, len(plan) * count), jnp.float32),
            jax.ShapeDtypeStruct((len(kept) * rank, columns), panels[0].dtype),
        ],
        in_specs=[smem] * (2 + len(lengths_of))
        + [vmem] * len(prior)
        + [pl.BlockSpec(memory_space=pl.ANY)] * copied,
        out_specs=[vmem, vmem],
        scratch_shapes=[
            pltpu.VMEM((len(tokens_of), count, depth), tokens_of[0].dtype),
            pltpu.VMEM((len(panels) * rank, depth), tokens_of[0].dtype),
            pltpu.SemaphoreType.DMA((chunks, copied + len(kept))),
        ],
        compiler_params=pltpu.CompilerParams(vmem_limit_bytes=40 << 20),
        cost_estimate=pl.CostEstimate(flops=0, bytes_accessed=0, transcendentals=0),
    )(tables[0], tables[1], *lengths_of, *prior, *tokens_of, *panels)


def base_kernel(chunks, tokens_ref, weight_ref, *refs):
    outs, (held_tokens, held_weight, sems) = refs[:-3], refs[-3:]
    cores, half = len(outs), lax.axis_index("tp")
    columns = outs[0].shape[1]
    height = tokens_ref.shape[1] // chunks
    copies = []
    for c in range(chunks):
        rows = pl.ds(c * height, height)
        pairs = [(tokens_ref.at[:, rows], held_tokens.at[:, rows])]
        for shift in range(cores):
            left = pl.multiple_of(lax.rem(half + shift, cores) * columns, 128)
            pairs.append((weight_ref.at[rows, pl.ds(left, columns)], held_weight.at[shift, rows, :]))
        copies.append([])
        for n, (source, target) in enumerate(pairs):
            copies[-1].append(pltpu.make_async_copy(source, target, sems.at[c, n]))
            copies[-1][-1].start()
    for c in range(chunks):
        for copy in copies[c]:
            copy.wait()
        rows = pl.ds(c * height, height)
        for shift, out in enumerate(outs):
            product = jnp.dot(
                held_tokens[:, rows], held_weight[shift, rows, :], preferred_element_type=jnp.float32
            )
            if c == 0:
                out[...] = product
            else:
                out[...] += product


def base_terms(tokens, weight, cores):
    count, depth = tokens.shape
    columns = weight.shape[1] // cores
    chunks = 4
    return list(
        pl.pallas_call(
            functools.partial(base_kernel, chunks),
            out_shape=[jax.ShapeDtypeStruct((count, columns), jnp.float32)] * cores,
            in_specs=[pl.BlockSpec(memory_space=pl.ANY)] * 2,
            out_specs=[pl.BlockSpec(memory_space=pltpu.VMEM)] * cores,
            scratch_shapes=[
                pltpu.VMEM((count, depth), tokens.dtype),
                pltpu.VMEM((cores, depth, columns), weight.dtype),
                pltpu.SemaphoreType.DMA((chunks, 1 + cores)),
            ],
            compiler_params=pltpu.CompilerParams(vmem_limit_bytes=40 << 20),
            cost_estimate=pl.CostEstimate(flops=0, bytes_accessed=0, transcendentals=0),
        )(tokens, weight)
    )


def finish_kernel(pieces, added, came, bases, per_home, home_ref, fetch_ref, lengths_ref, *refs):
    scores, others = refs[:added], refs[added : added + came]
    base, refs = refs[added + came : added + came + bases], refs[added + came + bases :]
    expand_ref, arrays, (out, held, sems) = refs[0], refs[1:-3], refs[-3:]
    me = lax.axis_index("rep")
    count, columns = out.shape
    rank = scores[0].shape[0]
    left = pl.multiple_of(lax.axis_index("tp") * columns, 128)
    slot = slot_for(me, me, per_home, home_ref, fetch_ref)
    copies = []
    for n, (at, row, _) in enumerate(pieces):
        if at is None:
            source = expand_ref.at[slot, :, pl.ds(left, columns)]
        else:
            source = arrays[at].at[pl.ds(row, rank), pl.ds(arrays[at].shape[1] - columns, columns)]
        copies.append(pltpu.make_async_copy(source, held.at[pl.ds(n * rank, rank)], sems.at[n]))
        copies[-1].start()
    row_steps = steps_of_rows(lengths_ref, count, me, per_home, home_ref, fetch_ref)
    shrink = scores[0][:, pl.ds(0, count)]
    for x in scores[1:]:
        shrink = shrink + x[:, pl.ds(0, count)]
    for x in others:
        shrink = shrink + x[...]
    shrink = adapter_scale * shrink
    high = shrink.astype(jnp.bfloat16).astype(jnp.float32)
    terms = [high, shrink - high]
    masks = [row_steps == by_part(group) for _, _, group in pieces]
    for copy in copies:
        copy.wait()
    total = base[0][...]
    for x in base[1:]:
        total = total + x[...]
    for term in terms:
        wide = jnp.concatenate([jnp.where(mask, term, 0.0) for mask in masks], axis=0)
        total = total + lax.dot_general(
            wide.astype(jnp.bfloat16),
            held[...],
            (((0,), (0,)), ((), ())),
            preferred_element_type=jnp.float32,
        )
    out[...] = total.astype(out.dtype)


def finish(pieces, tables, lengths, scores, others, base, arrays):
    count, columns = base[0].shape
    per_home, rank, _ = tables[2].shape
    smem, vmem = pl.BlockSpec(memory_space=pltpu.SMEM), pl.BlockSpec(memory_space=pltpu.VMEM)
    height = len(pieces) * rank
    return pl.pallas_call(
        functools.partial(finish_kernel, pieces, len(scores), len(others), len(base), per_home),
        out_shape=jax.ShapeDtypeStruct((count, columns), jnp.bfloat16),
        in_specs=[smem] * 3
        + [vmem] * (len(scores) + len(others) + len(base))
        + [pl.BlockSpec(memory_space=pl.ANY)] * (1 + len(arrays)),
        out_specs=vmem,
        scratch_shapes=[
            pltpu.VMEM((height, columns), jnp.bfloat16),
            pltpu.SemaphoreType.DMA((len(pieces),)),
        ],
        compiler_params=pltpu.CompilerParams(vmem_limit_bytes=24 << 20),
        cost_estimate=pl.CostEstimate(
            flops=4 * count * columns * height,
            bytes_accessed=2 * columns * height + 6 * count * columns,
            transcendentals=0,
        ),
    )(tables[0], tables[1], lengths, *scores, *others, *base, tables[3], *arrays)


def on_device(tokens, base_weight, shrink_panels, expand_panels, adapter_home, fetch_list, seg_len):
    replicas, parts, cores = lax.axis_size("rep"), lax.axis_size("parts"), lax.axis_size("tp")
    tok_count = tokens.shape[0]
    columns = expand_panels.shape[2] // cores
    panels = jnp.swapaxes(shrink_panels, 1, 2)
    rank = panels.shape[1]
    tie = lax.optimization_barrier

    alone, half = max(2, parts), replicas // 2

    def grouped(steps):
        size = len(steps) // parts
        return [tuple(steps[p * size + g] for p in range(parts)) for g in range(size)]

    far = grouped(list(range(half, replicas)))
    near = grouped(list(range(alone, half)))
    groups = far + near
    solo = [(step,) * parts for step in range(1, alone)]

    def hop(x, group):
        pairs = [
            (p * replicas + i, p * replicas + (i ^ group[p]))
            for p in range(parts)
            for i in range(replicas)
        ]
        return lax.ppermute(x, ("parts", "rep"), pairs)

    def shift_parts(x, shift):
        return lax.ppermute(x, "parts", [(i, (i + shift) % parts) for i in range(parts)])

    def shift_cores(x, shift):
        return lax.ppermute(x, "tp", [(i, (i + shift) % cores) for i in range(cores)])

    tables = (adapter_home, fetch_list, panels, expand_panels)
    groups = far + near + solo
    send = pack(groups, columns, *tables)
    tokens, send = tie((tokens, send))
    recv = [hop(x, group) for x, group in zip(send, groups)]
    tokens_of = [tokens] + [shift_parts(tokens, shift) for shift in range(1, parts)]
    solo_recv = recv[len(far) + len(near) :]
    near_recv = recv[len(far) : len(far) + len(near)]
    base_weight, seg_len, near_recv = tie((base_weight, seg_len, near_recv))
    base = base_terms(tokens, base_weight, cores)
    base, recv[: len(far) - 1] = tie((base, recv[: len(far) - 1]))
    base = base[:1] + [shift_cores(x, shift + 1) for shift, x in enumerate(base[1:])]
    lengths_of = [seg_len] + [shift_parts(seg_len, shift) for shift in range(1, parts)]
    early, early_groups = near_recv + recv[: len(far) - 1], near + far[:-1]
    last, last_group, own_group = recv[len(far) - 1], far[-1], (0,) * parts

    count = len(early)
    first, sent = score(
        [tuple(range(count + len(solo) + 1))],
        early_groups + solo + [own_group],
        tuple(range(count)),
        tables,
        columns,
        lengths_of[:1],
        [tokens],
        early + solo_recv + [panels],
    )
    passed = [shift_parts(sent, shift) for shift in range(1, parts)]
    base, first, passed, tokens_of[1:], last = tie((base, first, passed, tokens_of[1:], last))
    scores, sent = score(
        [(0,)] + [tuple(range(count + 1))] * (parts - 1),
        [last_group] + early_groups,
        (0,),
        tables,
        columns,
        lengths_of,
        tokens_of,
        [last] + early,
        first,
    )
    last_passed = [shift_parts(sent, shift) for shift in range(1, parts)]
    halves = [scores] + [shift_cores(scores, shift) for shift in range(1, cores)]
    whole = halves[0]
    for x in halves[1:]:
        whole = whole + x
    came = [
        shift_parts(whole[:, shift * tok_count : (shift + 1) * tok_count], -shift)
        for shift in range(1, parts)
    ]
    arrays = early + solo_recv + [last] + passed + last_passed
    pieces = [(None, 0, own_group)]
    pieces += [(n, 0, group) for n, group in enumerate(early_groups + solo + [last_group])]
    at = len(pieces) - 1
    for shift in range(1, parts):
        pieces += [(at, n * rank, turned(group, shift)) for n, group in enumerate(early_groups)]
        pieces.append((at + parts - 1, 0, turned(last_group, shift)))
        at += 1
    return finish(pieces, tables, seg_len, halves, came, base, arrays)


def solution(mesh):
    return jax.shard_map(
        on_device,
        mesh=mesh,
        in_specs=(
            P(("parts", "rep"), "tp"),
            P("tp", None),
            P("rep", "tp", None),
            P("rep", None, None),
            P(),
            P(),
            P(("parts", "rep"), None),
        ),
        out_specs=P(("parts", "rep"), "tp"),
        check_vma=False,
    )
```

```python
import functools
import jax
import jax.numpy as jnp
from jax import lax
from jax.experimental import pallas as pl
from jax.experimental.pallas import tpu as pltpu
from jax.sharding import PartitionSpec as P

adapter_scale = 2.0


def by_part(values):
    part = lax.axis_index("parts")
    chosen = jnp.int32(values[0])
    for p, value in enumerate(values):
        chosen = jnp.where(part == p, value, chosen)
    return chosen


def turned(group, shift):
    return tuple(group[(p - shift) % len(group)] for p in range(len(group)))


def slot_for(peer, me, per_home, home_ref, fetch_ref):
    first = me * per_home

    def look(j, slot):
        local = home_ref[fetch_ref[peer, j]] - first
        return jnp.where((local >= 0) & (local < per_home), local, slot)

    listed = fetch_ref.shape[1]
    return lax.fori_loop(0, listed, look, jnp.int32(0), unroll=listed <= 8)


def steps_of_rows(lengths_ref, count, me, per_home, home_ref, fetch_ref):
    rows = lax.broadcasted_iota(jnp.int32, (1, count), 1)
    result = jnp.zeros((1, count), jnp.int32)
    start = jnp.int32(0)
    for j in range(fetch_ref.shape[1]):
        step = lax.div(home_ref[fetch_ref[me, j]], jnp.int32(per_home)) ^ me
        result = jnp.where(rows >= start, step, result)
        start = start + lengths_ref[0, j]
    return result


def pack_kernel(groups, home_ref, fetch_ref, shrink_ref, expand_ref, *refs):
    count = len(groups)
    outs, held, in_sems, out_sems = refs[:count], refs[count], refs[count + 1], refs[count + 2]
    me = lax.axis_index("rep")
    per_home, _, depth = shrink_ref.shape
    columns = expand_ref.shape[2] // lax.axis_size("tp")
    left = pl.multiple_of(lax.axis_index("tp") * columns, 128)
    cuts = in_sems.shape[1] - 1
    width = depth // cuts
    arriving = []
    for at, group in enumerate(groups):
        slot = slot_for(me ^ by_part(group), me, per_home, home_ref, fetch_ref)
        pieces = [(shrink_ref.at[slot, :, pl.ds(n * width, width)], n * width, width) for n in range(cuts)]
        pieces.append((expand_ref.at[slot, :, pl.ds(left, columns)], depth, columns))
        for n, (source, start, size) in enumerate(pieces):
            target = held.at[at, :, pl.ds(start, size)]
            copy = pltpu.make_async_copy(source, target, in_sems.at[at, n])
            copy.start()
            leave = pltpu.make_async_copy(target, outs[at].at[:, pl.ds(start, size)], out_sems.at[at, n])
            arriving.append((copy, leave))
    for copy, leave in arriving:
        copy.wait()
        leave.start()
    for _, leave in arriving:
        leave.wait()


def pack(groups, columns, adapter_home, fetch_list, panels, expand_panels):
    rank, depth = panels.shape[1:]
    shape = (rank, depth + columns)
    cuts = 2
    return list(
        pl.pallas_call(
            functools.partial(pack_kernel, groups),
            out_shape=[jax.ShapeDtypeStruct(shape, panels.dtype)] * len(groups),
            in_specs=[pl.BlockSpec(memory_space=pltpu.SMEM)] * 2 + [pl.BlockSpec(memory_space=pl.ANY)] * 2,
            out_specs=[pl.BlockSpec(memory_space=pl.ANY)] * len(groups),
            scratch_shapes=[pltpu.VMEM((len(groups),) + shape, panels.dtype)]
            + [pltpu.SemaphoreType.DMA((len(groups), cuts + 1))] * 2,
            compiler_params=pltpu.CompilerParams(vmem_limit_bytes=56 << 20),
            cost_estimate=pl.CostEstimate(flops=0, bytes_accessed=0, transcendentals=0),
        )(adapter_home, fetch_list, panels, expand_panels)
    )


def score_kernel(plan, groups, chunks, has_prior, per_home, home_ref, fetch_ref, *refs):
    sets, many = len(plan), len(groups)
    lengths, refs = refs[:sets], refs[sets:]
    prior, refs = (refs[0], refs[1:]) if has_prior else (None, refs)
    tokens, panels = refs[:sets], refs[sets : sets + many]
    out, held_tokens, held_panels, sems = refs[sets + many :]
    me = lax.axis_index("rep")
    rank, count, depth = out.shape[0], held_tokens.shape[1], held_tokens.shape[2]
    width = depth // chunks
    slot = slot_for(me, me, per_home, home_ref, fetch_ref)
    copies = []
    for c in range(chunks):
        cols = pl.ds(c * width, width)
        pairs = []
        for n, ref in enumerate(panels):
            source = ref.at[:, cols] if len(ref.shape) == 2 else ref.at[slot, :, cols]
            pairs.append((source, held_panels.at[pl.ds(n * rank, rank), cols]))
        pairs += [(ref.at[:, cols], held_tokens.at[n, :, cols]) for n, ref in enumerate(tokens)]
        copies.append([])
        for n, (source, target) in enumerate(pairs):
            copies[-1].append(pltpu.make_async_copy(source, target, sems.at[c, n]))
            copies[-1][-1].start()
    row_steps = [steps_of_rows(x, count, me, per_home, home_ref, fetch_ref) for x in lengths]
    sums = [None] * sets
    for c in range(chunks):
        for copy in copies[c]:
            copy.wait()
        cols = pl.ds(c * width, width)
        for t, used in enumerate(plan):
            product = lax.dot_general(
                held_panels[pl.ds(used[0] * rank, len(used) * rank), cols],
                held_tokens[t, :, cols],
                (((1,), (1,)), ((), ())),
                preferred_element_type=jnp.float32,
            )
            sums[t] = product if c == 0 else sums[t] + product
    for t, used in enumerate(plan):
        mine = pl.ds(t * count, count)
        total = prior[:, mine] if has_prior else jnp.zeros((rank, count), jnp.float32)
        for n, panel in enumerate(used):
            term = sums[t][n * rank : (n + 1) * rank]
            total = total + jnp.where(row_steps[t] == by_part(groups[panel]), term, 0.0)
        out[:, mine] = total


def score(plan, groups, tables, lengths_of, tokens_of, panels, prior=None):
    count, depth = tokens_of[0].shape
    per_home, rank, _ = tables[2].shape
    chunks = 4
    prior = [] if prior is None else [prior]
    smem, vmem = pl.BlockSpec(memory_space=pltpu.SMEM), pl.BlockSpec(memory_space=pltpu.VMEM)
    copied = len(tokens_of) + len(panels)
    return pl.pallas_call(
        functools.partial(score_kernel, plan, groups, chunks, bool(prior), per_home),
        out_shape=jax.ShapeDtypeStruct((rank, len(plan) * count), jnp.float32),
        in_specs=[smem] * (2 + len(lengths_of))
        + [vmem] * len(prior)
        + [pl.BlockSpec(memory_space=pl.ANY)] * copied,
        out_specs=vmem,
        scratch_shapes=[
            pltpu.VMEM((len(tokens_of), count, depth), tokens_of[0].dtype),
            pltpu.VMEM((len(panels) * rank, depth), tokens_of[0].dtype),
            pltpu.SemaphoreType.DMA((chunks, copied)),
        ],
        compiler_params=pltpu.CompilerParams(vmem_limit_bytes=40 << 20),
        cost_estimate=pl.CostEstimate(flops=0, bytes_accessed=0, transcendentals=0),
    )(tables[0], tables[1], *lengths_of, *prior, *tokens_of, *panels)


def gather_kernel(*refs):
    blocks, out, sems = refs[:-2], refs[-2], refs[-1]
    columns = out.shape[1]
    copies, first = [], 0
    for n, block in enumerate(blocks):
        rows, width = block.shape
        source = block.at[:, pl.ds(width - columns, columns)]
        copies.append(pltpu.make_async_copy(source, out.at[pl.ds(first, rows)], sems.at[n]))
        copies[-1].start()
        first += rows
    for copy in copies:
        copy.wait()


def gather(blocks, columns):
    rows = sum(block.shape[0] for block in blocks)
    return pl.pallas_call(
        gather_kernel,
        out_shape=jax.ShapeDtypeStruct((rows, columns), blocks[0].dtype),
        in_specs=[pl.BlockSpec(memory_space=pl.ANY)] * len(blocks),
        out_specs=pl.BlockSpec(memory_space=pltpu.VMEM),
        scratch_shapes=[pltpu.SemaphoreType.DMA((len(blocks),))],
        cost_estimate=pl.CostEstimate(flops=0, bytes_accessed=0, transcendentals=0),
    )(*blocks)


def base_kernel(chunks, tokens_ref, weight_ref, *refs):
    outs, (held_tokens, held_weight, sems) = refs[:-3], refs[-3:]
    cores, half = len(outs), lax.axis_index("tp")
    columns = outs[0].shape[1]
    height = tokens_ref.shape[1] // chunks
    copies = []
    for c in range(chunks):
        rows = pl.ds(c * height, height)
        pairs = [(tokens_ref.at[:, rows], held_tokens.at[:, rows])]
        for shift in range(cores):
            left = pl.multiple_of(lax.rem(half + shift, cores) * columns, 128)
            pairs.append((weight_ref.at[rows, pl.ds(left, columns)], held_weight.at[shift, rows, :]))
        copies.append([])
        for n, (source, target) in enumerate(pairs):
            copies[-1].append(pltpu.make_async_copy(source, target, sems.at[c, n]))
            copies[-1][-1].start()
    for c in range(chunks):
        for copy in copies[c]:
            copy.wait()
        rows = pl.ds(c * height, height)
        for shift, out in enumerate(outs):
            product = jnp.dot(
                held_tokens[:, rows], held_weight[shift, rows, :], preferred_element_type=jnp.float32
            )
            if c == 0:
                out[...] = product
            else:
                out[...] += product


def base_terms(tokens, weight, cores):
    count, depth = tokens.shape
    columns = weight.shape[1] // cores
    chunks = 4
    return list(
        pl.pallas_call(
            functools.partial(base_kernel, chunks),
            out_shape=[jax.ShapeDtypeStruct((count, columns), jnp.float32)] * cores,
            in_specs=[pl.BlockSpec(memory_space=pl.ANY)] * 2,
            out_specs=[pl.BlockSpec(memory_space=pltpu.VMEM)] * cores,
            scratch_shapes=[
                pltpu.VMEM((count, depth), tokens.dtype),
                pltpu.VMEM((cores, depth, columns), weight.dtype),
                pltpu.SemaphoreType.DMA((chunks, 1 + cores)),
            ],
            compiler_params=pltpu.CompilerParams(vmem_limit_bytes=40 << 20),
            cost_estimate=pl.CostEstimate(flops=0, bytes_accessed=0, transcendentals=0),
        )(tokens, weight)
    )


def finish_kernel(pieces, added, came, bases, per_home, home_ref, fetch_ref, lengths_ref, *refs):
    scores, refs = refs[: added + came], refs[added + came :]
    base, expand_ref, refs = refs[:bases], refs[bases], refs[bases + 1 :]
    arrays, (out, held, held_scores, held_base, sems) = refs[:-5], refs[-5:]
    me = lax.axis_index("rep")
    count, columns = out.shape
    rank = scores[0].shape[0]
    left = pl.multiple_of(lax.axis_index("tp") * columns, 128)
    slot = slot_for(me, me, per_home, home_ref, fetch_ref)
    pairs = [(x.at[:, pl.ds(0, count)], held_scores.at[n]) for n, x in enumerate(scores)]
    pairs += [(x, held_base.at[n]) for n, x in enumerate(base)]
    for n, (at, row, _) in enumerate(pieces):
        if at is None:
            source = expand_ref.at[slot, :, pl.ds(left, columns)]
        else:
            source = arrays[at].at[pl.ds(row, rank), pl.ds(arrays[at].shape[1] - columns, columns)]
        pairs.append((source, held.at[pl.ds(n * rank, rank)]))
    copies = []
    for n, (source, target) in enumerate(pairs):
        copies.append(pltpu.make_async_copy(source, target, sems.at[n]))
        copies[-1].start()
    row_steps = steps_of_rows(lengths_ref, count, me, per_home, home_ref, fetch_ref)
    masks = [row_steps == by_part(group) for _, _, group in pieces]
    for copy in copies:
        copy.wait()
    shrink = held_scores[0]
    for n in range(1, added + came):
        shrink = shrink + held_scores[n]
    shrink = adapter_scale * shrink
    high = shrink.astype(jnp.bfloat16).astype(jnp.float32)
    total = held_base[0]
    for n in range(1, bases):
        total = total + held_base[n]
    for term in (high, shrink - high):
        wide = jnp.concatenate([jnp.where(mask, term, 0.0) for mask in masks], axis=0)
        total = total + lax.dot_general(
            wide.astype(jnp.bfloat16),
            held[...],
            (((0,), (0,)), ((), ())),
            preferred_element_type=jnp.float32,
        )
    out[...] = total.astype(out.dtype)


def finish(pieces, tables, lengths, scores, others, base, arrays):
    count, columns = base[0].shape
    per_home, rank, _ = tables[2].shape
    smem, anywhere = pl.BlockSpec(memory_space=pltpu.SMEM), pl.BlockSpec(memory_space=pl.ANY)
    copied = list(scores) + list(others) + list(base)
    return pl.pallas_call(
        functools.partial(finish_kernel, pieces, len(scores), len(others), len(base), per_home),
        out_shape=jax.ShapeDtypeStruct((count, columns), jnp.bfloat16),
        in_specs=[smem] * 3 + [anywhere] * (len(copied) + 1 + len(arrays)),
        out_specs=pl.BlockSpec(memory_space=pltpu.VMEM),
        scratch_shapes=[
            pltpu.VMEM((len(pieces) * rank, columns), jnp.bfloat16),
            pltpu.VMEM((len(scores) + len(others), rank, count), jnp.float32),
            pltpu.VMEM((len(base), count, columns), jnp.float32),
            pltpu.SemaphoreType.DMA((len(copied) + len(pieces),)),
        ],
        compiler_params=pltpu.CompilerParams(vmem_limit_bytes=24 << 20),
        cost_estimate=pl.CostEstimate(flops=0, bytes_accessed=0, transcendentals=0),
    )(tables[0], tables[1], lengths, *copied, tables[3], *arrays)


def on_device(tokens, base_weight, shrink_panels, expand_panels, adapter_home, fetch_list, seg_len):
    replicas, parts, cores = lax.axis_size("rep"), lax.axis_size("parts"), lax.axis_size("tp")
    tok_count = tokens.shape[0]
    columns = expand_panels.shape[2] // cores
    panels = jnp.swapaxes(shrink_panels, 1, 2)
    rank = panels.shape[1]
    tie = lax.optimization_barrier

    alone, half = max(2, parts), replicas // 2

    def grouped(steps):
        size = len(steps) // parts
        return [tuple(steps[p * size + g] for p in range(parts)) for g in range(size)]

    far = grouped(list(range(half, replicas)))
    near = grouped(list(range(alone, half)))
    groups = far + near
    solo = [(step,) * parts for step in range(1, alone)]

    def hop(x, group):
        pairs = [
            (p * replicas + i, p * replicas + (i ^ group[p]))
            for p in range(parts)
            for i in range(replicas)
        ]
        return lax.ppermute(x, ("parts", "rep"), pairs)

    def shift_parts(x, shift):
        return lax.ppermute(x, "parts", [(i, (i + shift) % parts) for i in range(parts)])

    def shift_cores(x, shift):
        return lax.ppermute(x, "tp", [(i, (i + shift) % cores) for i in range(cores)])

    tables = (adapter_home, fetch_list, panels, expand_panels)
    groups = far + near + solo
    send = pack(groups, columns, *tables)
    tokens, send = tie((tokens, send))
    recv = [hop(x, group) for x, group in zip(send, groups)]
    tokens_of = [tokens] + [shift_parts(tokens, shift) for shift in range(1, parts)]
    solo_recv = recv[len(far) + len(near) :]
    near_recv = recv[len(far) : len(far) + len(near)]
    base_weight, seg_len, near_recv = tie((base_weight, seg_len, near_recv))
    base = base_terms(tokens, base_weight, cores)
    base, recv[: len(far) - 1] = tie((base, recv[: len(far) - 1]))
    base = base[:1] + [shift_cores(x, shift + 1) for shift, x in enumerate(base[1:])]
    lengths_of = [seg_len] + [shift_parts(seg_len, shift) for shift in range(1, parts)]
    early, early_groups = near_recv + recv[: len(far) - 1], near + far[:-1]
    last, last_group, own_group = recv[len(far) - 1], far[-1], (0,) * parts

    count = len(early)
    sent = gather(early, columns)
    passed = [shift_parts(sent, shift) for shift in range(1, parts)]
    first = score(
        [tuple(range(count + len(solo) + 1))] + [tuple(range(count))] * (parts - 1),
        early_groups + solo + [own_group],
        tables,
        lengths_of,
        tokens_of,
        early + solo_recv + [panels],
    )
    base, first, passed, last = tie((base, first, passed, last))
    scores = score([(0,)] * parts, [last_group], tables, lengths_of, tokens_of, [last], first)
    last_passed = [shift_parts(gather([last], columns), shift) for shift in range(1, parts)]
    halves = [scores] + [shift_cores(scores, shift) for shift in range(1, cores)]
    whole = halves[0]
    for x in halves[1:]:
        whole = whole + x
    came = [
        shift_parts(whole[:, shift * tok_count : (shift + 1) * tok_count], -shift)
        for shift in range(1, parts)
    ]
    arrays = early + solo_recv + [last] + passed + last_passed
    pieces = [(None, 0, own_group)]
    pieces += [(n, 0, group) for n, group in enumerate(early_groups + solo + [last_group])]
    at = len(pieces) - 1
    for shift in range(1, parts):
        pieces += [(at, n * rank, turned(group, shift)) for n, group in enumerate(early_groups)]
        pieces.append((at + parts - 1, 0, turned(last_group, shift)))
        at += 1
    return finish(pieces, tables, seg_len, halves, came, base, arrays)


def solution(mesh):
    return jax.shard_map(
        on_device,
        mesh=mesh,
        in_specs=(
            P(("parts", "rep"), "tp"),
            P("tp", None),
            P("rep", "tp", None),
            P("rep", None, None),
            P(),
            P(),
            P(("parts", "rep"), None),
        ),
        out_specs=P(("parts", "rep"), "tp"),
        check_vma=False,
    )
```

```python
import functools
import jax
import jax.numpy as jnp
from jax import lax
from jax.experimental import pallas as pl
from jax.experimental.pallas import tpu as pltpu
from jax.sharding import PartitionSpec as P

adapter_scale = 2.0


def by_part(values):
    part = lax.axis_index("parts")
    chosen = jnp.int32(values[0])
    for p, value in enumerate(values):
        chosen = jnp.where(part == p, value, chosen)
    return chosen


def turned(group, shift):
    return tuple(group[(p - shift) % len(group)] for p in range(len(group)))


def slot_for(peer, me, per_home, home_ref, fetch_ref):
    first = me * per_home

    def look(j, slot):
        local = home_ref[fetch_ref[peer, j]] - first
        return jnp.where((local >= 0) & (local < per_home), local, slot)

    listed = fetch_ref.shape[1]
    return lax.fori_loop(0, listed, look, jnp.int32(0), unroll=listed <= 8)


def steps_of_rows(lengths_ref, count, me, per_home, home_ref, fetch_ref):
    rows = lax.broadcasted_iota(jnp.int32, (1, count), 1)
    result = jnp.zeros((1, count), jnp.int32)
    start = jnp.int32(0)
    for j in range(fetch_ref.shape[1]):
        step = lax.div(home_ref[fetch_ref[me, j]], jnp.int32(per_home)) ^ me
        result = jnp.where(rows >= start, step, result)
        start = start + lengths_ref[0, j]
    return result


def pack_kernel(groups, home_ref, fetch_ref, lengths_ref, shrink_ref, expand_ref, *refs):
    count = len(groups)
    outs, steps_out, refs = refs[:count], refs[count], refs[count + 1 :]
    held, in_sems, out_sems = refs
    me = lax.axis_index("rep")
    per_home, _, depth = shrink_ref.shape
    columns = expand_ref.shape[2] // lax.axis_size("tp")
    left = pl.multiple_of(lax.axis_index("tp") * columns, 128)
    cuts = in_sems.shape[1] - 1
    width = depth // cuts
    arriving = []
    for at, group in enumerate(groups):
        slot = slot_for(me ^ by_part(group), me, per_home, home_ref, fetch_ref)
        pieces = [(shrink_ref.at[slot, :, pl.ds(n * width, width)], n * width, width) for n in range(cuts)]
        pieces.append((expand_ref.at[slot, :, pl.ds(left, columns)], depth, columns))
        for n, (source, start, size) in enumerate(pieces):
            target = held.at[at, :, pl.ds(start, size)]
            copy = pltpu.make_async_copy(source, target, in_sems.at[at, n])
            copy.start()
            leave = pltpu.make_async_copy(target, outs[at].at[:, pl.ds(start, size)], out_sems.at[at, n])
            arriving.append((copy, leave))
    steps = steps_of_rows(lengths_ref, steps_out.shape[1], me, per_home, home_ref, fetch_ref)
    steps_out[...] = jnp.broadcast_to(steps, steps_out.shape)
    for copy, leave in arriving:
        copy.wait()
        leave.start()
    for _, leave in arriving:
        leave.wait()


def pack(groups, columns, count, lengths, adapter_home, fetch_list, panels, expand_panels):
    rank, depth = panels.shape[1:]
    shape = (rank, depth + columns)
    cuts = 2
    return list(
        pl.pallas_call(
            functools.partial(pack_kernel, groups),
            out_shape=[jax.ShapeDtypeStruct(shape, panels.dtype)] * len(groups)
            + [jax.ShapeDtypeStruct((8, count), jnp.int32)],
            in_specs=[pl.BlockSpec(memory_space=pltpu.SMEM)] * 3 + [pl.BlockSpec(memory_space=pl.ANY)] * 2,
            out_specs=[pl.BlockSpec(memory_space=pl.ANY)] * len(groups)
            + [pl.BlockSpec(memory_space=pltpu.VMEM)],
            scratch_shapes=[pltpu.VMEM((len(groups),) + shape, panels.dtype)]
            + [pltpu.SemaphoreType.DMA((len(groups), cuts + 1))] * 2,
            compiler_params=pltpu.CompilerParams(vmem_limit_bytes=56 << 20),
            cost_estimate=pl.CostEstimate(flops=0, bytes_accessed=0, transcendentals=0),
        )(adapter_home, fetch_list, lengths, panels, expand_panels)
    )


def score_kernel(plan, groups, kept, own, chunks, has_prior, *refs):
    sets, many = len(plan), len(groups)
    tables, refs = (refs[:2], refs[2:]) if own else (None, refs)
    row_steps, refs = refs[:sets], refs[sets:]
    prior, refs = (refs[0], refs[1:]) if has_prior else (None, refs)
    tokens, panels, refs = refs[:sets], refs[sets : sets + many], refs[sets + many :]
    expand_ref, refs = (refs[0], refs[1:]) if own else (None, refs)
    out, out_expand, refs = refs[0], refs[1], refs[2:]
    out_own, refs = (refs[0], refs[1:]) if own else (None, refs)
    held_tokens, held_panels, sems = refs
    rank, count, depth = out.shape[0], held_tokens.shape[1], held_tokens.shape[2]
    width, columns = depth // chunks, out_expand.shape[1]
    if own:
        me = lax.axis_index("rep")
        slot = slot_for(me, me, panels[-1].shape[0], *tables)
    copies = []
    for c in range(chunks):
        cols = pl.ds(c * width, width)
        pairs = []
        for n, ref in enumerate(panels):
            source = ref.at[:, cols] if len(ref.shape) == 2 else ref.at[slot, :, cols]
            pairs.append((source, held_panels.at[pl.ds(n * rank, rank), cols]))
        pairs += [(ref.at[:, cols], held_tokens.at[n, :, cols]) for n, ref in enumerate(tokens)]
        if c == chunks - 1:
            pairs += [
                (panels[n].at[:, pl.ds(depth, columns)], out_expand.at[pl.ds(i * rank, rank)])
                for i, n in enumerate(kept)
            ]
            if own:
                left = pl.multiple_of(lax.axis_index("tp") * columns, 128)
                pairs.append((expand_ref.at[slot, :, pl.ds(left, columns)], out_own))
        copies.append([])
        for n, (source, target) in enumerate(pairs):
            copies[-1].append(pltpu.make_async_copy(source, target, sems.at[c, n]))
            copies[-1][-1].start()
    sums = [None] * sets
    for c in range(chunks):
        for copy in copies[c]:
            copy.wait()
        cols = pl.ds(c * width, width)
        for t, used in enumerate(plan):
            product = lax.dot_general(
                held_panels[pl.ds(used[0] * rank, len(used) * rank), cols],
                held_tokens[t, :, cols],
                (((1,), (1,)), ((), ())),
                preferred_element_type=jnp.float32,
            )
            sums[t] = product if c == 0 else sums[t] + product
    for t, used in enumerate(plan):
        mine = row_steps[t][pl.ds(0, 1), :]
        total = prior[...] if has_prior and t == 0 else jnp.zeros((rank, count), jnp.float32)
        for n, panel in enumerate(used):
            term = sums[t][n * rank : (n + 1) * rank]
            total = total + jnp.where(mine == by_part(groups[panel]), term, 0.0)
        out[:, pl.ds(t * count, count)] = total


def score(plan, groups, kept, columns, row_steps, tokens_of, panels, prior=None, tables=None):
    count, depth = tokens_of[0].shape
    rank = panels[0].shape[0]
    chunks = 4
    own = tables is not None
    prior = [] if prior is None else [prior]
    smem, vmem = pl.BlockSpec(memory_space=pltpu.SMEM), pl.BlockSpec(memory_space=pltpu.VMEM)
    copied = list(tokens_of) + list(panels) + ([tables[3]] if own else [])
    outs = [(rank, len(plan) * count), (len(kept) * rank, columns)] + [(rank, columns)] * own
    return pl.pallas_call(
        functools.partial(score_kernel, plan, groups, kept, own, chunks, bool(prior)),
        out_shape=[
            jax.ShapeDtypeStruct(shape, panels[0].dtype if n else jnp.float32)
            for n, shape in enumerate(outs)
        ],
        in_specs=[smem] * (2 * own)
        + [vmem] * (len(row_steps) + len(prior))
        + [pl.BlockSpec(memory_space=pl.ANY)] * len(copied),
        out_specs=[vmem] * len(outs),
        scratch_shapes=[
            pltpu.VMEM((len(tokens_of), count, depth), tokens_of[0].dtype),
            pltpu.VMEM((len(panels) * rank, depth), tokens_of[0].dtype),
            pltpu.SemaphoreType.DMA((chunks, len(copied) + len(kept))),
        ],
        compiler_params=pltpu.CompilerParams(vmem_limit_bytes=40 << 20),
        cost_estimate=pl.CostEstimate(flops=0, bytes_accessed=0, transcendentals=0),
    )(*(tables[:2] if own else ()), *row_steps, *prior, *copied)


def base_kernel(chunks, tokens_ref, weight_ref, *refs):
    outs, (held_tokens, held_weight, sems) = refs[:-3], refs[-3:]
    cores, half = len(outs), lax.axis_index("tp")
    columns = outs[0].shape[1]
    height = tokens_ref.shape[1] // chunks
    copies = []
    for c in range(chunks):
        rows = pl.ds(c * height, height)
        pairs = [(tokens_ref.at[:, rows], held_tokens.at[:, rows])]
        for shift in range(cores):
            left = pl.multiple_of(lax.rem(half + shift, cores) * columns, 128)
            pairs.append((weight_ref.at[rows, pl.ds(left, columns)], held_weight.at[shift, rows, :]))
        copies.append([])
        for n, (source, target) in enumerate(pairs):
            copies[-1].append(pltpu.make_async_copy(source, target, sems.at[c, n]))
            copies[-1][-1].start()
    for c in range(chunks):
        for copy in copies[c]:
            copy.wait()
        rows = pl.ds(c * height, height)
        for shift, out in enumerate(outs):
            product = jnp.dot(
                held_tokens[:, rows], held_weight[shift, rows, :], preferred_element_type=jnp.float32
            )
            if c == 0:
                out[...] = product
            else:
                out[...] += product


def base_terms(tokens, weight, cores):
    count, depth = tokens.shape
    columns = weight.shape[1] // cores
    chunks = 4
    return list(
        pl.pallas_call(
            functools.partial(base_kernel, chunks),
            out_shape=[jax.ShapeDtypeStruct((count, columns), jnp.float32)] * cores,
            in_specs=[pl.BlockSpec(memory_space=pl.ANY)] * 2,
            out_specs=[pl.BlockSpec(memory_space=pltpu.VMEM)] * cores,
            scratch_shapes=[
                pltpu.VMEM((count, depth), tokens.dtype),
                pltpu.VMEM((cores, depth, columns), weight.dtype),
                pltpu.SemaphoreType.DMA((chunks, 1 + cores)),
            ],
            compiler_params=pltpu.CompilerParams(vmem_limit_bytes=40 << 20),
            cost_estimate=pl.CostEstimate(flops=0, bytes_accessed=0, transcendentals=0),
        )(tokens, weight)
    )


def end_kernel(pieces, added, bases, row_steps, *refs):
    scores, base, refs = refs[:added], refs[added : added + bases], refs[added + bases :]
    arrays, (out, held, sems) = refs[:-3], refs[-3:]
    count, columns = out.shape
    rank = scores[0].shape[0]
    copies = []
    for n, (at, row, _) in enumerate(pieces):
        source = arrays[at].at[pl.ds(row, rank), pl.ds(arrays[at].shape[1] - columns, columns)]
        copies.append(pltpu.make_async_copy(source, held.at[pl.ds(n * rank, rank)], sems.at[n]))
        copies[-1].start()
    shrink = scores[0][:, pl.ds(0, count)]
    for x in scores[1:]:
        shrink = shrink + x[:, pl.ds(0, count)]
    shrink = adapter_scale * shrink
    high = shrink.astype(jnp.bfloat16).astype(jnp.float32)
    masks = [row_steps[pl.ds(0, 1), :] == by_part(group) for _, _, group in pieces]
    total = base[0][...]
    for x in base[1:]:
        total = total + x[...]
    for copy in copies:
        copy.wait()
    for term in (high, shrink - high):
        wide = jnp.concatenate([jnp.where(mask, term, 0.0) for mask in masks], axis=0)
        total = total + lax.dot_general(
            wide.astype(jnp.bfloat16),
            held[...],
            (((0,), (0,)), ((), ())),
            preferred_element_type=jnp.float32,
        )
    out[...] = total.astype(out.dtype)


def end(pieces, row_steps, scores, base, arrays, kind, cost):
    count, columns = base[0].shape
    rank = scores[0].shape[0]
    vmem = pl.BlockSpec(memory_space=pltpu.VMEM)
    return pl.pallas_call(
        functools.partial(end_kernel, pieces, len(scores), len(base)),
        out_shape=jax.ShapeDtypeStruct((count, columns), kind),
        in_specs=[vmem] * (1 + len(scores) + len(base))
        + [pl.BlockSpec(memory_space=pl.ANY)] * len(arrays),
        out_specs=vmem,
        scratch_shapes=[
            pltpu.VMEM((len(pieces) * rank, columns), jnp.bfloat16),
            pltpu.SemaphoreType.DMA((len(pieces),)),
        ],
        compiler_params=pltpu.CompilerParams(vmem_limit_bytes=24 << 20),
        cost_estimate=pl.CostEstimate(flops=0, bytes_accessed=cost, transcendentals=0),
    )(row_steps, *scores, *base, *arrays)


def on_device(tokens, base_weight, shrink_panels, expand_panels, adapter_home, fetch_list, seg_len):
    replicas, parts, cores = lax.axis_size("rep"), lax.axis_size("parts"), lax.axis_size("tp")
    tok_count = tokens.shape[0]
    columns = expand_panels.shape[2] // cores
    panels = jnp.swapaxes(shrink_panels, 1, 2)
    rank = panels.shape[1]
    tie = lax.optimization_barrier

    alone, half = max(2, parts), replicas // 2

    def grouped(steps):
        size = len(steps) // parts
        return [tuple(steps[p * size + g] for p in range(parts)) for g in range(size)]

    far = grouped(list(range(half, replicas)))
    near = grouped(list(range(alone, half)))
    groups = far + near
    solo = [(step,) * parts for step in range(1, alone)]

    def hop(x, group):
        pairs = [
            (p * replicas + i, p * replicas + (i ^ group[p]))
            for p in range(parts)
            for i in range(replicas)
        ]
        return lax.ppermute(x, ("parts", "rep"), pairs)

    def shift_parts(x, shift):
        return lax.ppermute(x, "parts", [(i, (i + shift) % parts) for i in range(parts)])

    def shift_cores(x, shift):
        return lax.ppermute(x, "tp", [(i, (i + shift) % cores) for i in range(cores)])

    tables = (adapter_home, fetch_list, panels, expand_panels)
    groups = far + near + solo
    *send, row_steps = pack(groups, columns, tok_count, seg_len, *tables)
    tokens, send = tie((tokens, send))
    recv = [hop(x, group) for x, group in zip(send, groups)]
    tokens_of = [tokens] + [shift_parts(tokens, shift) for shift in range(1, parts)]
    solo_recv = recv[len(far) + len(near) :]
    near_recv = recv[len(far) : len(far) + len(near)]
    base_weight, row_steps, near_recv = tie((base_weight, row_steps, near_recv))
    base = base_terms(tokens, base_weight, cores)
    base, recv[: len(far) - 1] = tie((base, recv[: len(far) - 1]))
    base = base[:1] + [shift_cores(x, shift + 1) for shift, x in enumerate(base[1:])]
    steps_of = [row_steps] + [shift_parts(row_steps, shift) for shift in range(1, parts)]
    early, early_groups = near_recv + recv[: len(far) - 1], near + far[:-1]
    last, last_group, own_group = recv[len(far) - 1], far[-1], (0,) * parts

    count = len(early)
    first, sent, own_expand = score(
        [tuple(range(count + len(solo) + 1))],
        early_groups + solo + [own_group],
        tuple(range(count)),
        columns,
        steps_of[:1],
        [tokens],
        early + solo_recv + [panels],
        tables=tables,
    )
    passed = [shift_parts(sent, shift) for shift in range(1, parts)]
    base, first, passed, tokens_of[1:], last = tie((base, first, passed, tokens_of[1:], last))
    scores, sent = score(
        [(0,)] + [tuple(range(count + 1))] * (parts - 1),
        [last_group] + early_groups,
        (0,),
        columns,
        steps_of,
        tokens_of,
        [last] + early,
        first,
    )
    last_passed = [shift_parts(sent, shift) for shift in range(1, parts)]
    halves = [scores] + [shift_cores(scores, shift) for shift in range(1, cores)]
    whole = halves[0]
    for x in halves[1:]:
        whole = whole + x
    came = [
        shift_parts(whole[:, shift * tok_count : (shift + 1) * tok_count], -shift)
        for shift in range(1, parts)
    ]
    arrays = [own_expand] + early + solo_recv + [last]
    pieces = [(n, 0, group) for n, group in enumerate([own_group] + early_groups + solo + [last_group])]
    result = end(pieces, row_steps, halves, base, arrays, jnp.float32, 1 << 24)
    pieces = []
    for shift in range(1, parts):
        at = shift - 1
        pieces += [(at, n * rank, turned(group, shift)) for n, group in enumerate(early_groups)]
        pieces.append((at + parts - 1, 0, turned(last_group, shift)))
    return end(pieces, row_steps, came, [result], passed + last_passed, jnp.bfloat16, 0)


def solution(mesh):
    return jax.shard_map(
        on_device,
        mesh=mesh,
        in_specs=(
            P(("parts", "rep"), "tp"),
            P("tp", None),
            P("rep", "tp", None),
            P("rep", None, None),
            P(),
            P(),
            P(("parts", "rep"), None),
        ),
        out_specs=P(("parts", "rep"), "tp"),
        check_vma=False,
    )
```

```python
import functools
import jax
import jax.numpy as jnp
from jax import lax
from jax.experimental import pallas as pl
from jax.experimental.pallas import tpu as pltpu
from jax.sharding import PartitionSpec as P

adapter_scale = 2.0


def by_part(values):
    part = lax.axis_index("parts")
    chosen = jnp.int32(values[0])
    for p, value in enumerate(values):
        chosen = jnp.where(part == p, value, chosen)
    return chosen


def turned(group, shift):
    return tuple(group[(p - shift) % len(group)] for p in range(len(group)))


def slot_for(peer, me, per_home, home_ref, fetch_ref):
    first = me * per_home

    def look(j, slot):
        local = home_ref[fetch_ref[peer, j]] - first
        return jnp.where((local >= 0) & (local < per_home), local, slot)

    listed = fetch_ref.shape[1]
    return lax.fori_loop(0, listed, look, jnp.int32(0), unroll=listed <= 8)


def steps_kernel(per_home, home_ref, fetch_ref, lengths_ref, out):
    me = lax.axis_index("rep")
    rows = lax.broadcasted_iota(jnp.int32, out.shape, 1)
    result = jnp.zeros(out.shape, jnp.int32)
    start = jnp.int32(0)
    for j in range(fetch_ref.shape[1]):
        step = lax.div(home_ref[fetch_ref[me, j]], jnp.int32(per_home)) ^ me
        result = jnp.where(rows >= start, step, result)
        start = start + lengths_ref[0, j]
    out[...] = result


def steps_of_rows(count, per_home, adapter_home, fetch_list, seg_len):
    return pl.pallas_call(
        functools.partial(steps_kernel, per_home),
        out_shape=jax.ShapeDtypeStruct((8, count), jnp.int32),
        in_specs=[pl.BlockSpec(memory_space=pltpu.SMEM)] * 3,
        out_specs=pl.BlockSpec(memory_space=pltpu.VMEM),
        cost_estimate=pl.CostEstimate(flops=0, bytes_accessed=0, transcendentals=0),
    )(adapter_home, fetch_list, seg_len)


def pack_kernel(groups, home_ref, fetch_ref, shrink_ref, expand_ref, *refs):
    outs, (held, in_sems, out_sems) = refs[:-3], refs[-3:]
    me = lax.axis_index("rep")
    per_home, _, depth = shrink_ref.shape
    columns = expand_ref.shape[2] // lax.axis_size("tp")
    left = pl.multiple_of(lax.axis_index("tp") * columns, 128)
    cuts = in_sems.shape[1] - 1
    width = depth // cuts
    arriving = []
    for at, group in enumerate(groups):
        slot = slot_for(me ^ by_part(group), me, per_home, home_ref, fetch_ref)
        pieces = [(shrink_ref.at[slot, :, pl.ds(n * width, width)], n * width, width) for n in range(cuts)]
        pieces.append((expand_ref.at[slot, :, pl.ds(left, columns)], depth, columns))
        for n, (source, start, size) in enumerate(pieces):
            target = held.at[at, :, pl.ds(start, size)]
            copy = pltpu.make_async_copy(source, target, in_sems.at[at, n])
            copy.start()
            leave = pltpu.make_async_copy(target, outs[at].at[:, pl.ds(start, size)], out_sems.at[at, n])
            arriving.append((copy, leave))
    for copy, leave in arriving:
        copy.wait()
        leave.start()
    for _, leave in arriving:
        leave.wait()


def pack(groups, columns, adapter_home, fetch_list, panels, expand_panels):
    rank, depth = panels.shape[1:]
    shape = (rank, depth + columns)
    cuts = 2
    return list(
        pl.pallas_call(
            functools.partial(pack_kernel, groups),
            out_shape=[jax.ShapeDtypeStruct(shape, panels.dtype)] * len(groups),
            in_specs=[pl.BlockSpec(memory_space=pltpu.SMEM)] * 2 + [pl.BlockSpec(memory_space=pl.ANY)] * 2,
            out_specs=[pl.BlockSpec(memory_space=pl.ANY)] * len(groups),
            scratch_shapes=[pltpu.VMEM((len(groups),) + shape, panels.dtype)]
            + [pltpu.SemaphoreType.DMA((len(groups), cuts + 1))] * 2,
            compiler_params=pltpu.CompilerParams(vmem_limit_bytes=56 << 20),
            cost_estimate=pl.CostEstimate(flops=0, bytes_accessed=0, transcendentals=0),
        )(adapter_home, fetch_list, panels, expand_panels)
    )


def score_kernel(plan, groups, kept, own, chunks, has_prior, *refs):
    sets, many = len(plan), len(groups)
    tables, refs = (refs[:2], refs[2:]) if own else (None, refs)
    row_steps, refs = refs[:sets], refs[sets:]
    prior, refs = (refs[0], refs[1:]) if has_prior else (None, refs)
    tokens, panels, refs = refs[:sets], refs[sets : sets + many], refs[sets + many :]
    expand_ref, refs = (refs[0], refs[1:]) if own else (None, refs)
    out, out_expand, refs = refs[0], refs[1], refs[2:]
    out_own, refs = (refs[0], refs[1:]) if own else (None, refs)
    held_tokens, held_panels, sems = refs
    rank, count, depth = out.shape[0], held_tokens.shape[1], held_tokens.shape[2]
    width, columns = depth // chunks, out_expand.shape[1]
    if own:
        me = lax.axis_index("rep")
        slot = slot_for(me, me, panels[-1].shape[0], *tables)
    copies = []
    for c in range(chunks):
        cols = pl.ds(c * width, width)
        pairs = []
        for n, ref in enumerate(panels):
            source = ref.at[:, cols] if len(ref.shape) == 2 else ref.at[slot, :, cols]
            pairs.append((source, held_panels.at[pl.ds(n * rank, rank), cols]))
        pairs += [(ref.at[:, cols], held_tokens.at[n, :, cols]) for n, ref in enumerate(tokens)]
        if c == chunks - 1:
            pairs += [
                (panels[n].at[:, pl.ds(depth, columns)], out_expand.at[pl.ds(i * rank, rank)])
                for i, n in enumerate(kept)
            ]
            if own:
                left = pl.multiple_of(lax.axis_index("tp") * columns, 128)
                pairs.append((expand_ref.at[slot, :, pl.ds(left, columns)], out_own))
        copies.append([])
        for n, (source, target) in enumerate(pairs):
            copies[-1].append(pltpu.make_async_copy(source, target, sems.at[c, n]))
            copies[-1][-1].start()
    sums = [None] * sets
    for c in range(chunks):
        for copy in copies[c]:
            copy.wait()
        cols = pl.ds(c * width, width)
        for t, used in enumerate(plan):
            product = lax.dot_general(
                held_panels[pl.ds(used[0] * rank, len(used) * rank), cols],
                held_tokens[t, :, cols],
                (((1,), (1,)), ((), ())),
                preferred_element_type=jnp.float32,
            )
            sums[t] = product if c == 0 else sums[t] + product
    for t, used in enumerate(plan):
        mine = row_steps[t][pl.ds(0, 1), :]
        total = prior[...] if has_prior and t == 0 else jnp.zeros((rank, count), jnp.float32)
        for n, panel in enumerate(used):
            term = sums[t][n * rank : (n + 1) * rank]
            total = total + jnp.where(mine == by_part(groups[panel]), term, 0.0)
        out[:, pl.ds(t * count, count)] = total


def score(plan, groups, kept, columns, row_steps, tokens_of, panels, prior=None, tables=None):
    count, depth = tokens_of[0].shape
    rank = panels[0].shape[0]
    chunks = 4
    own = tables is not None
    prior = [] if prior is None else [prior]
    smem, vmem = pl.BlockSpec(memory_space=pltpu.SMEM), pl.BlockSpec(memory_space=pltpu.VMEM)
    copied = list(tokens_of) + list(panels) + ([tables[3]] if own else [])
    outs = [(rank, len(plan) * count), (len(kept) * rank, columns)] + [(rank, columns)] * own
    return pl.pallas_call(
        functools.partial(score_kernel, plan, groups, kept, own, chunks, bool(prior)),
        out_shape=[
            jax.ShapeDtypeStruct(shape, panels[0].dtype if n else jnp.float32)
            for n, shape in enumerate(outs)
        ],
        in_specs=[smem] * (2 * own)
        + [vmem] * (len(row_steps) + len(prior))
        + [pl.BlockSpec(memory_space=pl.ANY)] * len(copied),
        out_specs=[vmem] * len(outs),
        scratch_shapes=[
            pltpu.VMEM((len(tokens_of), count, depth), tokens_of[0].dtype),
            pltpu.VMEM((len(panels) * rank, depth), tokens_of[0].dtype),
            pltpu.SemaphoreType.DMA((chunks, len(copied) + len(kept))),
        ],
        compiler_params=pltpu.CompilerParams(vmem_limit_bytes=40 << 20),
        cost_estimate=pl.CostEstimate(flops=0, bytes_accessed=0, transcendentals=0),
    )(*(tables[:2] if own else ()), *row_steps, *prior, *copied)


def base_kernel(chunks, tokens_ref, weight_ref, *refs):
    outs, (held_tokens, held_weight, sems) = refs[:-3], refs[-3:]
    cores, half = len(outs), lax.axis_index("tp")
    columns = outs[0].shape[1]
    height = tokens_ref.shape[1] // chunks
    copies = []
    for c in range(chunks):
        rows = pl.ds(c * height, height)
        pairs = [(tokens_ref.at[:, rows], held_tokens.at[:, rows])]
        for shift in range(cores):
            left = pl.multiple_of(lax.rem(half + shift, cores) * columns, 128)
            pairs.append((weight_ref.at[rows, pl.ds(left, columns)], held_weight.at[shift, rows, :]))
        copies.append([])
        for n, (source, target) in enumerate(pairs):
            copies[-1].append(pltpu.make_async_copy(source, target, sems.at[c, n]))
            copies[-1][-1].start()
    for c in range(chunks):
        for copy in copies[c]:
            copy.wait()
        rows = pl.ds(c * height, height)
        for shift, out in enumerate(outs):
            product = jnp.dot(
                held_tokens[:, rows], held_weight[shift, rows, :], preferred_element_type=jnp.float32
            )
            if c == 0:
                out[...] = product
            else:
                out[...] += product


def base_terms(tokens, weight, cores):
    count, depth = tokens.shape
    columns = weight.shape[1] // cores
    chunks = 4
    return list(
        pl.pallas_call(
            functools.partial(base_kernel, chunks),
            out_shape=[jax.ShapeDtypeStruct((count, columns), jnp.float32)] * cores,
            in_specs=[pl.BlockSpec(memory_space=pl.ANY)] * 2,
            out_specs=[pl.BlockSpec(memory_space=pltpu.VMEM)] * cores,
            scratch_shapes=[
                pltpu.VMEM((count, depth), tokens.dtype),
                pltpu.VMEM((cores, depth, columns), weight.dtype),
                pltpu.SemaphoreType.DMA((chunks, 1 + cores)),
            ],
            compiler_params=pltpu.CompilerParams(vmem_limit_bytes=40 << 20),
            cost_estimate=pl.CostEstimate(flops=0, bytes_accessed=0, transcendentals=0),
        )(tokens, weight)
    )


def end_kernel(pieces, added, bases, row_steps, *refs):
    scores, base, refs = refs[:added], refs[added : added + bases], refs[added + bases :]
    arrays, (out, held, sems) = refs[:-3], refs[-3:]
    count, columns = out.shape
    rank = scores[0].shape[0]
    copies = []
    for n, (at, row, _) in enumerate(pieces):
        source = arrays[at].at[pl.ds(row, rank), pl.ds(arrays[at].shape[1] - columns, columns)]
        copies.append(pltpu.make_async_copy(source, held.at[pl.ds(n * rank, rank)], sems.at[n]))
        copies[-1].start()
    shrink = scores[0][:, pl.ds(0, count)]
    for x in scores[1:]:
        shrink = shrink + x[:, pl.ds(0, count)]
    shrink = adapter_scale * shrink
    high = shrink.astype(jnp.bfloat16).astype(jnp.float32)
    masks = [row_steps[pl.ds(0, 1), :] == by_part(group) for _, _, group in pieces]
    total = base[0][...]
    for x in base[1:]:
        total = total + x[...]
    for copy in copies:
        copy.wait()
    for term in (high, shrink - high):
        wide = jnp.concatenate([jnp.where(mask, term, 0.0) for mask in masks], axis=0)
        total = total + lax.dot_general(
            wide.astype(jnp.bfloat16),
            held[...],
            (((0,), (0,)), ((), ())),
            preferred_element_type=jnp.float32,
        )
    out[...] = total.astype(out.dtype)


def end(pieces, row_steps, scores, base, arrays, kind, cost):
    count, columns = base[0].shape
    rank = scores[0].shape[0]
    vmem = pl.BlockSpec(memory_space=pltpu.VMEM)
    return pl.pallas_call(
        functools.partial(end_kernel, pieces, len(scores), len(base)),
        out_shape=jax.ShapeDtypeStruct((count, columns), kind),
        in_specs=[vmem] * (1 + len(scores) + len(base))
        + [pl.BlockSpec(memory_space=pl.ANY)] * len(arrays),
        out_specs=vmem,
        scratch_shapes=[
            pltpu.VMEM((len(pieces) * rank, columns), jnp.bfloat16),
            pltpu.SemaphoreType.DMA((len(pieces),)),
        ],
        compiler_params=pltpu.CompilerParams(vmem_limit_bytes=24 << 20),
        cost_estimate=pl.CostEstimate(flops=0, bytes_accessed=cost, transcendentals=0),
    )(row_steps, *scores, *base, *arrays)


def on_device(tokens, base_weight, shrink_panels, expand_panels, adapter_home, fetch_list, seg_len):
    replicas, parts, cores = lax.axis_size("rep"), lax.axis_size("parts"), lax.axis_size("tp")
    tok_count = tokens.shape[0]
    columns = expand_panels.shape[2] // cores
    panels = jnp.swapaxes(shrink_panels, 1, 2)
    rank = panels.shape[1]
    tie = lax.optimization_barrier

    alone, half = max(2, parts), replicas // 2

    def grouped(steps):
        size = len(steps) // parts
        return [tuple(steps[p * size + g] for p in range(parts)) for g in range(size)]

    far = grouped(list(range(half, replicas)))
    near = grouped(list(range(alone, half)))
    groups = far + near
    solo = [(step,) * parts for step in range(1, alone)]

    def hop(x, group):
        pairs = [
            (p * replicas + i, p * replicas + (i ^ group[p]))
            for p in range(parts)
            for i in range(replicas)
        ]
        return lax.ppermute(x, ("parts", "rep"), pairs)

    def shift_parts(x, shift):
        return lax.ppermute(x, "parts", [(i, (i + shift) % parts) for i in range(parts)])

    def shift_cores(x, shift):
        return lax.ppermute(x, "tp", [(i, (i + shift) % cores) for i in range(cores)])

    tables = (adapter_home, fetch_list, panels, expand_panels)
    groups = far + near + solo
    send = pack(groups, columns, *tables)
    tokens, send = tie((tokens, send))
    recv = [hop(x, group) for x, group in zip(send, groups)]
    tokens_of = [tokens] + [shift_parts(tokens, shift) for shift in range(1, parts)]
    solo_recv = recv[len(far) + len(near) :]
    near_recv = recv[len(far) : len(far) + len(near)]
    seg_len, base_weight, solo_recv = tie((seg_len, base_weight, solo_recv))
    base = base_terms(tokens, base_weight, cores)
    base, recv[: len(far) - 1] = tie((base, recv[: len(far) - 1]))
    base = base[:1] + [shift_cores(x, shift + 1) for shift, x in enumerate(base[1:])]
    row_steps = steps_of_rows(tok_count, panels.shape[0], adapter_home, fetch_list, seg_len)
    steps_of = [row_steps] + [shift_parts(row_steps, shift) for shift in range(1, parts)]
    early, early_groups = near_recv + recv[: len(far) - 1], near + far[:-1]
    last, last_group, own_group = recv[len(far) - 1], far[-1], (0,) * parts

    count = len(early)
    first, sent, own_expand = score(
        [tuple(range(count + len(solo) + 1))],
        early_groups + solo + [own_group],
        tuple(range(count)),
        columns,
        steps_of[:1],
        [tokens],
        early + solo_recv + [panels],
        tables=tables,
    )
    passed = [shift_parts(sent, shift) for shift in range(1, parts)]
    base, first, passed, tokens_of[1:], last = tie((base, first, passed, tokens_of[1:], last))
    scores, sent = score(
        [(0,)] + [tuple(range(count + 1))] * (parts - 1),
        [last_group] + early_groups,
        (0,),
        columns,
        steps_of,
        tokens_of,
        [last] + early,
        first,
    )
    last_passed = [shift_parts(sent, shift) for shift in range(1, parts)]
    halves = [scores] + [shift_cores(scores, shift) for shift in range(1, cores)]
    whole = halves[0]
    for x in halves[1:]:
        whole = whole + x
    came = [
        shift_parts(whole[:, shift * tok_count : (shift + 1) * tok_count], -shift)
        for shift in range(1, parts)
    ]
    arrays = [own_expand] + early + solo_recv + [last]
    pieces = [(n, 0, group) for n, group in enumerate([own_group] + early_groups + solo + [last_group])]
    result = end(pieces, row_steps, halves, base, arrays, jnp.float32, 1 << 24)
    pieces = []
    for shift in range(1, parts):
        at = shift - 1
        pieces += [(at, n * rank, turned(group, shift)) for n, group in enumerate(early_groups)]
        pieces.append((at + parts - 1, 0, turned(last_group, shift)))
    return end(pieces, row_steps, came, [result], passed + last_passed, jnp.bfloat16, 0)


def solution(mesh):
    return jax.shard_map(
        on_device,
        mesh=mesh,
        in_specs=(
            P(("parts", "rep"), "tp"),
            P("tp", None),
            P("rep", "tp", None),
            P("rep", None, None),
            P(),
            P(),
            P(("parts", "rep"), None),
        ),
        out_specs=P(("parts", "rep"), "tp"),
        check_vma=False,
    )
```

```python
import functools
import jax
import jax.numpy as jnp
from jax import lax
from jax.experimental import pallas as pl
from jax.experimental.pallas import tpu as pltpu
from jax.sharding import PartitionSpec as P

adapter_scale = 2.0


def by_part(values):
    part = lax.axis_index("parts")
    chosen = jnp.int32(values[0])
    for p, value in enumerate(values):
        chosen = jnp.where(part == p, value, chosen)
    return chosen


def turned(group, shift):
    return tuple(group[(p - shift) % len(group)] for p in range(len(group)))


def slot_for(peer, me, per_home, home_ref, fetch_ref):
    first = me * per_home

    def look(j, slot):
        local = home_ref[fetch_ref[peer, j]] - first
        return jnp.where((local >= 0) & (local < per_home), local, slot)

    listed = fetch_ref.shape[1]
    return lax.fori_loop(0, listed, look, jnp.int32(0), unroll=listed <= 8)


def steps_kernel(per_home, home_ref, fetch_ref, lengths_ref, out):
    me = lax.axis_index("rep")
    rows = lax.broadcasted_iota(jnp.int32, out.shape, 1)
    result = jnp.zeros(out.shape, jnp.int32)
    start = jnp.int32(0)
    for j in range(fetch_ref.shape[1]):
        step = lax.div(home_ref[fetch_ref[me, j]], jnp.int32(per_home)) ^ me
        result = jnp.where(rows >= start, step, result)
        start = start + lengths_ref[0, j]
    out[...] = result


def steps_of_rows(count, per_home, adapter_home, fetch_list, seg_len):
    return pl.pallas_call(
        functools.partial(steps_kernel, per_home),
        out_shape=jax.ShapeDtypeStruct((8, count), jnp.int32),
        in_specs=[pl.BlockSpec(memory_space=pltpu.SMEM)] * 3,
        out_specs=pl.BlockSpec(memory_space=pltpu.VMEM),
        compiler_params=pltpu.CompilerParams(vmem_limit_bytes=2 << 20),
        cost_estimate=pl.CostEstimate(flops=0, bytes_accessed=0, transcendentals=0),
    )(adapter_home, fetch_list, seg_len)


def pack_kernel(groups, home_ref, fetch_ref, shrink_ref, expand_ref, *refs):
    outs, (held, in_sems, out_sems) = refs[:-3], refs[-3:]
    me = lax.axis_index("rep")
    per_home, _, depth = shrink_ref.shape
    columns = expand_ref.shape[2] // lax.axis_size("tp")
    left = pl.multiple_of(lax.axis_index("tp") * columns, 128)
    cuts = in_sems.shape[1] - 1
    width = depth // cuts
    arriving = []
    for at, group in enumerate(groups):
        slot = slot_for(me ^ by_part(group), me, per_home, home_ref, fetch_ref)
        pieces = [(shrink_ref.at[slot, :, pl.ds(n * width, width)], n * width, width) for n in range(cuts)]
        pieces.append((expand_ref.at[slot, :, pl.ds(left, columns)], depth, columns))
        for n, (source, start, size) in enumerate(pieces):
            target = held.at[at, :, pl.ds(start, size)]
            copy = pltpu.make_async_copy(source, target, in_sems.at[at, n])
            copy.start()
            leave = pltpu.make_async_copy(target, outs[at].at[:, pl.ds(start, size)], out_sems.at[at, n])
            arriving.append((copy, leave))
    for copy, leave in arriving:
        copy.wait()
        leave.start()
    for _, leave in arriving:
        leave.wait()


def pack(groups, columns, adapter_home, fetch_list, panels, expand_panels):
    rank, depth = panels.shape[1:]
    shape = (rank, depth + columns)
    cuts = 2
    return list(
        pl.pallas_call(
            functools.partial(pack_kernel, groups),
            out_shape=[jax.ShapeDtypeStruct(shape, panels.dtype)] * len(groups),
            in_specs=[pl.BlockSpec(memory_space=pltpu.SMEM)] * 2 + [pl.BlockSpec(memory_space=pl.ANY)] * 2,
            out_specs=[pl.BlockSpec(memory_space=pl.ANY)] * len(groups),
            scratch_shapes=[pltpu.VMEM((len(groups),) + shape, panels.dtype)]
            + [pltpu.SemaphoreType.DMA((len(groups), cuts + 1))] * 2,
            compiler_params=pltpu.CompilerParams(vmem_limit_bytes=56 << 20),
            cost_estimate=pl.CostEstimate(flops=0, bytes_accessed=0, transcendentals=0),
        )(adapter_home, fetch_list, panels, expand_panels)
    )


def score_kernel(plan, groups, kept, own, chunks, has_prior, *refs):
    sets, many = len(plan), len(groups)
    tables, refs = (refs[:2], refs[2:]) if own else (None, refs)
    row_steps, refs = refs[:sets], refs[sets:]
    prior, refs = (refs[0], refs[1:]) if has_prior else (None, refs)
    tokens, panels, refs = refs[:sets], refs[sets : sets + many], refs[sets + many :]
    expand_ref, refs = (refs[0], refs[1:]) if own else (None, refs)
    out, out_expand, refs = refs[0], refs[1], refs[2:]
    rank, (count, depth) = out.shape[0], tokens[0].shape
    columns = out_expand.shape[1]
    copies = []
    if own:
        out_own, held, sems = refs
        me = lax.axis_index("rep")
        slot = slot_for(me, me, panels[-1].shape[0], *tables)
        left = pl.multiple_of(lax.axis_index("tp") * columns, 128)
        for n, (source, target) in enumerate(
            ((panels[-1].at[slot], held), (expand_ref.at[slot, :, pl.ds(left, columns)], out_own))
        ):
            copies.append(pltpu.make_async_copy(source, target, sems.at[n]))
            copies[-1].start()
        panels = panels[:-1] + (held,)
    for i, n in enumerate(kept):
        out_expand[pl.ds(i * rank, rank), :] = panels[n][:, pl.ds(depth, columns)]
    for copy in copies:
        copy.wait()
    width = depth // chunks
    sums = [None] * sets
    for c in range(chunks):
        cols = pl.ds(c * width, width)
        for t, used in enumerate(plan):
            product = lax.dot_general(
                jnp.concatenate([panels[n][:, cols] for n in used], axis=0),
                tokens[t][:, cols],
                (((1,), (1,)), ((), ())),
                preferred_element_type=jnp.float32,
            )
            sums[t] = product if c == 0 else sums[t] + product
    for t, used in enumerate(plan):
        mine = row_steps[t][pl.ds(0, 1), :]
        total = prior[...] if has_prior and t == 0 else jnp.zeros((rank, count), jnp.float32)
        for n, panel in enumerate(used):
            term = sums[t][n * rank : (n + 1) * rank]
            total = total + jnp.where(mine == by_part(groups[panel]), term, 0.0)
        out[:, pl.ds(t * count, count)] = total


def score(plan, groups, kept, columns, row_steps, tokens_of, panels, prior=None, tables=None):
    count, depth = tokens_of[0].shape
    rank = panels[0].shape[0]
    chunks = 4
    own = tables is not None
    prior = [] if prior is None else [prior]
    smem, vmem = pl.BlockSpec(memory_space=pltpu.SMEM), pl.BlockSpec(memory_space=pltpu.VMEM)
    anywhere = pl.BlockSpec(memory_space=pl.ANY)
    outs = [(rank, len(plan) * count), (len(kept) * rank, columns)] + [(rank, columns)] * own
    arrays = list(row_steps) + prior + list(tokens_of) + list(panels)
    need = 4 * len(plan) * count * (rank * len(panels) + depth) + 4 * len(panels) * rank * (depth + columns)
    return pl.pallas_call(
        functools.partial(score_kernel, plan, groups, kept, own, chunks, bool(prior)),
        out_shape=[
            jax.ShapeDtypeStruct(shape, panels[0].dtype if n else jnp.float32)
            for n, shape in enumerate(outs)
        ],
        in_specs=[smem] * (2 * own)
        + [vmem] * (len(arrays) - own)
        + [anywhere] * (2 * own),
        out_specs=[vmem] * len(outs),
        scratch_shapes=[pltpu.VMEM((rank, depth), tokens_of[0].dtype), pltpu.SemaphoreType.DMA((2,))] * own,
        compiler_params=pltpu.CompilerParams(vmem_limit_bytes=need + (2 << 20)),
        cost_estimate=pl.CostEstimate(flops=0, bytes_accessed=0, transcendentals=0),
    )(*(tables[:2] if own else ()), *arrays, *([tables[3]] if own else ()))


def base_kernel(chunks, tokens_ref, weight_ref, *refs):
    outs, (held_tokens, held_weight, sems) = refs[:-3], refs[-3:]
    cores, half = len(outs), lax.axis_index("tp")
    columns = outs[0].shape[1]
    height = tokens_ref.shape[1] // chunks
    copies = []
    for c in range(chunks):
        rows = pl.ds(c * height, height)
        pairs = [(tokens_ref.at[:, rows], held_tokens.at[:, rows])]
        for shift in range(cores):
            left = pl.multiple_of(lax.rem(half + shift, cores) * columns, 128)
            pairs.append((weight_ref.at[rows, pl.ds(left, columns)], held_weight.at[shift, rows, :]))
        copies.append([])
        for n, (source, target) in enumerate(pairs):
            copies[-1].append(pltpu.make_async_copy(source, target, sems.at[c, n]))
            copies[-1][-1].start()
    for c in range(chunks):
        for copy in copies[c]:
            copy.wait()
        rows = pl.ds(c * height, height)
        for shift, out in enumerate(outs):
            product = jnp.dot(
                held_tokens[:, rows], held_weight[shift, rows, :], preferred_element_type=jnp.float32
            )
            if c == 0:
                out[...] = product
            else:
                out[...] += product


def base_terms(tokens, weight, cores):
    count, depth = tokens.shape
    columns = weight.shape[1] // cores
    chunks = 4
    return list(
        pl.pallas_call(
            functools.partial(base_kernel, chunks),
            out_shape=[jax.ShapeDtypeStruct((count, columns), jnp.float32)] * cores,
            in_specs=[pl.BlockSpec(memory_space=pl.ANY)] * 2,
            out_specs=[pl.BlockSpec(memory_space=pltpu.VMEM)] * cores,
            scratch_shapes=[
                pltpu.VMEM((count, depth), tokens.dtype),
                pltpu.VMEM((cores, depth, columns), weight.dtype),
                pltpu.SemaphoreType.DMA((chunks, 1 + cores)),
            ],
            compiler_params=pltpu.CompilerParams(vmem_limit_bytes=20 << 20),
            cost_estimate=pl.CostEstimate(flops=0, bytes_accessed=0, transcendentals=0),
        )(tokens, weight)
    )


def end_kernel(pieces, added, bases, row_steps, *refs):
    scores, base, refs = refs[:added], refs[added : added + bases], refs[added + bases :]
    arrays, (out, held, sems) = refs[:-3], refs[-3:]
    count, columns = out.shape
    rank = scores[0].shape[0]
    copies = []
    for n, (at, row, _) in enumerate(pieces):
        source = arrays[at].at[pl.ds(row, rank), pl.ds(arrays[at].shape[1] - columns, columns)]
        copies.append(pltpu.make_async_copy(source, held.at[pl.ds(n * rank, rank)], sems.at[n]))
        copies[-1].start()
    shrink = scores[0][:, pl.ds(0, count)]
    for x in scores[1:]:
        shrink = shrink + x[:, pl.ds(0, count)]
    shrink = adapter_scale * shrink
    high = shrink.astype(jnp.bfloat16).astype(jnp.float32)
    masks = [row_steps[pl.ds(0, 1), :] == by_part(group) for _, _, group in pieces]
    total = base[0][...]
    for x in base[1:]:
        total = total + x[...]
    for copy in copies:
        copy.wait()
    for term in (high, shrink - high):
        wide = jnp.concatenate([jnp.where(mask, term, 0.0) for mask in masks], axis=0)
        total = total + lax.dot_general(
            wide.astype(jnp.bfloat16),
            held[...],
            (((0,), (0,)), ((), ())),
            preferred_element_type=jnp.float32,
        )
    out[...] = total.astype(out.dtype)


def end(pieces, row_steps, scores, base, arrays, kind, cost):
    count, columns = base[0].shape
    rank = scores[0].shape[0]
    vmem = pl.BlockSpec(memory_space=pltpu.VMEM)
    return pl.pallas_call(
        functools.partial(end_kernel, pieces, len(scores), len(base)),
        out_shape=jax.ShapeDtypeStruct((count, columns), kind),
        in_specs=[vmem] * (1 + len(scores) + len(base))
        + [pl.BlockSpec(memory_space=pl.ANY)] * len(arrays),
        out_specs=vmem,
        scratch_shapes=[
            pltpu.VMEM((len(pieces) * rank, columns), jnp.bfloat16),
            pltpu.SemaphoreType.DMA((len(pieces),)),
        ],
        compiler_params=pltpu.CompilerParams(vmem_limit_bytes=16 << 20),
        cost_estimate=pl.CostEstimate(flops=0, bytes_accessed=cost, transcendentals=0),
    )(row_steps, *scores, *base, *arrays)


def on_device(tokens, base_weight, shrink_panels, expand_panels, adapter_home, fetch_list, seg_len):
    replicas, parts, cores = lax.axis_size("rep"), lax.axis_size("parts"), lax.axis_size("tp")
    tok_count = tokens.shape[0]
    columns = expand_panels.shape[2] // cores
    panels = jnp.swapaxes(shrink_panels, 1, 2)
    rank = panels.shape[1]
    tie = lax.optimization_barrier

    alone, half = max(2, parts), replicas // 2

    def grouped(steps):
        size = len(steps) // parts
        return [tuple(steps[p * size + g] for p in range(parts)) for g in range(size)]

    far = grouped(list(range(half, replicas)))
    near = grouped(list(range(alone, half)))
    groups = far + near
    solo = [(step,) * parts for step in range(1, alone)]

    def hop(x, group):
        pairs = [
            (p * replicas + i, p * replicas + (i ^ group[p]))
            for p in range(parts)
            for i in range(replicas)
        ]
        return lax.ppermute(x, ("parts", "rep"), pairs)

    def shift_parts(x, shift):
        return lax.ppermute(x, "parts", [(i, (i + shift) % parts) for i in range(parts)])

    def shift_cores(x, shift):
        return lax.ppermute(x, "tp", [(i, (i + shift) % cores) for i in range(cores)])

    tables = (adapter_home, fetch_list, panels, expand_panels)
    groups = far + near + solo
    send = pack(groups, columns, *tables)
    tokens, send = tie((tokens, send))
    recv = [hop(x, group) for x, group in zip(send, groups)]
    tokens_of = [tokens] + [shift_parts(tokens, shift) for shift in range(1, parts)]
    solo_recv = recv[len(far) + len(near) :]
    near_recv = recv[len(far) : len(far) + len(near)]
    seg_len, base_weight, solo_recv = tie((seg_len, base_weight, solo_recv))
    base = base_terms(tokens, base_weight, cores)
    base, recv[: len(far) - 1] = tie((base, recv[: len(far) - 1]))
    base = base[:1] + [shift_cores(x, shift + 1) for shift, x in enumerate(base[1:])]
    row_steps = steps_of_rows(tok_count, panels.shape[0], adapter_home, fetch_list, seg_len)
    steps_of = [row_steps] + [shift_parts(row_steps, shift) for shift in range(1, parts)]
    early, early_groups = near_recv + recv[: len(far) - 1], near + far[:-1]
    last, last_group, own_group = recv[len(far) - 1], far[-1], (0,) * parts

    count = len(early)
    first, sent, own_expand = score(
        [tuple(range(count + len(solo) + 1))],
        early_groups + solo + [own_group],
        tuple(range(count)),
        columns,
        steps_of[:1],
        [tokens],
        early + solo_recv + [panels],
        tables=tables,
    )
    passed = [shift_parts(sent, shift) for shift in range(1, parts)]
    base, first, passed, tokens_of[1:], last = tie((base, first, passed, tokens_of[1:], last))
    scores, sent = score(
        [(0,)] + [tuple(range(count + 1))] * (parts - 1),
        [last_group] + early_groups,
        (0,),
        columns,
        steps_of,
        tokens_of,
        [last] + early,
        first,
    )
    last_passed = [shift_parts(sent, shift) for shift in range(1, parts)]
    halves = [scores] + [shift_cores(scores, shift) for shift in range(1, cores)]
    whole = halves[0]
    for x in halves[1:]:
        whole = whole + x
    came = [
        shift_parts(whole[:, shift * tok_count : (shift + 1) * tok_count], -shift)
        for shift in range(1, parts)
    ]
    arrays = [own_expand] + early + solo_recv + [last]
    pieces = [(n, 0, group) for n, group in enumerate([own_group] + early_groups + solo + [last_group])]
    result = end(pieces, row_steps, halves, base, arrays, jnp.float32, 1 << 24)
    pieces = []
    for shift in range(1, parts):
        at = shift - 1
        pieces += [(at, n * rank, turned(group, shift)) for n, group in enumerate(early_groups)]
        pieces.append((at + parts - 1, 0, turned(last_group, shift)))
    return end(pieces, row_steps, came, [result], passed + last_passed, jnp.bfloat16, 0)


def solution(mesh):
    return jax.shard_map(
        on_device,
        mesh=mesh,
        in_specs=(
            P(("parts", "rep"), "tp"),
            P("tp", None),
            P("rep", "tp", None),
            P("rep", None, None),
            P(),
            P(),
            P(("parts", "rep"), None),
        ),
        out_specs=P(("parts", "rep"), "tp"),
        check_vma=False,
    )
```

```python
import functools
import jax
import jax.numpy as jnp
from jax import lax
from jax.experimental import pallas as pl
from jax.experimental.pallas import tpu as pltpu
from jax.sharding import PartitionSpec as P

adapter_scale = 2.0


def by_part(values):
    part = lax.axis_index("parts")
    chosen = jnp.int32(values[0])
    for p, value in enumerate(values):
        chosen = jnp.where(part == p, value, chosen)
    return chosen


def turned(group, shift):
    return tuple(group[(p - shift) % len(group)] for p in range(len(group)))


def slot_for(peer, me, per_home, home_ref, fetch_ref):
    first = me * per_home

    def look(j, slot):
        local = home_ref[fetch_ref[peer, j]] - first
        return jnp.where((local >= 0) & (local < per_home), local, slot)

    listed = fetch_ref.shape[1]
    return lax.fori_loop(0, listed, look, jnp.int32(0), unroll=listed <= 8)


def steps_kernel(per_home, home_ref, fetch_ref, lengths_ref, out):
    me = lax.axis_index("rep")
    rows = lax.broadcasted_iota(jnp.int32, out.shape, 1)
    result = jnp.zeros(out.shape, jnp.int32)
    start = jnp.int32(0)
    for j in range(fetch_ref.shape[1]):
        step = lax.div(home_ref[fetch_ref[me, j]], jnp.int32(per_home)) ^ me
        result = jnp.where(rows >= start, step, result)
        start = start + lengths_ref[0, j]
    out[...] = result


def steps_of_rows(count, per_home, adapter_home, fetch_list, seg_len):
    return pl.pallas_call(
        functools.partial(steps_kernel, per_home),
        out_shape=jax.ShapeDtypeStruct((8, count), jnp.int32),
        in_specs=[pl.BlockSpec(memory_space=pltpu.SMEM)] * 3,
        out_specs=pl.BlockSpec(memory_space=pltpu.VMEM),
        compiler_params=pltpu.CompilerParams(vmem_limit_bytes=2 << 20),
        cost_estimate=pl.CostEstimate(flops=0, bytes_accessed=0, transcendentals=0),
    )(adapter_home, fetch_list, seg_len)


def pack_kernel(groups, home_ref, fetch_ref, shrink_ref, expand_ref, *refs):
    outs, (held, in_sems, out_sems) = refs[:-3], refs[-3:]
    me = lax.axis_index("rep")
    per_home, _, depth = shrink_ref.shape
    columns = expand_ref.shape[2] // lax.axis_size("tp")
    left = pl.multiple_of(lax.axis_index("tp") * columns, 128)
    cuts = in_sems.shape[1] - 1
    width = depth // cuts
    arriving = []
    for at, group in enumerate(groups):
        slot = slot_for(me ^ by_part(group), me, per_home, home_ref, fetch_ref)
        pieces = [(shrink_ref.at[slot, :, pl.ds(n * width, width)], n * width, width) for n in range(cuts)]
        pieces.append((expand_ref.at[slot, :, pl.ds(left, columns)], depth, columns))
        for n, (source, start, size) in enumerate(pieces):
            target = held.at[at, :, pl.ds(start, size)]
            copy = pltpu.make_async_copy(source, target, in_sems.at[at, n])
            copy.start()
            leave = pltpu.make_async_copy(target, outs[at].at[:, pl.ds(start, size)], out_sems.at[at, n])
            arriving.append((copy, leave))
    for copy, leave in arriving:
        copy.wait()
        leave.start()
    for _, leave in arriving:
        leave.wait()


def pack(groups, columns, adapter_home, fetch_list, panels, expand_panels):
    rank, depth = panels.shape[1:]
    shape = (rank, depth + columns)
    cuts = 4
    return list(
        pl.pallas_call(
            functools.partial(pack_kernel, groups),
            out_shape=[jax.ShapeDtypeStruct(shape, panels.dtype)] * len(groups),
            in_specs=[pl.BlockSpec(memory_space=pltpu.SMEM)] * 2 + [pl.BlockSpec(memory_space=pl.ANY)] * 2,
            out_specs=[pl.BlockSpec(memory_space=pl.ANY)] * len(groups),
            scratch_shapes=[pltpu.VMEM((len(groups),) + shape, panels.dtype)]
            + [pltpu.SemaphoreType.DMA((len(groups), cuts + 1))] * 2,
            compiler_params=pltpu.CompilerParams(vmem_limit_bytes=56 << 20),
            cost_estimate=pl.CostEstimate(flops=0, bytes_accessed=0, transcendentals=0),
        )(adapter_home, fetch_list, panels, expand_panels)
    )


def score_kernel(plan, groups, kept, own, chunks, has_prior, *refs):
    sets, many = len(plan), len(groups)
    tables, refs = (refs[:2], refs[2:]) if own else (None, refs)
    row_steps, refs = refs[:sets], refs[sets:]
    prior, refs = (refs[0], refs[1:]) if has_prior else (None, refs)
    tokens, panels, refs = refs[:sets], refs[sets : sets + many], refs[sets + many :]
    expand_ref, refs = (refs[0], refs[1:]) if own else (None, refs)
    out, out_expand, refs = refs[0], refs[1], refs[2:]
    rank, (count, depth) = out.shape[0], tokens[0].shape
    columns = out_expand.shape[1]
    copies = []
    if own:
        out_own, held, sems = refs
        me = lax.axis_index("rep")
        slot = slot_for(me, me, panels[-1].shape[0], *tables)
        left = pl.multiple_of(lax.axis_index("tp") * columns, 128)
        for n, (source, target) in enumerate(
            ((panels[-1].at[slot], held), (expand_ref.at[slot, :, pl.ds(left, columns)], out_own))
        ):
            copies.append(pltpu.make_async_copy(source, target, sems.at[n]))
            copies[-1].start()
        panels = panels[:-1] + (held,)
    for i, n in enumerate(kept):
        out_expand[pl.ds(i * rank, rank), :] = panels[n][:, pl.ds(depth, columns)]
    for copy in copies:
        copy.wait()
    width = depth // chunks
    sums = [None] * sets
    for c in range(chunks):
        cols = pl.ds(c * width, width)
        for t, used in enumerate(plan):
            product = lax.dot_general(
                jnp.concatenate([panels[n][:, cols] for n in used], axis=0),
                tokens[t][:, cols],
                (((1,), (1,)), ((), ())),
                preferred_element_type=jnp.float32,
            )
            sums[t] = product if c == 0 else sums[t] + product
    for t, used in enumerate(plan):
        mine = row_steps[t][pl.ds(0, 1), :]
        total = prior[...] if has_prior and t == 0 else jnp.zeros((rank, count), jnp.float32)
        for n, panel in enumerate(used):
            term = sums[t][n * rank : (n + 1) * rank]
            total = total + jnp.where(mine == by_part(groups[panel]), term, 0.0)
        out[:, pl.ds(t * count, count)] = total


def score(plan, groups, kept, columns, row_steps, tokens_of, panels, prior=None, tables=None):
    count, depth = tokens_of[0].shape
    rank = panels[0].shape[0]
    chunks = 4
    own = tables is not None
    prior = [] if prior is None else [prior]
    smem, vmem = pl.BlockSpec(memory_space=pltpu.SMEM), pl.BlockSpec(memory_space=pltpu.VMEM)
    anywhere = pl.BlockSpec(memory_space=pl.ANY)
    outs = [(rank, len(plan) * count), (len(kept) * rank, columns)] + [(rank, columns)] * own
    arrays = list(row_steps) + prior + list(tokens_of) + list(panels)
    need = 4 * len(plan) * count * (rank * len(panels) + depth) + 4 * len(panels) * rank * (depth + columns)
    return pl.pallas_call(
        functools.partial(score_kernel, plan, groups, kept, own, chunks, bool(prior)),
        out_shape=[
            jax.ShapeDtypeStruct(shape, panels[0].dtype if n else jnp.float32)
            for n, shape in enumerate(outs)
        ],
        in_specs=[smem] * (2 * own)
        + [vmem] * (len(arrays) - own)
        + [anywhere] * (2 * own),
        out_specs=[vmem] * len(outs),
        scratch_shapes=[pltpu.VMEM((rank, depth), tokens_of[0].dtype), pltpu.SemaphoreType.DMA((2,))] * own,
        compiler_params=pltpu.CompilerParams(vmem_limit_bytes=need + (2 << 20)),
        cost_estimate=pl.CostEstimate(flops=0, bytes_accessed=0, transcendentals=0),
    )(*(tables[:2] if own else ()), *arrays, *([tables[3]] if own else ()))


def base_kernel(chunks, tokens_ref, weight_ref, *refs):
    outs, (held_tokens, held_weight, sems) = refs[:-3], refs[-3:]
    cores, half = len(outs), lax.axis_index("tp")
    columns = outs[0].shape[1]
    height = tokens_ref.shape[1] // chunks
    copies = []
    for c in range(chunks):
        rows = pl.ds(c * height, height)
        pairs = [(tokens_ref.at[:, rows], held_tokens.at[:, rows])]
        for shift in range(cores):
            left = pl.multiple_of(lax.rem(half + shift, cores) * columns, 128)
            pairs.append((weight_ref.at[rows, pl.ds(left, columns)], held_weight.at[shift, rows, :]))
        copies.append([])
        for n, (source, target) in enumerate(pairs):
            copies[-1].append(pltpu.make_async_copy(source, target, sems.at[c, n]))
            copies[-1][-1].start()
    for c in range(chunks):
        for copy in copies[c]:
            copy.wait()
        rows = pl.ds(c * height, height)
        for shift, out in enumerate(outs):
            product = jnp.dot(
                held_tokens[:, rows], held_weight[shift, rows, :], preferred_element_type=jnp.float32
            )
            if c == 0:
                out[...] = product
            else:
                out[...] += product


def base_terms(tokens, weight, cores):
    count, depth = tokens.shape
    columns = weight.shape[1] // cores
    chunks = 4
    return list(
        pl.pallas_call(
            functools.partial(base_kernel, chunks),
            out_shape=[jax.ShapeDtypeStruct((count, columns), jnp.float32)] * cores,
            in_specs=[pl.BlockSpec(memory_space=pl.ANY)] * 2,
            out_specs=[pl.BlockSpec(memory_space=pltpu.VMEM)] * cores,
            scratch_shapes=[
                pltpu.VMEM((count, depth), tokens.dtype),
                pltpu.VMEM((cores, depth, columns), weight.dtype),
                pltpu.SemaphoreType.DMA((chunks, 1 + cores)),
            ],
            compiler_params=pltpu.CompilerParams(vmem_limit_bytes=20 << 20),
            cost_estimate=pl.CostEstimate(flops=0, bytes_accessed=0, transcendentals=0),
        )(tokens, weight)
    )


def end_kernel(pieces, added, bases, row_steps, *refs):
    scores, base, refs = refs[:added], refs[added : added + bases], refs[added + bases :]
    arrays, (out, held, sems) = refs[:-3], refs[-3:]
    count, columns = out.shape
    rank = scores[0].shape[0]
    copies = []
    for n, (at, row, _) in enumerate(pieces):
        source = arrays[at].at[pl.ds(row, rank), pl.ds(arrays[at].shape[1] - columns, columns)]
        copies.append(pltpu.make_async_copy(source, held.at[pl.ds(n * rank, rank)], sems.at[n]))
        copies[-1].start()
    shrink = scores[0][:, pl.ds(0, count)]
    for x in scores[1:]:
        shrink = shrink + x[:, pl.ds(0, count)]
    shrink = adapter_scale * shrink
    high = shrink.astype(jnp.bfloat16).astype(jnp.float32)
    masks = [row_steps[pl.ds(0, 1), :] == by_part(group) for _, _, group in pieces]
    total = base[0][...]
    for x in base[1:]:
        total = total + x[...]
    for copy in copies:
        copy.wait()
    for term in (high, shrink - high):
        wide = jnp.concatenate([jnp.where(mask, term, 0.0) for mask in masks], axis=0)
        total = total + lax.dot_general(
            wide.astype(jnp.bfloat16),
            held[...],
            (((0,), (0,)), ((), ())),
            preferred_element_type=jnp.float32,
        )
    out[...] = total.astype(out.dtype)


def end(pieces, row_steps, scores, base, arrays, kind, cost):
    count, columns = base[0].shape
    rank = scores[0].shape[0]
    vmem = pl.BlockSpec(memory_space=pltpu.VMEM)
    return pl.pallas_call(
        functools.partial(end_kernel, pieces, len(scores), len(base)),
        out_shape=jax.ShapeDtypeStruct((count, columns), kind),
        in_specs=[vmem] * (1 + len(scores) + len(base))
        + [pl.BlockSpec(memory_space=pl.ANY)] * len(arrays),
        out_specs=vmem,
        scratch_shapes=[
            pltpu.VMEM((len(pieces) * rank, columns), jnp.bfloat16),
            pltpu.SemaphoreType.DMA((len(pieces),)),
        ],
        compiler_params=pltpu.CompilerParams(vmem_limit_bytes=16 << 20),
        cost_estimate=pl.CostEstimate(flops=0, bytes_accessed=cost, transcendentals=0),
    )(row_steps, *scores, *base, *arrays)


def on_device(tokens, base_weight, shrink_panels, expand_panels, adapter_home, fetch_list, seg_len):
    replicas, parts, cores = lax.axis_size("rep"), lax.axis_size("parts"), lax.axis_size("tp")
    tok_count = tokens.shape[0]
    columns = expand_panels.shape[2] // cores
    panels = jnp.swapaxes(shrink_panels, 1, 2)
    rank = panels.shape[1]
    tie = lax.optimization_barrier

    alone, half = max(2, parts), replicas // 2

    def grouped(steps):
        size = len(steps) // parts
        return [tuple(steps[p * size + g] for p in range(parts)) for g in range(size)]

    far = grouped(list(range(half, replicas)))
    near = grouped(list(range(alone, half)))
    groups = far + near
    solo = [(step,) * parts for step in range(1, alone)]

    def hop(x, group):
        pairs = [
            (p * replicas + i, p * replicas + (i ^ group[p]))
            for p in range(parts)
            for i in range(replicas)
        ]
        return lax.ppermute(x, ("parts", "rep"), pairs)

    def shift_parts(x, shift):
        return lax.ppermute(x, "parts", [(i, (i + shift) % parts) for i in range(parts)])

    def shift_cores(x, shift):
        return lax.ppermute(x, "tp", [(i, (i + shift) % cores) for i in range(cores)])

    tables = (adapter_home, fetch_list, panels, expand_panels)
    groups = far + near + solo
    send = pack(groups, columns, *tables)
    tokens, send = tie((tokens, send))
    recv = [hop(x, group) for x, group in zip(send, groups)]
    tokens_of = [tokens] + [shift_parts(tokens, shift) for shift in range(1, parts)]
    solo_recv = recv[len(far) + len(near) :]
    near_recv = recv[len(far) : len(far) + len(near)]
    base = base_terms(tokens, base_weight, cores)
    base, recv[: len(far) - 1] = tie((base, recv[: len(far) - 1]))
    base = base[:1] + [shift_cores(x, shift + 1) for shift, x in enumerate(base[1:])]
    row_steps = steps_of_rows(tok_count, panels.shape[0], adapter_home, fetch_list, seg_len)
    steps_of = [row_steps] + [shift_parts(row_steps, shift) for shift in range(1, parts)]
    early, early_groups = near_recv + recv[: len(far) - 1], near + far[:-1]
    last, last_group, own_group = recv[len(far) - 1], far[-1], (0,) * parts

    count = len(early)
    first, sent, own_expand = score(
        [tuple(range(count + len(solo) + 1))],
        early_groups + solo + [own_group],
        tuple(range(count)),
        columns,
        steps_of[:1],
        [tokens],
        early + solo_recv + [panels],
        tables=tables,
    )
    passed = [shift_parts(sent, shift) for shift in range(1, parts)]
    base, first, passed, tokens_of[1:], last = tie((base, first, passed, tokens_of[1:], last))
    scores, sent = score(
        [(0,)] + [tuple(range(count + 1))] * (parts - 1),
        [last_group] + early_groups,
        (0,),
        columns,
        steps_of,
        tokens_of,
        [last] + early,
        first,
    )
    last_passed = [shift_parts(sent, shift) for shift in range(1, parts)]
    halves = [scores] + [shift_cores(scores, shift) for shift in range(1, cores)]
    whole = halves[0]
    for x in halves[1:]:
        whole = whole + x
    came = [
        shift_parts(whole[:, shift * tok_count : (shift + 1) * tok_count], -shift)
        for shift in range(1, parts)
    ]
    arrays = [own_expand] + early + solo_recv + [last]
    pieces = [(n, 0, group) for n, group in enumerate([own_group] + early_groups + solo + [last_group])]
    result = end(pieces, row_steps, halves, base, arrays, jnp.float32, 1 << 24)
    pieces = []
    for shift in range(1, parts):
        at = shift - 1
        pieces += [(at, n * rank, turned(group, shift)) for n, group in enumerate(early_groups)]
        pieces.append((at + parts - 1, 0, turned(last_group, shift)))
    return end(pieces, row_steps, came, [result], passed + last_passed, jnp.bfloat16, 0)


def solution(mesh):
    return jax.shard_map(
        on_device,
        mesh=mesh,
        in_specs=(
            P(("parts", "rep"), "tp"),
            P("tp", None),
            P("rep", "tp", None),
            P("rep", None, None),
            P(),
            P(),
            P(("parts", "rep"), None),
        ),
        out_specs=P(("parts", "rep"), "tp"),
        check_vma=False,
    )
```

```python
import functools
import jax
import jax.numpy as jnp
from jax import lax
from jax.experimental import pallas as pl
from jax.experimental.pallas import tpu as pltpu
from jax.sharding import PartitionSpec as P

adapter_scale = 2.0


def by_part(values):
    part = lax.axis_index("parts")
    chosen = jnp.int32(values[0])
    for p, value in enumerate(values):
        chosen = jnp.where(part == p, value, chosen)
    return chosen


def turned(group, shift):
    return tuple(group[(p - shift) % len(group)] for p in range(len(group)))


def slot_for(peer, me, per_home, home_ref, fetch_ref):
    first = me * per_home

    def look(j, slot):
        local = home_ref[fetch_ref[peer, j]] - first
        return jnp.where((local >= 0) & (local < per_home), local, slot)

    listed = fetch_ref.shape[1]
    return lax.fori_loop(0, listed, look, jnp.int32(0), unroll=listed <= 8)


def steps_kernel(per_home, home_ref, fetch_ref, lengths_ref, out):
    me = lax.axis_index("rep")
    rows = lax.broadcasted_iota(jnp.int32, out.shape, 1)
    result = jnp.zeros(out.shape, jnp.int32)
    start = jnp.int32(0)
    for j in range(fetch_ref.shape[1]):
        step = lax.div(home_ref[fetch_ref[me, j]], jnp.int32(per_home)) ^ me
        result = jnp.where(rows >= start, step, result)
        start = start + lengths_ref[0, j]
    out[...] = result


def steps_of_rows(count, per_home, adapter_home, fetch_list, seg_len):
    return pl.pallas_call(
        functools.partial(steps_kernel, per_home),
        out_shape=jax.ShapeDtypeStruct((8, count), jnp.int32),
        in_specs=[pl.BlockSpec(memory_space=pltpu.SMEM)] * 3,
        out_specs=pl.BlockSpec(memory_space=pltpu.VMEM),
        compiler_params=pltpu.CompilerParams(vmem_limit_bytes=2 << 20),
        cost_estimate=pl.CostEstimate(flops=0, bytes_accessed=0, transcendentals=0),
    )(adapter_home, fetch_list, seg_len)


def pack_kernel(groups, home_ref, fetch_ref, shrink_ref, expand_ref, *refs):
    outs, (held, in_sems, out_sems) = refs[:-3], refs[-3:]
    me = lax.axis_index("rep")
    per_home, _, depth = shrink_ref.shape
    columns = expand_ref.shape[2] // lax.axis_size("tp")
    left = pl.multiple_of(lax.axis_index("tp") * columns, 128)
    cuts = in_sems.shape[1] - 1
    width = depth // cuts
    arriving = []
    for at, group in enumerate(groups):
        slot = slot_for(me ^ by_part(group), me, per_home, home_ref, fetch_ref)
        pieces = [(shrink_ref.at[slot, :, pl.ds(n * width, width)], n * width, width) for n in range(cuts)]
        pieces.append((expand_ref.at[slot, :, pl.ds(left, columns)], depth, columns))
        for n, (source, start, size) in enumerate(pieces):
            target = held.at[at, :, pl.ds(start, size)]
            copy = pltpu.make_async_copy(source, target, in_sems.at[at, n])
            copy.start()
            leave = pltpu.make_async_copy(target, outs[at].at[:, pl.ds(start, size)], out_sems.at[at, n])
            arriving.append((copy, leave))
    for copy, leave in arriving:
        copy.wait()
        leave.start()
    for _, leave in arriving:
        leave.wait()


def pack(groups, columns, adapter_home, fetch_list, panels, expand_panels):
    rank, depth = panels.shape[1:]
    shape = (rank, depth + columns)
    cuts = 4
    return list(
        pl.pallas_call(
            functools.partial(pack_kernel, groups),
            out_shape=[jax.ShapeDtypeStruct(shape, panels.dtype)] * len(groups),
            in_specs=[pl.BlockSpec(memory_space=pltpu.SMEM)] * 2 + [pl.BlockSpec(memory_space=pl.ANY)] * 2,
            out_specs=[pl.BlockSpec(memory_space=pl.ANY)] * len(groups),
            scratch_shapes=[pltpu.VMEM((len(groups),) + shape, panels.dtype)]
            + [pltpu.SemaphoreType.DMA((len(groups), cuts + 1))] * 2,
            compiler_params=pltpu.CompilerParams(vmem_limit_bytes=56 << 20),
            cost_estimate=pl.CostEstimate(flops=0, bytes_accessed=0, transcendentals=0),
        )(adapter_home, fetch_list, panels, expand_panels)
    )


def score_kernel(plan, groups, kept, chunks, has_prior, *refs):
    sets, many = len(plan), len(groups)
    row_steps, refs = refs[:sets], refs[sets:]
    prior, refs = (refs[0], refs[1:]) if has_prior else (None, refs)
    tokens, panels = refs[:sets], refs[sets : sets + many]
    out, out_expand = refs[sets + many :]
    rank, (count, depth) = out.shape[0], tokens[0].shape
    for i, n in enumerate(kept):
        out_expand[pl.ds(i * rank, rank), :] = panels[n][:, pl.ds(depth, out_expand.shape[1])]
    width = depth // chunks
    sums = [None] * sets
    for c in range(chunks):
        cols = pl.ds(c * width, width)
        for t, used in enumerate(plan):
            product = lax.dot_general(
                jnp.concatenate([panels[n][:, cols] for n in used], axis=0),
                tokens[t][:, cols],
                (((1,), (1,)), ((), ())),
                preferred_element_type=jnp.float32,
            )
            sums[t] = product if c == 0 else sums[t] + product
    for t, used in enumerate(plan):
        mine = row_steps[t][pl.ds(0, 1), :]
        total = prior[...] if has_prior and t == 0 else jnp.zeros((rank, count), jnp.float32)
        for n, panel in enumerate(used):
            term = sums[t][n * rank : (n + 1) * rank]
            total = total + jnp.where(mine == by_part(groups[panel]), term, 0.0)
        out[:, pl.ds(t * count, count)] = total


def score(plan, groups, kept, columns, row_steps, tokens_of, panels, prior=None):
    count, depth = tokens_of[0].shape
    rank = panels[0].shape[0]
    chunks = 4
    prior = [] if prior is None else [prior]
    vmem = pl.BlockSpec(memory_space=pltpu.VMEM)
    outs = [(rank, len(plan) * count), (len(kept) * rank, columns)]
    arrays = list(row_steps) + prior + list(tokens_of) + list(panels)
    need = 4 * len(plan) * count * (rank * len(panels) + depth) + 4 * len(panels) * rank * (depth + columns)
    return pl.pallas_call(
        functools.partial(score_kernel, plan, groups, kept, chunks, bool(prior)),
        out_shape=[
            jax.ShapeDtypeStruct(shape, panels[0].dtype if n else jnp.float32)
            for n, shape in enumerate(outs)
        ],
        in_specs=[vmem] * len(arrays),
        out_specs=[vmem] * len(outs),
        compiler_params=pltpu.CompilerParams(vmem_limit_bytes=need + (2 << 20)),
        cost_estimate=pl.CostEstimate(flops=0, bytes_accessed=0, transcendentals=0),
    )(*arrays)


def base_kernel(chunks, tokens_ref, weight_ref, *refs):
    outs, (held_tokens, held_weight, sems) = refs[:-3], refs[-3:]
    cores, half = len(outs), lax.axis_index("tp")
    columns = outs[0].shape[1]
    height = tokens_ref.shape[1] // chunks
    copies = []
    for c in range(chunks):
        rows = pl.ds(c * height, height)
        pairs = [(tokens_ref.at[:, rows], held_tokens.at[:, rows])]
        for shift in range(cores):
            left = pl.multiple_of(lax.rem(half + shift, cores) * columns, 128)
            pairs.append((weight_ref.at[rows, pl.ds(left, columns)], held_weight.at[shift, rows, :]))
        copies.append([])
        for n, (source, target) in enumerate(pairs):
            copies[-1].append(pltpu.make_async_copy(source, target, sems.at[c, n]))
            copies[-1][-1].start()
    for c in range(chunks):
        for copy in copies[c]:
            copy.wait()
        rows = pl.ds(c * height, height)
        for shift, out in enumerate(outs):
            product = jnp.dot(
                held_tokens[:, rows], held_weight[shift, rows, :], preferred_element_type=jnp.float32
            )
            if c == 0:
                out[...] = product
            else:
                out[...] += product


def base_terms(tokens, weight, cores):
    count, depth = tokens.shape
    columns = weight.shape[1] // cores
    chunks = 4
    return list(
        pl.pallas_call(
            functools.partial(base_kernel, chunks),
            out_shape=[jax.ShapeDtypeStruct((count, columns), jnp.float32)] * cores,
            in_specs=[pl.BlockSpec(memory_space=pl.ANY)] * 2,
            out_specs=[pl.BlockSpec(memory_space=pltpu.VMEM)] * cores,
            scratch_shapes=[
                pltpu.VMEM((count, depth), tokens.dtype),
                pltpu.VMEM((cores, depth, columns), weight.dtype),
                pltpu.SemaphoreType.DMA((chunks, 1 + cores)),
            ],
            compiler_params=pltpu.CompilerParams(vmem_limit_bytes=20 << 20),
            cost_estimate=pl.CostEstimate(flops=0, bytes_accessed=0, transcendentals=0),
        )(tokens, weight)
    )


def end_kernel(pieces, added, bases, row_steps, *refs):
    scores, base, refs = refs[:added], refs[added : added + bases], refs[added + bases :]
    arrays, (out, held, sems) = refs[:-3], refs[-3:]
    count, columns = out.shape
    rank = scores[0].shape[0]
    copies = []
    for n, (at, row, _) in enumerate(pieces):
        source = arrays[at].at[pl.ds(row, rank), pl.ds(arrays[at].shape[1] - columns, columns)]
        copies.append(pltpu.make_async_copy(source, held.at[pl.ds(n * rank, rank)], sems.at[n]))
        copies[-1].start()
    shrink = scores[0][:, pl.ds(0, count)]
    for x in scores[1:]:
        shrink = shrink + x[:, pl.ds(0, count)]
    shrink = adapter_scale * shrink
    high = shrink.astype(jnp.bfloat16).astype(jnp.float32)
    masks = [row_steps[pl.ds(0, 1), :] == by_part(group) for _, _, group in pieces]
    total = base[0][...]
    for x in base[1:]:
        total = total + x[...]
    for copy in copies:
        copy.wait()
    for term in (high, shrink - high):
        wide = jnp.concatenate([jnp.where(mask, term, 0.0) for mask in masks], axis=0)
        total = total + lax.dot_general(
            wide.astype(jnp.bfloat16),
            held[...],
            (((0,), (0,)), ((), ())),
            preferred_element_type=jnp.float32,
        )
    out[...] = total.astype(out.dtype)


def end(pieces, row_steps, scores, base, arrays, kind, cost):
    count, columns = base[0].shape
    rank = scores[0].shape[0]
    vmem = pl.BlockSpec(memory_space=pltpu.VMEM)
    return pl.pallas_call(
        functools.partial(end_kernel, pieces, len(scores), len(base)),
        out_shape=jax.ShapeDtypeStruct((count, columns), kind),
        in_specs=[vmem] * (1 + len(scores) + len(base))
        + [pl.BlockSpec(memory_space=pl.ANY)] * len(arrays),
        out_specs=vmem,
        scratch_shapes=[
            pltpu.VMEM((len(pieces) * rank, columns), jnp.bfloat16),
            pltpu.SemaphoreType.DMA((len(pieces),)),
        ],
        compiler_params=pltpu.CompilerParams(vmem_limit_bytes=16 << 20),
        cost_estimate=pl.CostEstimate(flops=0, bytes_accessed=cost, transcendentals=0),
    )(row_steps, *scores, *base, *arrays)


def on_device(tokens, base_weight, shrink_panels, expand_panels, adapter_home, fetch_list, seg_len):
    replicas, parts, cores = lax.axis_size("rep"), lax.axis_size("parts"), lax.axis_size("tp")
    tok_count = tokens.shape[0]
    columns = expand_panels.shape[2] // cores
    panels = jnp.swapaxes(shrink_panels, 1, 2)
    rank = panels.shape[1]
    tie = lax.optimization_barrier

    half = replicas // 2

    def grouped(steps):
        size = len(steps) // parts
        return [tuple(steps[p * size + g] for p in range(parts)) for g in range(size)]

    far = grouped(list(range(half, replicas)))
    near = grouped(list(range(parts, half))) + [tuple(reversed(range(parts)))]

    def hop(x, group):
        pairs = [
            (p * replicas + i, p * replicas + (i ^ group[p]))
            for p in range(parts)
            for i in range(replicas)
        ]
        return lax.ppermute(x, ("parts", "rep"), pairs)

    def shift_parts(x, shift):
        return lax.ppermute(x, "parts", [(i, (i + shift) % parts) for i in range(parts)])

    def shift_cores(x, shift):
        return lax.ppermute(x, "tp", [(i, (i + shift) % cores) for i in range(cores)])

    tables = (adapter_home, fetch_list, panels, expand_panels)
    groups = far + near
    send = pack(groups, columns, *tables)
    tokens, send = tie((tokens, send))
    recv = [hop(x, group) for x, group in zip(send, groups)]
    tokens_of = [tokens] + [shift_parts(tokens, shift) for shift in range(1, parts)]
    base = base_terms(tokens, base_weight, cores)
    base, recv[: len(far) - 1] = tie((base, recv[: len(far) - 1]))
    base = base[:1] + [shift_cores(x, shift + 1) for shift, x in enumerate(base[1:])]
    row_steps = steps_of_rows(tok_count, panels.shape[0], adapter_home, fetch_list, seg_len)
    steps_of = [row_steps] + [shift_parts(row_steps, shift) for shift in range(1, parts)]
    early, early_groups = recv[len(far) :] + recv[: len(far) - 1], near + far[:-1]
    last, last_group = recv[len(far) - 1], far[-1]

    count = len(early)
    first, sent = score(
        [tuple(range(count))],
        early_groups,
        tuple(range(count)),
        columns,
        steps_of[:1],
        [tokens],
        early,
    )
    passed = [shift_parts(sent, shift) for shift in range(1, parts)]
    base, first, passed, tokens_of[1:], last = tie((base, first, passed, tokens_of[1:], last))
    scores, sent = score(
        [(0,)] + [tuple(range(count + 1))] * (parts - 1),
        [last_group] + early_groups,
        (0,),
        columns,
        steps_of,
        tokens_of,
        [last] + early,
        first,
    )
    last_passed = [shift_parts(sent, shift) for shift in range(1, parts)]
    halves = [scores] + [shift_cores(scores, shift) for shift in range(1, cores)]
    whole = halves[0]
    for x in halves[1:]:
        whole = whole + x
    came = [
        shift_parts(whole[:, shift * tok_count : (shift + 1) * tok_count], -shift)
        for shift in range(1, parts)
    ]
    pieces = [(n, 0, group) for n, group in enumerate(early_groups + [last_group])]
    result = end(pieces, row_steps, halves, base, early + [last], jnp.float32, 1 << 24)
    pieces = []
    for shift in range(1, parts):
        at = shift - 1
        pieces += [(at, n * rank, turned(group, shift)) for n, group in enumerate(early_groups)]
        pieces.append((at + parts - 1, 0, turned(last_group, shift)))
    return end(pieces, row_steps, came, [result], passed + last_passed, jnp.bfloat16, 0)


def solution(mesh):
    return jax.shard_map(
        on_device,
        mesh=mesh,
        in_specs=(
            P(("parts", "rep"), "tp"),
            P("tp", None),
            P("rep", "tp", None),
            P("rep", None, None),
            P(),
            P(),
            P(("parts", "rep"), None),
        ),
        out_specs=P(("parts", "rep"), "tp"),
        check_vma=False,
    )
```

```python
import functools
import jax
import jax.numpy as jnp
from jax import lax
from jax.experimental import pallas as pl
from jax.experimental.pallas import tpu as pltpu
from jax.sharding import PartitionSpec as P

adapter_scale = 2.0


def upper(replicas):
    return (lax.axis_index("rep") >= replicas // 2).astype(jnp.int32)


def step_of(group, high):
    steps, moves = group
    part = lax.axis_index("parts")
    if moves:
        part = lax.rem(part + high, jnp.int32(len(steps)))
    chosen = jnp.int32(steps[0])
    for p, step in enumerate(steps):
        chosen = jnp.where(part == p, step, chosen)
    return chosen


def turned(group, shift):
    steps, moves = group
    return (tuple(steps[(p - shift) % len(steps)] for p in range(len(steps))), moves)


def slot_for(peer, me, per_home, home_ref, fetch_ref):
    first = me * per_home

    def look(j, slot):
        local = home_ref[fetch_ref[peer, j]] - first
        return jnp.where((local >= 0) & (local < per_home), local, slot)

    listed = fetch_ref.shape[1]
    return lax.fori_loop(0, listed, look, jnp.int32(0), unroll=listed <= 8)


def steps_kernel(per_home, home_ref, fetch_ref, lengths_ref, out):
    me = lax.axis_index("rep")
    rows = lax.broadcasted_iota(jnp.int32, out.shape, 1)
    result = jnp.zeros(out.shape, jnp.int32)
    start = jnp.int32(0)
    for j in range(fetch_ref.shape[1]):
        step = lax.div(home_ref[fetch_ref[me, j]], jnp.int32(per_home)) ^ me
        result = jnp.where(rows >= start, step, result)
        start = start + lengths_ref[0, j]
    out[...] = result


def steps_of_rows(count, per_home, adapter_home, fetch_list, seg_len):
    return pl.pallas_call(
        functools.partial(steps_kernel, per_home),
        out_shape=jax.ShapeDtypeStruct((8, count), jnp.int32),
        in_specs=[pl.BlockSpec(memory_space=pltpu.SMEM)] * 3,
        out_specs=pl.BlockSpec(memory_space=pltpu.VMEM),
        compiler_params=pltpu.CompilerParams(vmem_limit_bytes=2 << 20),
        cost_estimate=pl.CostEstimate(flops=0, bytes_accessed=0, transcendentals=0),
    )(adapter_home, fetch_list, seg_len)


def pack_kernel(groups, home_ref, fetch_ref, shrink_ref, expand_ref, *refs):
    outs, (held, in_sems, out_sems) = refs[:-3], refs[-3:]
    me = lax.axis_index("rep")
    other = 1 - upper(fetch_ref.shape[0])
    per_home, _, depth = shrink_ref.shape
    columns = expand_ref.shape[2] // lax.axis_size("tp")
    left = pl.multiple_of(lax.axis_index("tp") * columns, 128)
    cuts = in_sems.shape[1] - 1
    width = depth // cuts
    arriving = []
    for at, group in enumerate(groups):
        slot = slot_for(me ^ step_of(group, other), me, per_home, home_ref, fetch_ref)
        pieces = [(shrink_ref.at[slot, :, pl.ds(n * width, width)], n * width, width) for n in range(cuts)]
        pieces.append((expand_ref.at[slot, :, pl.ds(left, columns)], depth, columns))
        for n, (source, start, size) in enumerate(pieces):
            target = held.at[at, :, pl.ds(start, size)]
            copy = pltpu.make_async_copy(source, target, in_sems.at[at, n])
            copy.start()
            leave = pltpu.make_async_copy(target, outs[at].at[:, pl.ds(start, size)], out_sems.at[at, n])
            arriving.append((copy, leave))
    for copy, leave in arriving:
        copy.wait()
        leave.start()
    for _, leave in arriving:
        leave.wait()


def pack(groups, columns, adapter_home, fetch_list, panels, expand_panels):
    rank, depth = panels.shape[1:]
    shape = (rank, depth + columns)
    cuts = 4
    return list(
        pl.pallas_call(
            functools.partial(pack_kernel, groups),
            out_shape=[jax.ShapeDtypeStruct(shape, panels.dtype)] * len(groups),
            in_specs=[pl.BlockSpec(memory_space=pltpu.SMEM)] * 2 + [pl.BlockSpec(memory_space=pl.ANY)] * 2,
            out_specs=[pl.BlockSpec(memory_space=pl.ANY)] * len(groups),
            scratch_shapes=[pltpu.VMEM((len(groups),) + shape, panels.dtype)]
            + [pltpu.SemaphoreType.DMA((len(groups), cuts + 1))] * 2,
            compiler_params=pltpu.CompilerParams(vmem_limit_bytes=56 << 20),
            cost_estimate=pl.CostEstimate(flops=0, bytes_accessed=0, transcendentals=0),
        )(adapter_home, fetch_list, panels, expand_panels)
    )


def score_kernel(plan, groups, kept, chunks, has_prior, replicas, *refs):
    sets, many = len(plan), len(groups)
    row_steps, refs = refs[:sets], refs[sets:]
    prior, refs = (refs[0], refs[1:]) if has_prior else (None, refs)
    tokens, panels = refs[:sets], refs[sets : sets + many]
    out, out_expand = refs[sets + many :]
    rank, (count, depth) = out.shape[0], tokens[0].shape
    for i, n in enumerate(kept):
        out_expand[pl.ds(i * rank, rank), :] = panels[n][:, pl.ds(depth, out_expand.shape[1])]
    high = upper(replicas)
    width = depth // chunks
    sums = [None] * sets
    for c in range(chunks):
        cols = pl.ds(c * width, width)
        for t, used in enumerate(plan):
            product = lax.dot_general(
                jnp.concatenate([panels[n][:, cols] for n in used], axis=0),
                tokens[t][:, cols],
                (((1,), (1,)), ((), ())),
                preferred_element_type=jnp.float32,
            )
            sums[t] = product if c == 0 else sums[t] + product
    for t, used in enumerate(plan):
        mine = row_steps[t][pl.ds(0, 1), :]
        total = prior[...] if has_prior and t == 0 else jnp.zeros((rank, count), jnp.float32)
        for n, panel in enumerate(used):
            term = sums[t][n * rank : (n + 1) * rank]
            total = total + jnp.where(mine == step_of(groups[panel], high), term, 0.0)
        out[:, pl.ds(t * count, count)] = total


def score(plan, groups, kept, columns, row_steps, tokens_of, panels, prior=None):
    count, depth = tokens_of[0].shape
    rank = panels[0].shape[0]
    chunks = 4
    prior = [] if prior is None else [prior]
    vmem = pl.BlockSpec(memory_space=pltpu.VMEM)
    outs = [(rank, len(plan) * count), (len(kept) * rank, columns)]
    arrays = list(row_steps) + prior + list(tokens_of) + list(panels)
    need = 4 * len(plan) * count * (rank * len(panels) + depth) + 4 * len(panels) * rank * (depth + columns)
    return pl.pallas_call(
        functools.partial(
            score_kernel, plan, groups, kept, chunks, bool(prior), lax.axis_size("rep")
        ),
        out_shape=[
            jax.ShapeDtypeStruct(shape, panels[0].dtype if n else jnp.float32)
            for n, shape in enumerate(outs)
        ],
        in_specs=[vmem] * len(arrays),
        out_specs=[vmem] * len(outs),
        compiler_params=pltpu.CompilerParams(vmem_limit_bytes=need + (2 << 20)),
        cost_estimate=pl.CostEstimate(flops=0, bytes_accessed=0, transcendentals=0),
    )(*arrays)


def base_kernel(chunks, tokens_ref, weight_ref, *refs):
    outs, (held_tokens, held_weight, sems) = refs[:-3], refs[-3:]
    cores, half = len(outs), lax.axis_index("tp")
    columns = outs[0].shape[1]
    height = tokens_ref.shape[1] // chunks
    copies = []
    for c in range(chunks):
        rows = pl.ds(c * height, height)
        pairs = [(tokens_ref.at[:, rows], held_tokens.at[:, rows])]
        for shift in range(cores):
            left = pl.multiple_of(lax.rem(half + shift, cores) * columns, 128)
            pairs.append((weight_ref.at[rows, pl.ds(left, columns)], held_weight.at[shift, rows, :]))
        copies.append([])
        for n, (source, target) in enumerate(pairs):
            copies[-1].append(pltpu.make_async_copy(source, target, sems.at[c, n]))
            copies[-1][-1].start()
    for c in range(chunks):
        for copy in copies[c]:
            copy.wait()
        rows = pl.ds(c * height, height)
        for shift, out in enumerate(outs):
            product = jnp.dot(
                held_tokens[:, rows], held_weight[shift, rows, :], preferred_element_type=jnp.float32
            )
            if c == 0:
                out[...] = product
            else:
                out[...] += product


def base_terms(tokens, weight, cores):
    count, depth = tokens.shape
    columns = weight.shape[1] // cores
    chunks = 4
    return list(
        pl.pallas_call(
            functools.partial(base_kernel, chunks),
            out_shape=[jax.ShapeDtypeStruct((count, columns), jnp.float32)] * cores,
            in_specs=[pl.BlockSpec(memory_space=pl.ANY)] * 2,
            out_specs=[pl.BlockSpec(memory_space=pltpu.VMEM)] * cores,
            scratch_shapes=[
                pltpu.VMEM((count, depth), tokens.dtype),
                pltpu.VMEM((cores, depth, columns), weight.dtype),
                pltpu.SemaphoreType.DMA((chunks, 1 + cores)),
            ],
            compiler_params=pltpu.CompilerParams(vmem_limit_bytes=20 << 20),
            cost_estimate=pl.CostEstimate(flops=0, bytes_accessed=0, transcendentals=0),
        )(tokens, weight)
    )


def end_kernel(pieces, added, bases, replicas, row_steps, *refs):
    scores, base, refs = refs[:added], refs[added : added + bases], refs[added + bases :]
    arrays, (out, held, sems) = refs[:-3], refs[-3:]
    count, columns = out.shape
    rank = scores[0].shape[0]
    copies = []
    for n, (at, row, _) in enumerate(pieces):
        source = arrays[at].at[pl.ds(row, rank), pl.ds(arrays[at].shape[1] - columns, columns)]
        copies.append(pltpu.make_async_copy(source, held.at[pl.ds(n * rank, rank)], sems.at[n]))
        copies[-1].start()
    shrink = scores[0][:, pl.ds(0, count)]
    for x in scores[1:]:
        shrink = shrink + x[:, pl.ds(0, count)]
    shrink = adapter_scale * shrink
    high = shrink.astype(jnp.bfloat16).astype(jnp.float32)
    place = upper(replicas)
    masks = [row_steps[pl.ds(0, 1), :] == step_of(group, place) for _, _, group in pieces]
    total = base[0][...]
    for x in base[1:]:
        total = total + x[...]
    for copy in copies:
        copy.wait()
    for term in (high, shrink - high):
        wide = jnp.concatenate([jnp.where(mask, term, 0.0) for mask in masks], axis=0)
        total = total + lax.dot_general(
            wide.astype(jnp.bfloat16),
            held[...],
            (((0,), (0,)), ((), ())),
            preferred_element_type=jnp.float32,
        )
    out[...] = total.astype(out.dtype)


def end(pieces, row_steps, scores, base, arrays, kind, cost):
    count, columns = base[0].shape
    rank = scores[0].shape[0]
    vmem = pl.BlockSpec(memory_space=pltpu.VMEM)
    return pl.pallas_call(
        functools.partial(end_kernel, pieces, len(scores), len(base), lax.axis_size("rep")),
        out_shape=jax.ShapeDtypeStruct((count, columns), kind),
        in_specs=[vmem] * (1 + len(scores) + len(base))
        + [pl.BlockSpec(memory_space=pl.ANY)] * len(arrays),
        out_specs=vmem,
        scratch_shapes=[
            pltpu.VMEM((len(pieces) * rank, columns), jnp.bfloat16),
            pltpu.SemaphoreType.DMA((len(pieces),)),
        ],
        compiler_params=pltpu.CompilerParams(vmem_limit_bytes=16 << 20),
        cost_estimate=pl.CostEstimate(flops=0, bytes_accessed=cost, transcendentals=0),
    )(row_steps, *scores, *base, *arrays)


def on_device(tokens, base_weight, shrink_panels, expand_panels, adapter_home, fetch_list, seg_len):
    replicas, parts, cores = lax.axis_size("rep"), lax.axis_size("parts"), lax.axis_size("tp")
    tok_count = tokens.shape[0]
    columns = expand_panels.shape[2] // cores
    panels = jnp.swapaxes(shrink_panels, 1, 2)
    rank = panels.shape[1]
    tie = lax.optimization_barrier

    half = replicas // 2
    far = [(tuple(range(step, step + parts)), True) for step in range(half, replicas, parts)]
    size = half // parts - 1
    near = [(tuple(parts + p * size + g for p in range(parts)), False) for g in range(size)]
    near.append((tuple(reversed(range(parts))), False))

    def hop(x, group):
        steps, moves = group
        pairs = []
        for p in range(parts):
            for i in range(replicas):
                step = steps[(p + (moves and i >= half)) % parts]
                pairs.append((p * replicas + (i ^ step), p * replicas + i))
        return lax.ppermute(x, ("parts", "rep"), pairs)

    def shift_parts(x, shift):
        return lax.ppermute(x, "parts", [(i, (i + shift) % parts) for i in range(parts)])

    def shift_cores(x, shift):
        return lax.ppermute(x, "tp", [(i, (i + shift) % cores) for i in range(cores)])

    tables = (adapter_home, fetch_list, panels, expand_panels)
    groups = far + near
    send = pack(groups, columns, *tables)
    tokens, send = tie((tokens, send))
    recv = [hop(x, group) for x, group in zip(send, groups)]
    tokens_of = [tokens] + [shift_parts(tokens, shift) for shift in range(1, parts)]
    base = base_terms(tokens, base_weight, cores)
    base, recv[: len(far) - 1] = tie((base, recv[: len(far) - 1]))
    base = base[:1] + [shift_cores(x, shift + 1) for shift, x in enumerate(base[1:])]
    row_steps = steps_of_rows(tok_count, panels.shape[0], adapter_home, fetch_list, seg_len)
    steps_of = [row_steps] + [shift_parts(row_steps, shift) for shift in range(1, parts)]
    early, early_groups = recv[len(far) :] + recv[: len(far) - 1], near + far[:-1]
    last, last_group = recv[len(far) - 1], far[-1]

    count = len(early)
    first, sent = score(
        [tuple(range(count))],
        early_groups,
        tuple(range(count)),
        columns,
        steps_of[:1],
        [tokens],
        early,
    )
    passed = [shift_parts(sent, shift) for shift in range(1, parts)]
    base, first, passed, tokens_of[1:], last = tie((base, first, passed, tokens_of[1:], last))
    scores, sent = score(
        [(0,)] + [tuple(range(count + 1))] * (parts - 1),
        [last_group] + early_groups,
        (0,),
        columns,
        steps_of,
        tokens_of,
        [last] + early,
        first,
    )
    last_passed = [shift_parts(sent, shift) for shift in range(1, parts)]
    halves = [scores] + [shift_cores(scores, shift) for shift in range(1, cores)]
    whole = halves[0]
    for x in halves[1:]:
        whole = whole + x
    came = [
        shift_parts(whole[:, shift * tok_count : (shift + 1) * tok_count], -shift)
        for shift in range(1, parts)
    ]
    pieces = [(n, 0, group) for n, group in enumerate(early_groups + [last_group])]
    result = end(pieces, row_steps, halves, base, early + [last], jnp.float32, 1 << 24)
    pieces = []
    for shift in range(1, parts):
        at = shift - 1
        pieces += [(at, n * rank, turned(group, shift)) for n, group in enumerate(early_groups)]
        pieces.append((at + parts - 1, 0, turned(last_group, shift)))
    return end(pieces, row_steps, came, [result], passed + last_passed, jnp.bfloat16, 0)


def solution(mesh):
    return jax.shard_map(
        on_device,
        mesh=mesh,
        in_specs=(
            P(("parts", "rep"), "tp"),
            P("tp", None),
            P("rep", "tp", None),
            P("rep", None, None),
            P(),
            P(),
            P(("parts", "rep"), None),
        ),
        out_specs=P(("parts", "rep"), "tp"),
        check_vma=False,
    )
```

```python
import functools
import jax
import jax.numpy as jnp
from jax import lax
from jax.experimental import pallas as pl
from jax.experimental.pallas import tpu as pltpu
from jax.sharding import PartitionSpec as P

adapter_scale = 2.0


def upper(replicas):
    return (lax.axis_index("rep") >= replicas // 2).astype(jnp.int32)


def step_of(group, high):
    steps, moves = group
    part = lax.axis_index("parts")
    if moves:
        part = lax.rem(part + high, jnp.int32(len(steps)))
    chosen = jnp.int32(steps[0])
    for p, step in enumerate(steps):
        chosen = jnp.where(part == p, step, chosen)
    return chosen


def turned(group, shift):
    steps, moves = group
    return (tuple(steps[(p - shift) % len(steps)] for p in range(len(steps))), moves)


def slot_for(peer, me, per_home, home_ref, fetch_ref):
    first = me * per_home

    def look(j, slot):
        local = home_ref[fetch_ref[peer, j]] - first
        return jnp.where((local >= 0) & (local < per_home), local, slot)

    listed = fetch_ref.shape[1]
    return lax.fori_loop(0, listed, look, jnp.int32(0), unroll=listed <= 8)


def steps_kernel(per_home, home_ref, fetch_ref, lengths_ref, out):
    me = lax.axis_index("rep")
    rows = lax.broadcasted_iota(jnp.int32, out.shape, 1)
    result = jnp.zeros(out.shape, jnp.int32)
    start = jnp.int32(0)
    for j in range(fetch_ref.shape[1]):
        step = lax.div(home_ref[fetch_ref[me, j]], jnp.int32(per_home)) ^ me
        result = jnp.where(rows >= start, step, result)
        start = start + lengths_ref[0, j]
    out[...] = result


def steps_of_rows(count, per_home, adapter_home, fetch_list, seg_len):
    return pl.pallas_call(
        functools.partial(steps_kernel, per_home),
        out_shape=jax.ShapeDtypeStruct((8, count), jnp.int32),
        in_specs=[pl.BlockSpec(memory_space=pltpu.SMEM)] * 3,
        out_specs=pl.BlockSpec(memory_space=pltpu.VMEM),
        compiler_params=pltpu.CompilerParams(vmem_limit_bytes=2 << 20),
        cost_estimate=pl.CostEstimate(flops=0, bytes_accessed=0, transcendentals=0),
    )(adapter_home, fetch_list, seg_len)


def pack_kernel(blocks, home_ref, fetch_ref, shrink_ref, expand_ref, *refs):
    outs, (held, in_sems, out_sems) = refs[:-3], refs[-3:]
    me = lax.axis_index("rep")
    other = 1 - upper(fetch_ref.shape[0])
    per_home, _, depth = shrink_ref.shape
    columns = expand_ref.shape[2] // lax.axis_size("tp")
    left = pl.multiple_of(lax.axis_index("tp") * columns, 128)
    cuts = in_sems.shape[1] - 1
    width = depth // cuts
    arriving = []
    for at, (group, first, rows) in enumerate(blocks):
        step = jnp.maximum(step_of(group, other), 0)
        slot = slot_for(me ^ step, me, per_home, home_ref, fetch_ref)
        rows = pl.ds(first, rows)
        pieces = [(shrink_ref.at[slot, rows, pl.ds(n * width, width)], n * width, width) for n in range(cuts)]
        pieces.append((expand_ref.at[slot, rows, pl.ds(left, columns)], depth, columns))
        for n, (source, start, size) in enumerate(pieces):
            target = held.at[at, rows, pl.ds(start, size)]
            copy = pltpu.make_async_copy(source, target, in_sems.at[at, n])
            copy.start()
            leave = pltpu.make_async_copy(target, outs[at].at[:, pl.ds(start, size)], out_sems.at[at, n])
            arriving.append((copy, leave))
    for copy, leave in arriving:
        copy.wait()
        leave.start()
    for _, leave in arriving:
        leave.wait()


def pack(blocks, columns, adapter_home, fetch_list, panels, expand_panels):
    rank, depth = panels.shape[1:]
    width = depth + columns
    cuts = 4
    return list(
        pl.pallas_call(
            functools.partial(pack_kernel, blocks),
            out_shape=[jax.ShapeDtypeStruct((rows, width), panels.dtype) for _, _, rows in blocks],
            in_specs=[pl.BlockSpec(memory_space=pltpu.SMEM)] * 2 + [pl.BlockSpec(memory_space=pl.ANY)] * 2,
            out_specs=[pl.BlockSpec(memory_space=pl.ANY)] * len(blocks),
            scratch_shapes=[pltpu.VMEM((len(blocks), rank, width), panels.dtype)]
            + [pltpu.SemaphoreType.DMA((len(blocks), cuts + 1))] * 2,
            compiler_params=pltpu.CompilerParams(vmem_limit_bytes=56 << 20),
            cost_estimate=pl.CostEstimate(flops=0, bytes_accessed=0, transcendentals=0),
        )(adapter_home, fetch_list, panels, expand_panels)
    )


def score_kernel(plan, blocks, kept, chunks, has_prior, replicas, *refs):
    sets, many = len(plan), len(blocks)
    row_steps, refs = refs[:sets], refs[sets:]
    prior, refs = (refs[0], refs[1:]) if has_prior else (None, refs)
    tokens, panels = refs[:sets], refs[sets : sets + many]
    out, out_expand = refs[sets + many :]
    rank, (count, depth) = out.shape[0], tokens[0].shape
    filled = 0
    for n in kept:
        rows = blocks[n][2]
        out_expand[pl.ds(filled, rows), :] = panels[n][:, pl.ds(depth, out_expand.shape[1])]
        filled += rows
    high = upper(replicas)
    width = depth // chunks
    sums = [None] * sets
    for c in range(chunks):
        cols = pl.ds(c * width, width)
        for t, used in enumerate(plan):
            product = lax.dot_general(
                jnp.concatenate([panels[n][:, cols] for n in used], axis=0),
                tokens[t][:, cols],
                (((1,), (1,)), ((), ())),
                preferred_element_type=jnp.float32,
            )
            sums[t] = product if c == 0 else sums[t] + product
    for t, used in enumerate(plan):
        mine = row_steps[t][pl.ds(0, 1), :]
        total = prior[...] if has_prior and t == 0 else jnp.zeros((rank, count), jnp.float32)
        filled = 0
        for panel in used:
            group, first, rows = blocks[panel]
            term = jnp.where(mine == step_of(group, high), sums[t][filled : filled + rows], 0.0)
            filled += rows
            ends = [jnp.zeros((size, count), jnp.float32) for size in (first, rank - first - rows)]
            term = [x for x in (ends[0], term, ends[1]) if x.shape[0]]
            total = total + (jnp.concatenate(term, axis=0) if len(term) > 1 else term[0])
        out[:, pl.ds(t * count, count)] = total


def score(plan, blocks, kept, rank, columns, row_steps, tokens_of, panels, prior=None):
    count, depth = tokens_of[0].shape
    chunks = 4
    prior = [] if prior is None else [prior]
    vmem = pl.BlockSpec(memory_space=pltpu.VMEM)
    outs = [(rank, len(plan) * count), (sum(blocks[n][2] for n in kept), columns)]
    arrays = list(row_steps) + prior + list(tokens_of) + list(panels)
    need = 4 * len(plan) * count * (rank * len(panels) + depth) + 4 * len(panels) * rank * (depth + columns)
    return pl.pallas_call(
        functools.partial(
            score_kernel, plan, blocks, kept, chunks, bool(prior), lax.axis_size("rep")
        ),
        out_shape=[
            jax.ShapeDtypeStruct(shape, panels[0].dtype if n else jnp.float32)
            for n, shape in enumerate(outs)
        ],
        in_specs=[vmem] * len(arrays),
        out_specs=[vmem] * len(outs),
        compiler_params=pltpu.CompilerParams(vmem_limit_bytes=need + (2 << 20)),
        cost_estimate=pl.CostEstimate(flops=0, bytes_accessed=0, transcendentals=0),
    )(*arrays)


def base_kernel(chunks, tokens_ref, weight_ref, *refs):
    outs, (held_tokens, held_weight, sems) = refs[:-3], refs[-3:]
    cores, half = len(outs), lax.axis_index("tp")
    columns = outs[0].shape[1]
    height = tokens_ref.shape[1] // chunks
    copies = []
    for c in range(chunks):
        rows = pl.ds(c * height, height)
        pairs = [(tokens_ref.at[:, rows], held_tokens.at[:, rows])]
        for shift in range(cores):
            left = pl.multiple_of(lax.rem(half + shift, cores) * columns, 128)
            pairs.append((weight_ref.at[rows, pl.ds(left, columns)], held_weight.at[shift, rows, :]))
        copies.append([])
        for n, (source, target) in enumerate(pairs):
            copies[-1].append(pltpu.make_async_copy(source, target, sems.at[c, n]))
            copies[-1][-1].start()
    for c in range(chunks):
        for copy in copies[c]:
            copy.wait()
        rows = pl.ds(c * height, height)
        for shift, out in enumerate(outs):
            product = jnp.dot(
                held_tokens[:, rows], held_weight[shift, rows, :], preferred_element_type=jnp.float32
            )
            if c == 0:
                out[...] = product
            else:
                out[...] += product


def base_terms(tokens, weight, cores):
    count, depth = tokens.shape
    columns = weight.shape[1] // cores
    chunks = 4
    return list(
        pl.pallas_call(
            functools.partial(base_kernel, chunks),
            out_shape=[jax.ShapeDtypeStruct((count, columns), jnp.float32)] * cores,
            in_specs=[pl.BlockSpec(memory_space=pl.ANY)] * 2,
            out_specs=[pl.BlockSpec(memory_space=pltpu.VMEM)] * cores,
            scratch_shapes=[
                pltpu.VMEM((count, depth), tokens.dtype),
                pltpu.VMEM((cores, depth, columns), weight.dtype),
                pltpu.SemaphoreType.DMA((chunks, 1 + cores)),
            ],
            compiler_params=pltpu.CompilerParams(vmem_limit_bytes=20 << 20),
            cost_estimate=pl.CostEstimate(flops=0, bytes_accessed=0, transcendentals=0),
        )(tokens, weight)
    )


def end_kernel(pieces, added, bases, replicas, row_steps, *refs):
    scores, base, refs = refs[:added], refs[added : added + bases], refs[added + bases :]
    arrays, (out, held, sems) = refs[:-3], refs[-3:]
    count, columns = out.shape
    copies, filled = [], 0
    for n, (at, row, (_, _, rows)) in enumerate(pieces):
        source = arrays[at].at[pl.ds(row, rows), pl.ds(arrays[at].shape[1] - columns, columns)]
        copies.append(pltpu.make_async_copy(source, held.at[pl.ds(filled, rows)], sems.at[n]))
        copies[-1].start()
        filled += rows
    shrink = scores[0][:, pl.ds(0, count)]
    for x in scores[1:]:
        shrink = shrink + x[:, pl.ds(0, count)]
    shrink = adapter_scale * shrink
    high = shrink.astype(jnp.bfloat16).astype(jnp.float32)
    place = upper(replicas)
    masks = [row_steps[pl.ds(0, 1), :] == step_of(block[0], place) for _, _, block in pieces]
    total = base[0][...]
    for x in base[1:]:
        total = total + x[...]
    for copy in copies:
        copy.wait()
    for term in (high, shrink - high):
        wide = [
            jnp.where(mask, term[first : first + rows], 0.0)
            for mask, (_, _, (_, first, rows)) in zip(masks, pieces)
        ]
        wide = jnp.concatenate(wide, axis=0)
        total = total + lax.dot_general(
            wide.astype(jnp.bfloat16),
            held[...],
            (((0,), (0,)), ((), ())),
            preferred_element_type=jnp.float32,
        )
    out[...] = total.astype(out.dtype)


def end(pieces, row_steps, scores, base, arrays, kind, cost):
    count, columns = base[0].shape
    vmem = pl.BlockSpec(memory_space=pltpu.VMEM)
    return pl.pallas_call(
        functools.partial(end_kernel, pieces, len(scores), len(base), lax.axis_size("rep")),
        out_shape=jax.ShapeDtypeStruct((count, columns), kind),
        in_specs=[vmem] * (1 + len(scores) + len(base))
        + [pl.BlockSpec(memory_space=pl.ANY)] * len(arrays),
        out_specs=vmem,
        scratch_shapes=[
            pltpu.VMEM((sum(rows for _, _, (_, _, rows) in pieces), columns), jnp.bfloat16),
            pltpu.SemaphoreType.DMA((len(pieces),)),
        ],
        compiler_params=pltpu.CompilerParams(vmem_limit_bytes=16 << 20),
        cost_estimate=pl.CostEstimate(flops=0, bytes_accessed=cost, transcendentals=0),
    )(row_steps, *scores, *base, *arrays)


def on_device(tokens, base_weight, shrink_panels, expand_panels, adapter_home, fetch_list, seg_len):
    replicas, parts, cores = lax.axis_size("rep"), lax.axis_size("parts"), lax.axis_size("tp")
    tok_count = tokens.shape[0]
    columns = expand_panels.shape[2] // cores
    panels = jnp.swapaxes(shrink_panels, 1, 2)
    rank = panels.shape[1]
    tie = lax.optimization_barrier

    half = replicas // 2
    far = [(tuple(range(step, step + parts)), True) for step in range(half, replicas, parts)]
    size = half // parts - 1
    near = [(tuple(parts + p * size + g for p in range(parts)), False) for g in range(size)]
    near.append((tuple(reversed(range(parts))), False))

    def hop(x, group):
        steps, moves = group
        pairs = []
        for p in range(parts):
            for i in range(replicas):
                step = steps[(p + (moves and i >= half)) % parts]
                if step < 0:
                    continue
                pairs.append((p * replicas + (i ^ step), p * replicas + i))
        return lax.ppermute(x, ("parts", "rep"), pairs)

    def shift_parts(x, shift):
        return lax.ppermute(x, "parts", [(i, (i + shift) % parts) for i in range(parts)])

    def shift_cores(x, shift):
        return lax.ppermute(x, "tp", [(i, (i + shift) % cores) for i in range(cores)])

    tables = (adapter_home, fetch_list, panels, expand_panels)
    low = rank - 16
    steps, moves = far[0]
    keep = (tuple(step if p % 2 == 0 else -1 for p, step in enumerate(steps)), moves)
    take = (tuple(steps[p + 1] if p % 2 == 0 else -1 for p in range(parts)), moves)
    blocks = [(group, 0, rank) for group in near + far[1:-1]]
    blocks += [(far[0], 0, low), (keep, low, rank - low), (take, low, rank - low)]
    last_blocks = [(far[-1], 0, rank)]
    *send, keep_send, take_send, last_send = pack(blocks + last_blocks, columns, *tables)
    tokens, send, last_send = tie((tokens, send, last_send))
    early = [hop(x, block[0]) for x, block in zip(send, blocks)]
    last = [hop(last_send, far[-1])]
    tokens_of = [tokens] + [shift_parts(tokens, shift) for shift in range(1, parts)]
    at = len(near) - 1
    keep_send, early[at] = tie((keep_send, early[at]))
    early.append(hop(keep_send, keep))
    take_send, base_weight, seg_len, early[-1] = tie((take_send, base_weight, seg_len, early[-1]))
    early.append(hop(take_send, take))
    base = base_terms(tokens, base_weight, cores)
    base, early[len(near) : -2] = tie((base, early[len(near) : -2]))
    base = base[:1] + [shift_cores(x, shift + 1) for shift, x in enumerate(base[1:])]
    row_steps = steps_of_rows(tok_count, panels.shape[0], adapter_home, fetch_list, seg_len)
    steps_of = [row_steps] + [shift_parts(row_steps, shift) for shift in range(1, parts)]

    count = len(early)
    first, sent = score(
        [tuple(range(count))], blocks, tuple(range(count)), rank, columns, steps_of[:1], [tokens], early
    )
    passed = [shift_parts(sent, shift) for shift in range(1, parts)]
    base, first, passed, tokens_of[1:], last = tie((base, first, passed, tokens_of[1:], last))
    ends = tuple(range(len(last)))
    scores, sent = score(
        [ends] + [tuple(range(len(last) + count))] * (parts - 1),
        last_blocks + blocks,
        ends,
        rank,
        columns,
        steps_of,
        tokens_of,
        last + early,
        first,
    )
    last_passed = [shift_parts(sent, shift) for shift in range(1, parts)]
    halves = [scores] + [shift_cores(scores, shift) for shift in range(1, cores)]
    whole = halves[0]
    for x in halves[1:]:
        whole = whole + x
    came = [
        shift_parts(whole[:, shift * tok_count : (shift + 1) * tok_count], -shift)
        for shift in range(1, parts)
    ]
    pieces = [(n, 0, block) for n, block in enumerate(blocks + last_blocks)]
    result = end(pieces, row_steps, halves, base, early + last, jnp.float32, 1 << 24)
    pieces = []
    for at in range(parts - 1):
        for number, many in ((at, blocks), (at + parts - 1, last_blocks)):
            row = 0
            for group, top, rows in many:
                pieces.append((number, row, (turned(group, at + 1), top, rows)))
                row += rows
    return end(pieces, row_steps, came, [result], passed + last_passed, jnp.bfloat16, 0)


def solution(mesh):
    return jax.shard_map(
        on_device,
        mesh=mesh,
        in_specs=(
            P(("parts", "rep"), "tp"),
            P("tp", None),
            P("rep", "tp", None),
            P("rep", None, None),
            P(),
            P(),
            P(("parts", "rep"), None),
        ),
        out_specs=P(("parts", "rep"), "tp"),
        check_vma=False,
    )
```

```python
import functools
import jax
import jax.numpy as jnp
from jax import lax
from jax.experimental import pallas as pl
from jax.experimental.pallas import tpu as pltpu
from jax.sharding import PartitionSpec as P

adapter_scale = 2.0


def upper(replicas):
    return (lax.axis_index("rep") >= replicas // 2).astype(jnp.int32)


def step_of(group, high):
    steps, moves = group
    part = lax.axis_index("parts")
    if moves:
        part = lax.rem(part + high, jnp.int32(len(steps)))
    chosen = jnp.int32(steps[0])
    for p, step in enumerate(steps):
        chosen = jnp.where(part == p, step, chosen)
    return chosen


def turned(group, shift):
    steps, moves = group
    return (tuple(steps[(p - shift) % len(steps)] for p in range(len(steps))), moves)


def slot_for(peer, me, per_home, home_ref, fetch_ref):
    first = me * per_home

    def look(j, slot):
        local = home_ref[fetch_ref[peer, j]] - first
        return jnp.where((local >= 0) & (local < per_home), local, slot)

    listed = fetch_ref.shape[1]
    return lax.fori_loop(0, listed, look, jnp.int32(0), unroll=listed <= 8)


def steps_kernel(per_home, home_ref, fetch_ref, lengths_ref, out):
    me = lax.axis_index("rep")
    rows = lax.broadcasted_iota(jnp.int32, out.shape, 1)
    result = jnp.zeros(out.shape, jnp.int32)
    start = jnp.int32(0)
    for j in range(fetch_ref.shape[1]):
        step = lax.div(home_ref[fetch_ref[me, j]], jnp.int32(per_home)) ^ me
        result = jnp.where(rows >= start, step, result)
        start = start + lengths_ref[0, j]
    out[...] = result


def steps_of_rows(count, per_home, adapter_home, fetch_list, seg_len):
    return pl.pallas_call(
        functools.partial(steps_kernel, per_home),
        out_shape=jax.ShapeDtypeStruct((8, count), jnp.int32),
        in_specs=[pl.BlockSpec(memory_space=pltpu.SMEM)] * 3,
        out_specs=pl.BlockSpec(memory_space=pltpu.VMEM),
        compiler_params=pltpu.CompilerParams(vmem_limit_bytes=2 << 20),
        cost_estimate=pl.CostEstimate(flops=0, bytes_accessed=0, transcendentals=0),
    )(adapter_home, fetch_list, seg_len)


def pack_kernel(groups, home_ref, fetch_ref, shrink_ref, expand_ref, *refs):
    outs, (held, in_sems, out_sems) = refs[:-3], refs[-3:]
    me = lax.axis_index("rep")
    other = 1 - upper(fetch_ref.shape[0])
    per_home, _, depth = shrink_ref.shape
    columns = expand_ref.shape[2] // lax.axis_size("tp")
    left = pl.multiple_of(lax.axis_index("tp") * columns, 128)
    cuts = in_sems.shape[1] - 1
    width = depth // cuts
    arriving = []
    for at, group in enumerate(groups):
        slot = slot_for(me ^ step_of(group, other), me, per_home, home_ref, fetch_ref)
        pieces = [(shrink_ref.at[slot, :, pl.ds(n * width, width)], n * width, width) for n in range(cuts)]
        pieces.append((expand_ref.at[slot, :, pl.ds(left, columns)], depth, columns))
        for n, (source, start, size) in enumerate(pieces):
            target = held.at[at, :, pl.ds(start, size)]
            copy = pltpu.make_async_copy(source, target, in_sems.at[at, n])
            copy.start()
            leave = pltpu.make_async_copy(target, outs[at].at[:, pl.ds(start, size)], out_sems.at[at, n])
            arriving.append((copy, leave))
    for copy, leave in arriving:
        copy.wait()
        leave.start()
    for _, leave in arriving:
        leave.wait()


def pack(groups, columns, adapter_home, fetch_list, panels, expand_panels):
    rank, depth = panels.shape[1:]
    shape = (rank, depth + columns)
    cuts = 4
    return list(
        pl.pallas_call(
            functools.partial(pack_kernel, groups),
            out_shape=[jax.ShapeDtypeStruct(shape, panels.dtype)] * len(groups),
            in_specs=[pl.BlockSpec(memory_space=pltpu.SMEM)] * 2 + [pl.BlockSpec(memory_space=pl.ANY)] * 2,
            out_specs=[pl.BlockSpec(memory_space=pl.ANY)] * len(groups),
            scratch_shapes=[pltpu.VMEM((len(groups),) + shape, panels.dtype)]
            + [pltpu.SemaphoreType.DMA((len(groups), cuts + 1))] * 2,
            compiler_params=pltpu.CompilerParams(vmem_limit_bytes=56 << 20),
            cost_estimate=pl.CostEstimate(flops=0, bytes_accessed=0, transcendentals=0),
        )(adapter_home, fetch_list, panels, expand_panels)
    )


def score_kernel(plan, groups, kept, chunks, has_prior, replicas, *refs):
    sets, many = len(plan), len(groups)
    row_steps, refs = refs[:sets], refs[sets:]
    prior, refs = (refs[0], refs[1:]) if has_prior else (None, refs)
    tokens, panels = refs[:sets], refs[sets : sets + many]
    out, out_expand = refs[sets + many :]
    rank, (count, depth) = out.shape[0], tokens[0].shape
    for i, n in enumerate(kept):
        out_expand[pl.ds(i * rank, rank), :] = panels[n][:, pl.ds(depth, out_expand.shape[1])]
    high = upper(replicas)
    width = depth // chunks
    sums = [None] * sets
    for c in range(chunks):
        cols = pl.ds(c * width, width)
        for t, used in enumerate(plan):
            product = lax.dot_general(
                jnp.concatenate([panels[n][:, cols] for n in used], axis=0),
                tokens[t][:, cols],
                (((1,), (1,)), ((), ())),
                preferred_element_type=jnp.float32,
            )
            sums[t] = product if c == 0 else sums[t] + product
    for t, used in enumerate(plan):
        mine = row_steps[t][pl.ds(0, 1), :]
        total = prior[...] if has_prior and t == 0 else jnp.zeros((rank, count), jnp.float32)
        for n, panel in enumerate(used):
            term = sums[t][n * rank : (n + 1) * rank]
            total = total + jnp.where(mine == step_of(groups[panel], high), term, 0.0)
        out[:, pl.ds(t * count, count)] = total


def score(plan, groups, kept, columns, row_steps, tokens_of, panels, prior=None):
    count, depth = tokens_of[0].shape
    rank = panels[0].shape[0]
    chunks = 4
    prior = [] if prior is None else [prior]
    vmem = pl.BlockSpec(memory_space=pltpu.VMEM)
    outs = [(rank, len(plan) * count), (len(kept) * rank, columns)]
    arrays = list(row_steps) + prior + list(tokens_of) + list(panels)
    need = 4 * len(plan) * count * (rank * len(panels) + depth) + 4 * len(panels) * rank * (depth + columns)
    return pl.pallas_call(
        functools.partial(
            score_kernel, plan, groups, kept, chunks, bool(prior), lax.axis_size("rep")
        ),
        out_shape=[
            jax.ShapeDtypeStruct(shape, panels[0].dtype if n else jnp.float32)
            for n, shape in enumerate(outs)
        ],
        in_specs=[vmem] * len(arrays),
        out_specs=[vmem] * len(outs),
        compiler_params=pltpu.CompilerParams(vmem_limit_bytes=need + (2 << 20)),
        cost_estimate=pl.CostEstimate(flops=0, bytes_accessed=0, transcendentals=0),
    )(*arrays)


def base_kernel(chunks, tokens_ref, weight_ref, *refs):
    outs, (held_tokens, held_weight, sems) = refs[:-3], refs[-3:]
    cores, half = len(outs), lax.axis_index("tp")
    columns = outs[0].shape[1]
    height = tokens_ref.shape[1] // chunks
    copies = []
    for c in range(chunks):
        rows = pl.ds(c * height, height)
        pairs = [(tokens_ref.at[:, rows], held_tokens.at[:, rows])]
        for shift in range(cores):
            left = pl.multiple_of(lax.rem(half + shift, cores) * columns, 128)
            pairs.append((weight_ref.at[rows, pl.ds(left, columns)], held_weight.at[shift, rows, :]))
        copies.append([])
        for n, (source, target) in enumerate(pairs):
            copies[-1].append(pltpu.make_async_copy(source, target, sems.at[c, n]))
            copies[-1][-1].start()
    for c in range(chunks):
        for copy in copies[c]:
            copy.wait()
        rows = pl.ds(c * height, height)
        for shift, out in enumerate(outs):
            product = jnp.dot(
                held_tokens[:, rows], held_weight[shift, rows, :], preferred_element_type=jnp.float32
            )
            if c == 0:
                out[...] = product
            else:
                out[...] += product


def base_terms(tokens, weight, cores):
    count, depth = tokens.shape
    columns = weight.shape[1] // cores
    chunks = 4
    return list(
        pl.pallas_call(
            functools.partial(base_kernel, chunks),
            out_shape=[jax.ShapeDtypeStruct((count, columns), jnp.float32)] * cores,
            in_specs=[pl.BlockSpec(memory_space=pl.ANY)] * 2,
            out_specs=[pl.BlockSpec(memory_space=pltpu.VMEM)] * cores,
            scratch_shapes=[
                pltpu.VMEM((count, depth), tokens.dtype),
                pltpu.VMEM((cores, depth, columns), weight.dtype),
                pltpu.SemaphoreType.DMA((chunks, 1 + cores)),
            ],
            compiler_params=pltpu.CompilerParams(vmem_limit_bytes=20 << 20),
            cost_estimate=pl.CostEstimate(flops=0, bytes_accessed=0, transcendentals=0),
        )(tokens, weight)
    )


def end_kernel(pieces, added, bases, replicas, row_steps, *refs):
    scores, base, refs = refs[:added], refs[added : added + bases], refs[added + bases :]
    arrays, (out, held, sems) = refs[:-3], refs[-3:]
    count, columns = out.shape
    rank = scores[0].shape[0]
    copies = []
    for n, (at, row, _) in enumerate(pieces):
        source = arrays[at].at[pl.ds(row, rank), pl.ds(arrays[at].shape[1] - columns, columns)]
        copies.append(pltpu.make_async_copy(source, held.at[pl.ds(n * rank, rank)], sems.at[n]))
        copies[-1].start()
    shrink = scores[0][:, pl.ds(0, count)]
    for x in scores[1:]:
        shrink = shrink + x[:, pl.ds(0, count)]
    shrink = adapter_scale * shrink
    high = shrink.astype(jnp.bfloat16).astype(jnp.float32)
    place = upper(replicas)
    masks = [row_steps[pl.ds(0, 1), :] == step_of(group, place) for _, _, group in pieces]
    total = base[0][...]
    for x in base[1:]:
        total = total + x[...]
    for copy in copies:
        copy.wait()
    for term in (high, shrink - high):
        wide = jnp.concatenate([jnp.where(mask, term, 0.0) for mask in masks], axis=0)
        total = total + lax.dot_general(
            wide.astype(jnp.bfloat16),
            held[...],
            (((0,), (0,)), ((), ())),
            preferred_element_type=jnp.float32,
        )
    out[...] = total.astype(out.dtype)


def end(pieces, row_steps, scores, base, arrays, kind, cost):
    count, columns = base[0].shape
    rank = scores[0].shape[0]
    vmem = pl.BlockSpec(memory_space=pltpu.VMEM)
    return pl.pallas_call(
        functools.partial(end_kernel, pieces, len(scores), len(base), lax.axis_size("rep")),
        out_shape=jax.ShapeDtypeStruct((count, columns), kind),
        in_specs=[vmem] * (1 + len(scores) + len(base))
        + [pl.BlockSpec(memory_space=pl.ANY)] * len(arrays),
        out_specs=vmem,
        scratch_shapes=[
            pltpu.VMEM((len(pieces) * rank, columns), jnp.bfloat16),
            pltpu.SemaphoreType.DMA((len(pieces),)),
        ],
        compiler_params=pltpu.CompilerParams(vmem_limit_bytes=16 << 20),
        cost_estimate=pl.CostEstimate(flops=0, bytes_accessed=cost, transcendentals=0),
    )(row_steps, *scores, *base, *arrays)


def on_device(tokens, base_weight, shrink_panels, expand_panels, adapter_home, fetch_list, seg_len):
    replicas, parts, cores = lax.axis_size("rep"), lax.axis_size("parts"), lax.axis_size("tp")
    tok_count = tokens.shape[0]
    columns = expand_panels.shape[2] // cores
    panels = jnp.swapaxes(shrink_panels, 1, 2)
    rank = panels.shape[1]
    tie = lax.optimization_barrier

    half = replicas // 2
    far = [(tuple(range(step, step + parts)), True) for step in range(half, replicas, parts)][::-1]
    size = half // parts - 1
    near = [(tuple(parts + p * size + g for p in range(parts)), False) for g in range(size)]
    near.append((tuple(reversed(range(parts))), False))

    def hop(x, group):
        steps, moves = group
        pairs = []
        for p in range(parts):
            for i in range(replicas):
                step = steps[(p + (moves and i >= half)) % parts]
                pairs.append((p * replicas + (i ^ step), p * replicas + i))
        return lax.ppermute(x, ("parts", "rep"), pairs)

    def shift_parts(x, shift):
        return lax.ppermute(x, "parts", [(i, (i + shift) % parts) for i in range(parts)])

    def shift_cores(x, shift):
        return lax.ppermute(x, "tp", [(i, (i + shift) % cores) for i in range(cores)])

    tables = (adapter_home, fetch_list, panels, expand_panels)
    groups = far + near
    send = pack(groups, columns, *tables)
    tokens, send = tie((tokens, send))
    recv = [hop(x, group) for x, group in zip(send, groups)]
    tokens_of = [tokens] + [shift_parts(tokens, shift) for shift in range(1, parts)]
    base = base_terms(tokens, base_weight, cores)
    base, recv[: len(far) - 1] = tie((base, recv[: len(far) - 1]))
    base = base[:1] + [shift_cores(x, shift + 1) for shift, x in enumerate(base[1:])]
    row_steps = steps_of_rows(tok_count, panels.shape[0], adapter_home, fetch_list, seg_len)
    steps_of = [row_steps] + [shift_parts(row_steps, shift) for shift in range(1, parts)]
    early, early_groups = recv[len(far) :] + recv[: len(far) - 1], near + far[:-1]
    last, last_group = recv[len(far) - 1], far[-1]

    count = len(early)
    first, sent = score(
        [tuple(range(count))],
        early_groups,
        tuple(range(count)),
        columns,
        steps_of[:1],
        [tokens],
        early,
    )
    passed = [shift_parts(sent, shift) for shift in range(1, parts)]
    base, first, passed, tokens_of[1:], last = tie((base, first, passed, tokens_of[1:], last))
    scores, sent = score(
        [(0,)] + [tuple(range(count + 1))] * (parts - 1),
        [last_group] + early_groups,
        (0,),
        columns,
        steps_of,
        tokens_of,
        [last] + early,
        first,
    )
    last_passed = [shift_parts(sent, shift) for shift in range(1, parts)]
    halves = [scores] + [shift_cores(scores, shift) for shift in range(1, cores)]
    whole = halves[0]
    for x in halves[1:]:
        whole = whole + x
    came = [
        shift_parts(whole[:, shift * tok_count : (shift + 1) * tok_count], -shift)
        for shift in range(1, parts)
    ]
    pieces = [(n, 0, group) for n, group in enumerate(early_groups + [last_group])]
    result = end(pieces, row_steps, halves, base, early + [last], jnp.float32, 1 << 24)
    pieces = []
    for shift in range(1, parts):
        at = shift - 1
        pieces += [(at, n * rank, turned(group, shift)) for n, group in enumerate(early_groups)]
        pieces.append((at + parts - 1, 0, turned(last_group, shift)))
    return end(pieces, row_steps, came, [result], passed + last_passed, jnp.bfloat16, 0)


def solution(mesh):
    return jax.shard_map(
        on_device,
        mesh=mesh,
        in_specs=(
            P(("parts", "rep"), "tp"),
            P("tp", None),
            P("rep", "tp", None),
            P("rep", None, None),
            P(),
            P(),
            P(("parts", "rep"), None),
        ),
        out_specs=P(("parts", "rep"), "tp"),
        check_vma=False,
    )
```

```python
import functools
import jax
import jax.numpy as jnp
from jax import lax
from jax.experimental import pallas as pl
from jax.experimental.pallas import tpu as pltpu
from jax.sharding import PartitionSpec as P

adapter_scale = 2.0


def upper(replicas):
    return (lax.axis_index("rep") >= replicas // 2).astype(jnp.int32)


def step_of(group, high):
    steps, moves = group
    part = lax.axis_index("parts")
    if moves:
        part = lax.rem(part + high, jnp.int32(len(steps)))
    chosen = jnp.int32(steps[0])
    for p, step in enumerate(steps):
        chosen = jnp.where(part == p, step, chosen)
    return chosen


def turned(group, shift):
    steps, moves = group
    return (tuple(steps[(p - shift) % len(steps)] for p in range(len(steps))), moves)


def slot_for(peer, me, per_home, home_ref, fetch_ref):
    first = me * per_home

    def look(j, slot):
        local = home_ref[fetch_ref[peer, j]] - first
        return jnp.where((local >= 0) & (local < per_home), local, slot)

    listed = fetch_ref.shape[1]
    return lax.fori_loop(0, listed, look, jnp.int32(0), unroll=listed <= 8)


def steps_kernel(per_home, home_ref, fetch_ref, lengths_ref, out):
    me = lax.axis_index("rep")
    rows = lax.broadcasted_iota(jnp.int32, out.shape, 1)
    result = jnp.zeros(out.shape, jnp.int32)
    start = jnp.int32(0)
    for j in range(fetch_ref.shape[1]):
        step = lax.div(home_ref[fetch_ref[me, j]], jnp.int32(per_home)) ^ me
        result = jnp.where(rows >= start, step, result)
        start = start + lengths_ref[0, j]
    out[...] = result


def steps_of_rows(count, per_home, adapter_home, fetch_list, seg_len):
    return pl.pallas_call(
        functools.partial(steps_kernel, per_home),
        out_shape=jax.ShapeDtypeStruct((8, count), jnp.int32),
        in_specs=[pl.BlockSpec(memory_space=pltpu.SMEM)] * 3,
        out_specs=pl.BlockSpec(memory_space=pltpu.VMEM),
        compiler_params=pltpu.CompilerParams(vmem_limit_bytes=2 << 20),
        cost_estimate=pl.CostEstimate(flops=0, bytes_accessed=0, transcendentals=0),
    )(adapter_home, fetch_list, seg_len)


def pack_kernel(groups, home_ref, fetch_ref, shrink_ref, expand_ref, *refs):
    outs, (held, in_sems, out_sems) = refs[:-3], refs[-3:]
    me = lax.axis_index("rep")
    other = 1 - upper(fetch_ref.shape[0])
    per_home, _, depth = shrink_ref.shape
    columns = expand_ref.shape[2] // lax.axis_size("tp")
    left = pl.multiple_of(lax.axis_index("tp") * columns, 128)
    cuts = in_sems.shape[1] - 1
    width = depth // cuts
    arriving = []
    for at, group in enumerate(groups):
        slot = slot_for(me ^ step_of(group, other), me, per_home, home_ref, fetch_ref)
        pieces = [(shrink_ref.at[slot, :, pl.ds(n * width, width)], n * width, width) for n in range(cuts)]
        pieces.append((expand_ref.at[slot, :, pl.ds(left, columns)], depth, columns))
        for n, (source, start, size) in enumerate(pieces):
            target = held.at[at, :, pl.ds(start, size)]
            copy = pltpu.make_async_copy(source, target, in_sems.at[at, n])
            copy.start()
            leave = pltpu.make_async_copy(target, outs[at].at[:, pl.ds(start, size)], out_sems.at[at, n])
            arriving.append((copy, leave))
    for copy, leave in arriving:
        copy.wait()
        leave.start()
    for _, leave in arriving:
        leave.wait()


def pack(groups, columns, adapter_home, fetch_list, panels, expand_panels):
    rank, depth = panels.shape[1:]
    shape = (rank, depth + columns)
    cuts = 4
    return list(
        pl.pallas_call(
            functools.partial(pack_kernel, groups),
            out_shape=[jax.ShapeDtypeStruct(shape, panels.dtype)] * len(groups),
            in_specs=[pl.BlockSpec(memory_space=pltpu.SMEM)] * 2 + [pl.BlockSpec(memory_space=pl.ANY)] * 2,
            out_specs=[pl.BlockSpec(memory_space=pl.ANY)] * len(groups),
            scratch_shapes=[pltpu.VMEM((len(groups),) + shape, panels.dtype)]
            + [pltpu.SemaphoreType.DMA((len(groups), cuts + 1))] * 2,
            compiler_params=pltpu.CompilerParams(vmem_limit_bytes=56 << 20),
            cost_estimate=pl.CostEstimate(flops=0, bytes_accessed=0, transcendentals=0),
        )(adapter_home, fetch_list, panels, expand_panels)
    )


def score_kernel(plan, groups, kept, chunks, has_prior, replicas, *refs):
    sets, many = len(plan), len(groups)
    row_steps, refs = refs[:sets], refs[sets:]
    prior, refs = (refs[0], refs[1:]) if has_prior else (None, refs)
    tokens, panels = refs[:sets], refs[sets : sets + many]
    out, out_expand = refs[sets + many :]
    rank, (count, depth) = out.shape[0], tokens[0].shape
    for i, n in enumerate(kept):
        out_expand[pl.ds(i * rank, rank), :] = panels[n][:, pl.ds(depth, out_expand.shape[1])]
    high = upper(replicas)
    width = depth // chunks
    sums = [None] * sets
    for c in range(chunks):
        cols = pl.ds(c * width, width)
        for t, used in enumerate(plan):
            product = lax.dot_general(
                jnp.concatenate([panels[n][:, cols] for n in used], axis=0),
                tokens[t][:, cols],
                (((1,), (1,)), ((), ())),
                preferred_element_type=jnp.float32,
            )
            sums[t] = product if c == 0 else sums[t] + product
    for t, used in enumerate(plan):
        mine = row_steps[t][pl.ds(0, 1), :]
        total = prior[...] if has_prior and t == 0 else jnp.zeros((rank, count), jnp.float32)
        for n, panel in enumerate(used):
            term = sums[t][n * rank : (n + 1) * rank]
            total = total + jnp.where(mine == step_of(groups[panel], high), term, 0.0)
        out[:, pl.ds(t * count, count)] = total


def score(plan, groups, kept, columns, row_steps, tokens_of, panels, prior=None):
    count, depth = tokens_of[0].shape
    rank = panels[0].shape[0]
    chunks = 4
    prior = [] if prior is None else [prior]
    vmem = pl.BlockSpec(memory_space=pltpu.VMEM)
    outs = [(rank, len(plan) * count), (len(kept) * rank, columns)]
    arrays = list(row_steps) + prior + list(tokens_of) + list(panels)
    need = 4 * len(plan) * count * (rank * len(panels) + depth) + 4 * len(panels) * rank * (depth + columns)
    return pl.pallas_call(
        functools.partial(
            score_kernel, plan, groups, kept, chunks, bool(prior), lax.axis_size("rep")
        ),
        out_shape=[
            jax.ShapeDtypeStruct(shape, panels[0].dtype if n else jnp.float32)
            for n, shape in enumerate(outs)
        ],
        in_specs=[vmem] * len(arrays),
        out_specs=[vmem] * len(outs),
        compiler_params=pltpu.CompilerParams(vmem_limit_bytes=need + (2 << 20)),
        cost_estimate=pl.CostEstimate(flops=0, bytes_accessed=0, transcendentals=0),
    )(*arrays)


def base_kernel(chunks, tokens_ref, weight_ref, *refs):
    outs, (held_tokens, held_weight, sems) = refs[:-3], refs[-3:]
    cores, half = len(outs), lax.axis_index("tp")
    columns = outs[0].shape[1]
    height = tokens_ref.shape[1] // chunks
    copies = []
    for c in range(chunks):
        rows = pl.ds(c * height, height)
        pairs = [(tokens_ref.at[:, rows], held_tokens.at[:, rows])]
        for shift in range(cores):
            left = pl.multiple_of(lax.rem(half + shift, cores) * columns, 128)
            pairs.append((weight_ref.at[rows, pl.ds(left, columns)], held_weight.at[shift, rows, :]))
        copies.append([])
        for n, (source, target) in enumerate(pairs):
            copies[-1].append(pltpu.make_async_copy(source, target, sems.at[c, n]))
            copies[-1][-1].start()
    for c in range(chunks):
        for copy in copies[c]:
            copy.wait()
        rows = pl.ds(c * height, height)
        for shift, out in enumerate(outs):
            product = jnp.dot(
                held_tokens[:, rows], held_weight[shift, rows, :], preferred_element_type=jnp.float32
            )
            if c == 0:
                out[...] = product
            else:
                out[...] += product


def base_terms(tokens, weight, cores):
    count, depth = tokens.shape
    columns = weight.shape[1] // cores
    chunks = 4
    return list(
        pl.pallas_call(
            functools.partial(base_kernel, chunks),
            out_shape=[jax.ShapeDtypeStruct((count, columns), jnp.float32)] * cores,
            in_specs=[pl.BlockSpec(memory_space=pl.ANY)] * 2,
            out_specs=[pl.BlockSpec(memory_space=pltpu.VMEM)] * cores,
            scratch_shapes=[
                pltpu.VMEM((count, depth), tokens.dtype),
                pltpu.VMEM((cores, depth, columns), weight.dtype),
                pltpu.SemaphoreType.DMA((chunks, 1 + cores)),
            ],
            compiler_params=pltpu.CompilerParams(vmem_limit_bytes=20 << 20),
            cost_estimate=pl.CostEstimate(flops=0, bytes_accessed=0, transcendentals=0),
        )(tokens, weight)
    )


def end_kernel(pieces, added, bases, replicas, row_steps, *refs):
    scores, base, refs = refs[:added], refs[added : added + bases], refs[added + bases :]
    arrays, (out, held, sems) = refs[:-3], refs[-3:]
    count, columns = out.shape
    rank = scores[0].shape[0]
    copies = []
    for n, (at, row, _) in enumerate(pieces):
        source = arrays[at].at[pl.ds(row, rank), pl.ds(arrays[at].shape[1] - columns, columns)]
        copies.append(pltpu.make_async_copy(source, held.at[pl.ds(n * rank, rank)], sems.at[n]))
        copies[-1].start()
    shrink = scores[0][:, pl.ds(0, count)]
    for x in scores[1:]:
        shrink = shrink + x[:, pl.ds(0, count)]
    shrink = adapter_scale * shrink
    high = shrink.astype(jnp.bfloat16).astype(jnp.float32)
    place = upper(replicas)
    masks = [row_steps[pl.ds(0, 1), :] == step_of(group, place) for _, _, group in pieces]
    total = base[0][...]
    for x in base[1:]:
        total = total + x[...]
    for copy in copies:
        copy.wait()
    for term in (high, shrink - high):
        wide = jnp.concatenate([jnp.where(mask, term, 0.0) for mask in masks], axis=0)
        total = total + lax.dot_general(
            wide.astype(jnp.bfloat16),
            held[...],
            (((0,), (0,)), ((), ())),
            preferred_element_type=jnp.float32,
        )
    out[...] = total.astype(out.dtype)


def end(pieces, row_steps, scores, base, arrays, kind, cost):
    count, columns = base[0].shape
    rank = scores[0].shape[0]
    vmem = pl.BlockSpec(memory_space=pltpu.VMEM)
    return pl.pallas_call(
        functools.partial(end_kernel, pieces, len(scores), len(base), lax.axis_size("rep")),
        out_shape=jax.ShapeDtypeStruct((count, columns), kind),
        in_specs=[vmem] * (1 + len(scores) + len(base))
        + [pl.BlockSpec(memory_space=pl.ANY)] * len(arrays),
        out_specs=vmem,
        scratch_shapes=[
            pltpu.VMEM((len(pieces) * rank, columns), jnp.bfloat16),
            pltpu.SemaphoreType.DMA((len(pieces),)),
        ],
        compiler_params=pltpu.CompilerParams(vmem_limit_bytes=16 << 20),
        cost_estimate=pl.CostEstimate(flops=0, bytes_accessed=cost, transcendentals=0),
    )(row_steps, *scores, *base, *arrays)


def on_device(tokens, base_weight, shrink_panels, expand_panels, adapter_home, fetch_list, seg_len):
    replicas, parts, cores = lax.axis_size("rep"), lax.axis_size("parts"), lax.axis_size("tp")
    tok_count = tokens.shape[0]
    columns = expand_panels.shape[2] // cores
    panels = jnp.swapaxes(shrink_panels, 1, 2)
    rank = panels.shape[1]
    tie = lax.optimization_barrier

    half = replicas // 2
    far = [(tuple(range(step, step + parts)), True) for step in range(half, replicas, parts)]
    far[-1] = (far[-1][0][::-1], True)
    size = half // parts - 1
    near = [(tuple(parts + p * size + g for p in range(parts)), False) for g in range(size)]
    near.append((tuple(reversed(range(parts))), False))

    def hop(x, group):
        steps, moves = group
        pairs = []
        for p in range(parts):
            for i in range(replicas):
                step = steps[(p + (moves and i >= half)) % parts]
                pairs.append((p * replicas + (i ^ step), p * replicas + i))
        return lax.ppermute(x, ("parts", "rep"), pairs)

    def shift_parts(x, shift):
        return lax.ppermute(x, "parts", [(i, (i + shift) % parts) for i in range(parts)])

    def shift_cores(x, shift):
        return lax.ppermute(x, "tp", [(i, (i + shift) % cores) for i in range(cores)])

    tables = (adapter_home, fetch_list, panels, expand_panels)
    groups = far + near
    send = pack(groups, columns, *tables)
    tokens, send = tie((tokens, send))
    recv = [hop(x, group) for x, group in zip(send, groups)]
    tokens_of = [tokens] + [shift_parts(tokens, shift) for shift in range(1, parts)]
    base = base_terms(tokens, base_weight, cores)
    base, recv[: len(far) - 1] = tie((base, recv[: len(far) - 1]))
    base = base[:1] + [shift_cores(x, shift + 1) for shift, x in enumerate(base[1:])]
    row_steps = steps_of_rows(tok_count, panels.shape[0], adapter_home, fetch_list, seg_len)
    steps_of = [row_steps] + [shift_parts(row_steps, shift) for shift in range(1, parts)]
    early, early_groups = recv[len(far) :] + recv[: len(far) - 1], near + far[:-1]
    last, last_group = recv[len(far) - 1], far[-1]

    count = len(early)
    first, sent = score(
        [tuple(range(count))],
        early_groups,
        tuple(range(count)),
        columns,
        steps_of[:1],
        [tokens],
        early,
    )
    passed = [shift_parts(sent, shift) for shift in range(1, parts)]
    base, first, passed, tokens_of[1:], last = tie((base, first, passed, tokens_of[1:], last))
    scores, sent = score(
        [(0,)] + [tuple(range(count + 1))] * (parts - 1),
        [last_group] + early_groups,
        (0,),
        columns,
        steps_of,
        tokens_of,
        [last] + early,
        first,
    )
    last_passed = [shift_parts(sent, shift) for shift in range(1, parts)]
    halves = [scores] + [shift_cores(scores, shift) for shift in range(1, cores)]
    whole = halves[0]
    for x in halves[1:]:
        whole = whole + x
    came = [
        shift_parts(whole[:, shift * tok_count : (shift + 1) * tok_count], -shift)
        for shift in range(1, parts)
    ]
    pieces = [(n, 0, group) for n, group in enumerate(early_groups + [last_group])]
    result = end(pieces, row_steps, halves, base, early + [last], jnp.float32, 1 << 24)
    pieces = []
    for shift in range(1, parts):
        at = shift - 1
        pieces += [(at, n * rank, turned(group, shift)) for n, group in enumerate(early_groups)]
        pieces.append((at + parts - 1, 0, turned(last_group, shift)))
    return end(pieces, row_steps, came, [result], passed + last_passed, jnp.bfloat16, 0)


def solution(mesh):
    return jax.shard_map(
        on_device,
        mesh=mesh,
        in_specs=(
            P(("parts", "rep"), "tp"),
            P("tp", None),
            P("rep", "tp", None),
            P("rep", None, None),
            P(),
            P(),
            P(("parts", "rep"), None),
        ),
        out_specs=P(("parts", "rep"), "tp"),
        check_vma=False,
    )
```

```python
import functools
import jax
import jax.numpy as jnp
from jax import lax
from jax.experimental import pallas as pl
from jax.experimental.pallas import tpu as pltpu
from jax.sharding import PartitionSpec as P

adapter_scale = 2.0


def upper(replicas):
    return (lax.axis_index("rep") >= replicas // 2).astype(jnp.int32)


def step_of(group, high):
    steps, moves = group
    part = lax.axis_index("parts")
    if moves:
        part = lax.rem(part + high, jnp.int32(len(steps)))
    chosen = jnp.int32(steps[0])
    for p, step in enumerate(steps):
        chosen = jnp.where(part == p, step, chosen)
    return chosen


def turned(group, shift):
    steps, moves = group
    return (tuple(steps[(p - shift) % len(steps)] for p in range(len(steps))), moves)


def slot_for(peer, me, per_home, home_ref, fetch_ref):
    first = me * per_home

    def look(j, slot):
        local = home_ref[fetch_ref[peer, j]] - first
        return jnp.where((local >= 0) & (local < per_home), local, slot)

    listed = fetch_ref.shape[1]
    return lax.fori_loop(0, listed, look, jnp.int32(0), unroll=listed <= 8)


def steps_kernel(per_home, home_ref, fetch_ref, lengths_ref, out):
    me = lax.axis_index("rep")
    rows = lax.broadcasted_iota(jnp.int32, out.shape, 1)
    result = jnp.zeros(out.shape, jnp.int32)
    start = jnp.int32(0)
    for j in range(fetch_ref.shape[1]):
        step = lax.div(home_ref[fetch_ref[me, j]], jnp.int32(per_home)) ^ me
        result = jnp.where(rows >= start, step, result)
        start = start + lengths_ref[0, j]
    out[...] = result


def steps_of_rows(count, per_home, adapter_home, fetch_list, seg_len):
    return pl.pallas_call(
        functools.partial(steps_kernel, per_home),
        out_shape=jax.ShapeDtypeStruct((8, count), jnp.int32),
        in_specs=[pl.BlockSpec(memory_space=pltpu.SMEM)] * 3,
        out_specs=pl.BlockSpec(memory_space=pltpu.VMEM),
        compiler_params=pltpu.CompilerParams(vmem_limit_bytes=2 << 20),
        cost_estimate=pl.CostEstimate(flops=0, bytes_accessed=0, transcendentals=0),
    )(adapter_home, fetch_list, seg_len)


def pack_kernel(groups, home_ref, fetch_ref, shrink_ref, expand_ref, *refs):
    outs, (held, in_sems, out_sems) = refs[:-3], refs[-3:]
    me = lax.axis_index("rep")
    other = 1 - upper(fetch_ref.shape[0])
    per_home, _, depth = shrink_ref.shape
    columns = expand_ref.shape[2] // lax.axis_size("tp")
    left = pl.multiple_of(lax.axis_index("tp") * columns, 128)
    cuts = in_sems.shape[1] - 1
    width = depth // cuts
    arriving = []
    for at, group in enumerate(groups):
        slot = slot_for(me ^ step_of(group, other), me, per_home, home_ref, fetch_ref)
        pieces = [(shrink_ref.at[slot, :, pl.ds(n * width, width)], n * width, width) for n in range(cuts)]
        pieces.append((expand_ref.at[slot, :, pl.ds(left, columns)], depth, columns))
        for n, (source, start, size) in enumerate(pieces):
            target = held.at[at, :, pl.ds(start, size)]
            copy = pltpu.make_async_copy(source, target, in_sems.at[at, n])
            copy.start()
            leave = pltpu.make_async_copy(target, outs[at].at[:, pl.ds(start, size)], out_sems.at[at, n])
            arriving.append((copy, leave))
    for copy, leave in arriving:
        copy.wait()
        leave.start()
    for _, leave in arriving:
        leave.wait()


def pack(groups, columns, adapter_home, fetch_list, panels, expand_panels):
    rank, depth = panels.shape[1:]
    shape = (rank, depth + columns)
    cuts = 2
    return list(
        pl.pallas_call(
            functools.partial(pack_kernel, groups),
            out_shape=[jax.ShapeDtypeStruct(shape, panels.dtype)] * len(groups),
            in_specs=[pl.BlockSpec(memory_space=pltpu.SMEM)] * 2 + [pl.BlockSpec(memory_space=pl.ANY)] * 2,
            out_specs=[pl.BlockSpec(memory_space=pl.ANY)] * len(groups),
            scratch_shapes=[pltpu.VMEM((len(groups),) + shape, panels.dtype)]
            + [pltpu.SemaphoreType.DMA((len(groups), cuts + 1))] * 2,
            compiler_params=pltpu.CompilerParams(vmem_limit_bytes=56 << 20),
            cost_estimate=pl.CostEstimate(flops=0, bytes_accessed=0, transcendentals=0),
        )(adapter_home, fetch_list, panels, expand_panels)
    )


def score_kernel(plan, groups, kept, chunks, has_prior, replicas, *refs):
    sets, many = len(plan), len(groups)
    row_steps, refs = refs[:sets], refs[sets:]
    prior, refs = (refs[0], refs[1:]) if has_prior else (None, refs)
    tokens, panels = refs[:sets], refs[sets : sets + many]
    out, out_expand = refs[sets + many :]
    rank, (count, depth) = out.shape[0], tokens[0].shape
    for i, n in enumerate(kept):
        out_expand[pl.ds(i * rank, rank), :] = panels[n][:, pl.ds(depth, out_expand.shape[1])]
    high = upper(replicas)
    width = depth // chunks
    sums = [None] * sets
    for c in range(chunks):
        cols = pl.ds(c * width, width)
        for t, used in enumerate(plan):
            product = lax.dot_general(
                jnp.concatenate([panels[n][:, cols] for n in used], axis=0),
                tokens[t][:, cols],
                (((1,), (1,)), ((), ())),
                preferred_element_type=jnp.float32,
            )
            sums[t] = product if c == 0 else sums[t] + product
    for t, used in enumerate(plan):
        mine = row_steps[t][pl.ds(0, 1), :]
        total = prior[...] if has_prior and t == 0 else jnp.zeros((rank, count), jnp.float32)
        for n, panel in enumerate(used):
            term = sums[t][n * rank : (n + 1) * rank]
            total = total + jnp.where(mine == step_of(groups[panel], high), term, 0.0)
        out[:, pl.ds(t * count, count)] = total


def score(plan, groups, kept, columns, row_steps, tokens_of, panels, prior=None):
    count, depth = tokens_of[0].shape
    rank = panels[0].shape[0]
    chunks = 4
    prior = [] if prior is None else [prior]
    vmem = pl.BlockSpec(memory_space=pltpu.VMEM)
    outs = [(rank, len(plan) * count), (len(kept) * rank, columns)]
    arrays = list(row_steps) + prior + list(tokens_of) + list(panels)
    need = 4 * len(plan) * count * (rank * len(panels) + depth) + 4 * len(panels) * rank * (depth + columns)
    return pl.pallas_call(
        functools.partial(
            score_kernel, plan, groups, kept, chunks, bool(prior), lax.axis_size("rep")
        ),
        out_shape=[
            jax.ShapeDtypeStruct(shape, panels[0].dtype if n else jnp.float32)
            for n, shape in enumerate(outs)
        ],
        in_specs=[vmem] * len(arrays),
        out_specs=[vmem] * len(outs),
        compiler_params=pltpu.CompilerParams(vmem_limit_bytes=need + (2 << 20)),
        cost_estimate=pl.CostEstimate(flops=0, bytes_accessed=0, transcendentals=0),
    )(*arrays)


def base_kernel(chunks, tokens_ref, weight_ref, *refs):
    outs, (held_tokens, held_weight, sems) = refs[:-3], refs[-3:]
    cores, half = len(outs), lax.axis_index("tp")
    columns = outs[0].shape[1]
    height = tokens_ref.shape[1] // chunks
    copies = []
    for c in range(chunks):
        rows = pl.ds(c * height, height)
        pairs = [(tokens_ref.at[:, rows], held_tokens.at[:, rows])]
        for shift in range(cores):
            left = pl.multiple_of(lax.rem(half + shift, cores) * columns, 128)
            pairs.append((weight_ref.at[rows, pl.ds(left, columns)], held_weight.at[shift, rows, :]))
        copies.append([])
        for n, (source, target) in enumerate(pairs):
            copies[-1].append(pltpu.make_async_copy(source, target, sems.at[c, n]))
            copies[-1][-1].start()
    for c in range(chunks):
        for copy in copies[c]:
            copy.wait()
        rows = pl.ds(c * height, height)
        for shift, out in enumerate(outs):
            product = jnp.dot(
                held_tokens[:, rows], held_weight[shift, rows, :], preferred_element_type=jnp.float32
            )
            if c == 0:
                out[...] = product
            else:
                out[...] += product


def base_terms(tokens, weight, cores):
    count, depth = tokens.shape
    columns = weight.shape[1] // cores
    chunks = 4
    return list(
        pl.pallas_call(
            functools.partial(base_kernel, chunks),
            out_shape=[jax.ShapeDtypeStruct((count, columns), jnp.float32)] * cores,
            in_specs=[pl.BlockSpec(memory_space=pl.ANY)] * 2,
            out_specs=[pl.BlockSpec(memory_space=pltpu.VMEM)] * cores,
            scratch_shapes=[
                pltpu.VMEM((count, depth), tokens.dtype),
                pltpu.VMEM((cores, depth, columns), weight.dtype),
                pltpu.SemaphoreType.DMA((chunks, 1 + cores)),
            ],
            compiler_params=pltpu.CompilerParams(vmem_limit_bytes=20 << 20),
            cost_estimate=pl.CostEstimate(flops=0, bytes_accessed=0, transcendentals=0),
        )(tokens, weight)
    )


def end_kernel(pieces, added, bases, replicas, row_steps, *refs):
    scores, base, refs = refs[:added], refs[added : added + bases], refs[added + bases :]
    arrays, (out, held, sems) = refs[:-3], refs[-3:]
    count, columns = out.shape
    rank = scores[0].shape[0]
    copies = []
    for n, (at, row, _) in enumerate(pieces):
        source = arrays[at].at[pl.ds(row, rank), pl.ds(arrays[at].shape[1] - columns, columns)]
        copies.append(pltpu.make_async_copy(source, held.at[pl.ds(n * rank, rank)], sems.at[n]))
        copies[-1].start()
    shrink = scores[0][:, pl.ds(0, count)]
    for x in scores[1:]:
        shrink = shrink + x[:, pl.ds(0, count)]
    shrink = adapter_scale * shrink
    high = shrink.astype(jnp.bfloat16).astype(jnp.float32)
    place = upper(replicas)
    masks = [row_steps[pl.ds(0, 1), :] == step_of(group, place) for _, _, group in pieces]
    total = base[0][...]
    for x in base[1:]:
        total = total + x[...]
    for copy in copies:
        copy.wait()
    for term in (high, shrink - high):
        wide = jnp.concatenate([jnp.where(mask, term, 0.0) for mask in masks], axis=0)
        total = total + lax.dot_general(
            wide.astype(jnp.bfloat16),
            held[...],
            (((0,), (0,)), ((), ())),
            preferred_element_type=jnp.float32,
        )
    out[...] = total.astype(out.dtype)


def end(pieces, row_steps, scores, base, arrays, kind, cost):
    count, columns = base[0].shape
    rank = scores[0].shape[0]
    vmem = pl.BlockSpec(memory_space=pltpu.VMEM)
    return pl.pallas_call(
        functools.partial(end_kernel, pieces, len(scores), len(base), lax.axis_size("rep")),
        out_shape=jax.ShapeDtypeStruct((count, columns), kind),
        in_specs=[vmem] * (1 + len(scores) + len(base))
        + [pl.BlockSpec(memory_space=pl.ANY)] * len(arrays),
        out_specs=vmem,
        scratch_shapes=[
            pltpu.VMEM((len(pieces) * rank, columns), jnp.bfloat16),
            pltpu.SemaphoreType.DMA((len(pieces),)),
        ],
        compiler_params=pltpu.CompilerParams(vmem_limit_bytes=16 << 20),
        cost_estimate=pl.CostEstimate(flops=0, bytes_accessed=cost, transcendentals=0),
    )(row_steps, *scores, *base, *arrays)


def on_device(tokens, base_weight, shrink_panels, expand_panels, adapter_home, fetch_list, seg_len):
    replicas, parts, cores = lax.axis_size("rep"), lax.axis_size("parts"), lax.axis_size("tp")
    tok_count = tokens.shape[0]
    columns = expand_panels.shape[2] // cores
    panels = jnp.swapaxes(shrink_panels, 1, 2)
    rank = panels.shape[1]
    tie = lax.optimization_barrier

    half = replicas // 2
    far = [(tuple(range(step, step + parts)), True) for step in range(half, replicas, parts)]
    size = half // parts - 1
    near = [(tuple(parts + p * size + g for p in reversed(range(parts))), False) for g in range(size)]
    near.append((tuple(range(parts)), False))

    def hop(x, group):
        steps, moves = group
        pairs = []
        for p in range(parts):
            for i in range(replicas):
                step = steps[(p + (moves and i >= half)) % parts]
                pairs.append((p * replicas + (i ^ step), p * replicas + i))
        return lax.ppermute(x, ("parts", "rep"), pairs)

    def shift_parts(x, shift):
        return lax.ppermute(x, "parts", [(i, (i + shift) % parts) for i in range(parts)])

    def shift_cores(x, shift):
        return lax.ppermute(x, "tp", [(i, (i + shift) % cores) for i in range(cores)])

    tables = (adapter_home, fetch_list, panels, expand_panels)
    groups = far + near
    send = pack(groups, columns, *tables)
    tokens, send = tie((tokens, send))
    recv = [hop(x, group) for x, group in zip(send, groups)]
    tokens_of = [tokens] + [shift_parts(tokens, shift) for shift in range(1, parts)]
    base = base_terms(tokens, base_weight, cores)
    base, recv[: len(far) - 1] = tie((base, recv[: len(far) - 1]))
    base = base[:1] + [shift_cores(x, shift + 1) for shift, x in enumerate(base[1:])]
    row_steps = steps_of_rows(tok_count, panels.shape[0], adapter_home, fetch_list, seg_len)
    steps_of = [row_steps] + [shift_parts(row_steps, shift) for shift in range(1, parts)]
    early, early_groups = recv[len(far) :] + recv[: len(far) - 1], near + far[:-1]
    last, last_group = recv[len(far) - 1], far[-1]

    count = len(early)
    first, sent = score(
        [tuple(range(count))],
        early_groups,
        tuple(range(count)),
        columns,
        steps_of[:1],
        [tokens],
        early,
    )
    passed = [shift_parts(sent, shift) for shift in range(1, parts)]
    base, first, passed, tokens_of[1:], last = tie((base, first, passed, tokens_of[1:], last))
    scores, sent = score(
        [(0,)] + [tuple(range(count + 1))] * (parts - 1),
        [last_group] + early_groups,
        (0,),
        columns,
        steps_of,
        tokens_of,
        [last] + early,
        first,
    )
    last_passed = [shift_parts(sent, shift) for shift in range(1, parts)]
    halves = [scores] + [shift_cores(scores, shift) for shift in range(1, cores)]
    whole = halves[0]
    for x in halves[1:]:
        whole = whole + x
    came = [
        shift_parts(whole[:, shift * tok_count : (shift + 1) * tok_count], -shift)
        for shift in range(1, parts)
    ]
    pieces = [(n, 0, group) for n, group in enumerate(early_groups + [last_group])]
    result = end(pieces, row_steps, halves, base, early + [last], jnp.float32, 1 << 24)
    pieces = []
    for shift in range(1, parts):
        at = shift - 1
        pieces += [(at, n * rank, turned(group, shift)) for n, group in enumerate(early_groups)]
        pieces.append((at + parts - 1, 0, turned(last_group, shift)))
    return end(pieces, row_steps, came, [result], passed + last_passed, jnp.bfloat16, 0)


def solution(mesh):
    return jax.shard_map(
        on_device,
        mesh=mesh,
        in_specs=(
            P(("parts", "rep"), "tp"),
            P("tp", None),
            P("rep", "tp", None),
            P("rep", None, None),
            P(),
            P(),
            P(("parts", "rep"), None),
        ),
        out_specs=P(("parts", "rep"), "tp"),
        check_vma=False,
    )
```

```python
import functools
import jax
import jax.numpy as jnp
from jax import lax
from jax.experimental import pallas as pl
from jax.experimental.pallas import tpu as pltpu
from jax.sharding import PartitionSpec as P

adapter_scale = 2.0


def upper(replicas):
    return (lax.axis_index("rep") >= replicas // 2).astype(jnp.int32)


def step_of(group, high):
    steps, moves = group
    part = lax.axis_index("parts")
    if moves:
        part = lax.rem(part + high, jnp.int32(len(steps)))
    chosen = jnp.int32(steps[0])
    for p, step in enumerate(steps):
        chosen = jnp.where(part == p, step, chosen)
    return chosen


def turned(group, shift):
    steps, moves = group
    return (tuple(steps[(p - shift) % len(steps)] for p in range(len(steps))), moves)


def slot_for(peer, me, per_home, home_ref, fetch_ref):
    first = me * per_home

    def look(j, slot):
        local = home_ref[fetch_ref[peer, j]] - first
        return jnp.where((local >= 0) & (local < per_home), local, slot)

    listed = fetch_ref.shape[1]
    return lax.fori_loop(0, listed, look, jnp.int32(0), unroll=listed <= 8)


def steps_kernel(per_home, home_ref, fetch_ref, lengths_ref, out):
    me = lax.axis_index("rep")
    rows = lax.broadcasted_iota(jnp.int32, out.shape, 1)
    result = jnp.zeros(out.shape, jnp.int32)
    start = jnp.int32(0)
    for j in range(fetch_ref.shape[1]):
        step = lax.div(home_ref[fetch_ref[me, j]], jnp.int32(per_home)) ^ me
        result = jnp.where(rows >= start, step, result)
        start = start + lengths_ref[0, j]
    out[...] = result


def steps_of_rows(count, per_home, adapter_home, fetch_list, seg_len):
    return pl.pallas_call(
        functools.partial(steps_kernel, per_home),
        out_shape=jax.ShapeDtypeStruct((8, count), jnp.int32),
        in_specs=[pl.BlockSpec(memory_space=pltpu.SMEM)] * 3,
        out_specs=pl.BlockSpec(memory_space=pltpu.VMEM),
        compiler_params=pltpu.CompilerParams(vmem_limit_bytes=2 << 20),
        cost_estimate=pl.CostEstimate(flops=0, bytes_accessed=0, transcendentals=0),
    )(adapter_home, fetch_list, seg_len)


def pack_kernel(groups, home_ref, fetch_ref, shrink_ref, expand_ref, *refs):
    outs, (held, in_sems, out_sems) = refs[:-3], refs[-3:]
    me = lax.axis_index("rep")
    other = 1 - upper(fetch_ref.shape[0])
    per_home, _, depth = shrink_ref.shape
    columns = expand_ref.shape[2] // lax.axis_size("tp")
    left = pl.multiple_of(lax.axis_index("tp") * columns, 128)
    cuts = in_sems.shape[1] - 1
    width = depth // cuts
    arriving = []
    for at, group in enumerate(groups):
        slot = slot_for(me ^ step_of(group, other), me, per_home, home_ref, fetch_ref)
        pieces = [(shrink_ref.at[slot, :, pl.ds(n * width, width)], n * width, width) for n in range(cuts)]
        pieces.append((expand_ref.at[slot, :, pl.ds(left, columns)], depth, columns))
        for n, (source, start, size) in enumerate(pieces):
            target = held.at[at, :, pl.ds(start, size)]
            copy = pltpu.make_async_copy(source, target, in_sems.at[at, n])
            copy.start()
            leave = pltpu.make_async_copy(target, outs[at].at[:, pl.ds(start, size)], out_sems.at[at, n])
            arriving.append((copy, leave))
    for copy, leave in arriving:
        copy.wait()
        leave.start()
    for _, leave in arriving:
        leave.wait()


def pack(groups, columns, adapter_home, fetch_list, panels, expand_panels):
    rank, depth = panels.shape[1:]
    shape = (rank, depth + columns)
    cuts = 2
    return list(
        pl.pallas_call(
            functools.partial(pack_kernel, groups),
            out_shape=[jax.ShapeDtypeStruct(shape, panels.dtype)] * len(groups),
            in_specs=[pl.BlockSpec(memory_space=pltpu.SMEM)] * 2 + [pl.BlockSpec(memory_space=pl.ANY)] * 2,
            out_specs=[pl.BlockSpec(memory_space=pl.ANY)] * len(groups),
            scratch_shapes=[pltpu.VMEM((len(groups),) + shape, panels.dtype)]
            + [pltpu.SemaphoreType.DMA((len(groups), cuts + 1))] * 2,
            compiler_params=pltpu.CompilerParams(vmem_limit_bytes=56 << 20),
            cost_estimate=pl.CostEstimate(flops=0, bytes_accessed=0, transcendentals=0),
        )(adapter_home, fetch_list, panels, expand_panels)
    )


def score_kernel(plan, groups, kept, chunks, has_prior, replicas, *refs):
    sets, many = len(plan), len(groups)
    row_steps, refs = refs[:sets], refs[sets:]
    prior, refs = (refs[0], refs[1:]) if has_prior else (None, refs)
    tokens, panels = refs[:sets], refs[sets : sets + many]
    out, out_expand = refs[sets + many :]
    rank, (count, depth) = out.shape[0], tokens[0].shape
    for i, n in enumerate(kept):
        out_expand[pl.ds(i * rank, rank), :] = panels[n][:, pl.ds(depth, out_expand.shape[1])]
    high = upper(replicas)
    width = depth // chunks
    sums = [None] * sets
    for c in range(chunks):
        cols = pl.ds(c * width, width)
        for t, used in enumerate(plan):
            product = lax.dot_general(
                jnp.concatenate([panels[n][:, cols] for n in used], axis=0),
                tokens[t][:, cols],
                (((1,), (1,)), ((), ())),
                preferred_element_type=jnp.float32,
            )
            sums[t] = product if c == 0 else sums[t] + product
    for t, used in enumerate(plan):
        mine = row_steps[t][pl.ds(0, 1), :]
        total = prior[...] if has_prior and t == 0 else jnp.zeros((rank, count), jnp.float32)
        for n, panel in enumerate(used):
            term = sums[t][n * rank : (n + 1) * rank]
            total = total + jnp.where(mine == step_of(groups[panel], high), term, 0.0)
        out[:, pl.ds(t * count, count)] = total


def score(plan, groups, kept, columns, row_steps, tokens_of, panels, prior=None):
    count, depth = tokens_of[0].shape
    rank = panels[0].shape[0]
    chunks = 4
    prior = [] if prior is None else [prior]
    vmem = pl.BlockSpec(memory_space=pltpu.VMEM)
    outs = [(rank, len(plan) * count), (len(kept) * rank, columns)]
    arrays = list(row_steps) + prior + list(tokens_of) + list(panels)
    need = 4 * len(plan) * count * (rank * len(panels) + depth) + 4 * len(panels) * rank * (depth + columns)
    return pl.pallas_call(
        functools.partial(
            score_kernel, plan, groups, kept, chunks, bool(prior), lax.axis_size("rep")
        ),
        out_shape=[
            jax.ShapeDtypeStruct(shape, panels[0].dtype if n else jnp.float32)
            for n, shape in enumerate(outs)
        ],
        in_specs=[vmem] * len(arrays),
        out_specs=[vmem] * len(outs),
        compiler_params=pltpu.CompilerParams(vmem_limit_bytes=need + (2 << 20)),
        cost_estimate=pl.CostEstimate(flops=0, bytes_accessed=0, transcendentals=0),
    )(*arrays)


def base_kernel(chunks, tokens_ref, weight_ref, *refs):
    outs, (held_tokens, held_weight, sems) = refs[:-3], refs[-3:]
    cores, half = len(outs), lax.axis_index("tp")
    columns = outs[0].shape[1]
    height = tokens_ref.shape[1] // chunks
    copies = []
    for c in range(chunks):
        rows = pl.ds(c * height, height)
        pairs = [(tokens_ref.at[:, rows], held_tokens.at[:, rows])]
        for shift in range(cores):
            left = pl.multiple_of(lax.rem(half + shift, cores) * columns, 128)
            pairs.append((weight_ref.at[rows, pl.ds(left, columns)], held_weight.at[shift, rows, :]))
        copies.append([])
        for n, (source, target) in enumerate(pairs):
            copies[-1].append(pltpu.make_async_copy(source, target, sems.at[c, n]))
            copies[-1][-1].start()
    for c in range(chunks):
        for copy in copies[c]:
            copy.wait()
        rows = pl.ds(c * height, height)
        for shift, out in enumerate(outs):
            product = jnp.dot(
                held_tokens[:, rows], held_weight[shift, rows, :], preferred_element_type=jnp.float32
            )
            if c == 0:
                out[...] = product
            else:
                out[...] += product


def base_terms(tokens, weight, cores):
    count, depth = tokens.shape
    columns = weight.shape[1] // cores
    chunks = 4
    return list(
        pl.pallas_call(
            functools.partial(base_kernel, chunks),
            out_shape=[jax.ShapeDtypeStruct((count, columns), jnp.float32)] * cores,
            in_specs=[pl.BlockSpec(memory_space=pl.ANY)] * 2,
            out_specs=[pl.BlockSpec(memory_space=pltpu.VMEM)] * cores,
            scratch_shapes=[
                pltpu.VMEM((count, depth), tokens.dtype),
                pltpu.VMEM((cores, depth, columns), weight.dtype),
                pltpu.SemaphoreType.DMA((chunks, 1 + cores)),
            ],
            compiler_params=pltpu.CompilerParams(vmem_limit_bytes=20 << 20),
            cost_estimate=pl.CostEstimate(flops=0, bytes_accessed=0, transcendentals=0),
        )(tokens, weight)
    )


def end_kernel(pieces, added, bases, replicas, row_steps, *refs):
    scores, base, refs = refs[:added], refs[added : added + bases], refs[added + bases :]
    arrays, (out, held, sems) = refs[:-3], refs[-3:]
    count, columns = out.shape
    rank = scores[0].shape[0]
    copies = []
    for n, (at, row, _) in enumerate(pieces):
        source = arrays[at].at[pl.ds(row, rank), pl.ds(arrays[at].shape[1] - columns, columns)]
        copies.append(pltpu.make_async_copy(source, held.at[pl.ds(n * rank, rank)], sems.at[n]))
        copies[-1].start()
    shrink = scores[0][:, pl.ds(0, count)]
    for x in scores[1:]:
        shrink = shrink + x[:, pl.ds(0, count)]
    shrink = adapter_scale * shrink
    high = shrink.astype(jnp.bfloat16).astype(jnp.float32)
    place = upper(replicas)
    masks = [row_steps[pl.ds(0, 1), :] == step_of(group, place) for _, _, group in pieces]
    total = base[0][...]
    for x in base[1:]:
        total = total + x[...]
    for copy in copies:
        copy.wait()
    for term in (high, shrink - high):
        wide = jnp.concatenate([jnp.where(mask, term, 0.0) for mask in masks], axis=0)
        total = total + lax.dot_general(
            wide.astype(jnp.bfloat16),
            held[...],
            (((0,), (0,)), ((), ())),
            preferred_element_type=jnp.float32,
        )
    out[...] = total.astype(out.dtype)


def end(pieces, row_steps, scores, base, arrays, kind, cost):
    count, columns = base[0].shape
    rank = scores[0].shape[0]
    vmem = pl.BlockSpec(memory_space=pltpu.VMEM)
    return pl.pallas_call(
        functools.partial(end_kernel, pieces, len(scores), len(base), lax.axis_size("rep")),
        out_shape=jax.ShapeDtypeStruct((count, columns), kind),
        in_specs=[vmem] * (1 + len(scores) + len(base))
        + [pl.BlockSpec(memory_space=pl.ANY)] * len(arrays),
        out_specs=vmem,
        scratch_shapes=[
            pltpu.VMEM((len(pieces) * rank, columns), jnp.bfloat16),
            pltpu.SemaphoreType.DMA((len(pieces),)),
        ],
        compiler_params=pltpu.CompilerParams(vmem_limit_bytes=16 << 20),
        cost_estimate=pl.CostEstimate(flops=0, bytes_accessed=cost, transcendentals=0),
    )(row_steps, *scores, *base, *arrays)


def on_device(tokens, base_weight, shrink_panels, expand_panels, adapter_home, fetch_list, seg_len):
    replicas, parts, cores = lax.axis_size("rep"), lax.axis_size("parts"), lax.axis_size("tp")
    tok_count = tokens.shape[0]
    columns = expand_panels.shape[2] // cores
    panels = jnp.swapaxes(shrink_panels, 1, 2)
    rank = panels.shape[1]
    tie = lax.optimization_barrier

    half = replicas // 2
    far = [(tuple(range(step, step + parts))[::-1], True) for step in range(half, replicas, parts)]
    size = half // parts - 1
    near = [(tuple(parts + p * size + g for p in reversed(range(parts))), False) for g in range(size)]
    near.append((tuple(range(parts)), False))

    def hop(x, group):
        steps, moves = group
        pairs = []
        for p in range(parts):
            for i in range(replicas):
                step = steps[(p + (moves and i >= half)) % parts]
                pairs.append((p * replicas + (i ^ step), p * replicas + i))
        return lax.ppermute(x, ("parts", "rep"), pairs)

    def shift_parts(x, shift):
        return lax.ppermute(x, "parts", [(i, (i + shift) % parts) for i in range(parts)])

    def shift_cores(x, shift):
        return lax.ppermute(x, "tp", [(i, (i + shift) % cores) for i in range(cores)])

    tables = (adapter_home, fetch_list, panels, expand_panels)
    groups = far + near
    send = pack(groups, columns, *tables)
    tokens, send = tie((tokens, send))
    recv = [hop(x, group) for x, group in zip(send, groups)]
    tokens_of = [tokens] + [shift_parts(tokens, shift) for shift in range(1, parts)]
    base = base_terms(tokens, base_weight, cores)
    base, recv[: len(far) - 1] = tie((base, recv[: len(far) - 1]))
    base = base[:1] + [shift_cores(x, shift + 1) for shift, x in enumerate(base[1:])]
    row_steps = steps_of_rows(tok_count, panels.shape[0], adapter_home, fetch_list, seg_len)
    steps_of = [row_steps] + [shift_parts(row_steps, shift) for shift in range(1, parts)]
    early, early_groups = recv[len(far) :] + recv[: len(far) - 1], near + far[:-1]
    last, last_group = recv[len(far) - 1], far[-1]

    count = len(early)
    first, sent = score(
        [tuple(range(count))],
        early_groups,
        tuple(range(count)),
        columns,
        steps_of[:1],
        [tokens],
        early,
    )
    passed = [shift_parts(sent, shift) for shift in range(1, parts)]
    base, first, passed, tokens_of[1:], last = tie((base, first, passed, tokens_of[1:], last))
    scores, sent = score(
        [(0,)] + [tuple(range(count + 1))] * (parts - 1),
        [last_group] + early_groups,
        (0,),
        columns,
        steps_of,
        tokens_of,
        [last] + early,
        first,
    )
    last_passed = [shift_parts(sent, shift) for shift in range(1, parts)]
    halves = [scores] + [shift_cores(scores, shift) for shift in range(1, cores)]
    whole = halves[0]
    for x in halves[1:]:
        whole = whole + x
    came = [
        shift_parts(whole[:, shift * tok_count : (shift + 1) * tok_count], -shift)
        for shift in range(1, parts)
    ]
    pieces = [(n, 0, group) for n, group in enumerate(early_groups + [last_group])]
    result = end(pieces, row_steps, halves, base, early + [last], jnp.float32, 1 << 24)
    pieces = []
    for shift in range(1, parts):
        at = shift - 1
        pieces += [(at, n * rank, turned(group, shift)) for n, group in enumerate(early_groups)]
        pieces.append((at + parts - 1, 0, turned(last_group, shift)))
    return end(pieces, row_steps, came, [result], passed + last_passed, jnp.bfloat16, 0)


def solution(mesh):
    return jax.shard_map(
        on_device,
        mesh=mesh,
        in_specs=(
            P(("parts", "rep"), "tp"),
            P("tp", None),
            P("rep", "tp", None),
            P("rep", None, None),
            P(),
            P(),
            P(("parts", "rep"), None),
        ),
        out_specs=P(("parts", "rep"), "tp"),
        check_vma=False,
    )
```

```python
import functools
import jax
import jax.numpy as jnp
from jax import lax
from jax.experimental import pallas as pl
from jax.experimental.pallas import tpu as pltpu
from jax.sharding import PartitionSpec as P

adapter_scale = 2.0


def upper(replicas):
    return (lax.axis_index("rep") >= replicas // 2).astype(jnp.int32)


def step_of(group, high):
    steps, moves = group
    part = lax.axis_index("parts")
    if moves:
        part = lax.rem(part + high, jnp.int32(len(steps)))
    chosen = jnp.int32(steps[0])
    for p, step in enumerate(steps):
        chosen = jnp.where(part == p, step, chosen)
    return chosen


def turned(group, shift):
    steps, moves = group
    return (tuple(steps[(p - shift) % len(steps)] for p in range(len(steps))), moves)


def slot_for(peer, me, per_home, home_ref, fetch_ref):
    first = me * per_home

    def look(j, slot):
        local = home_ref[fetch_ref[peer, j]] - first
        return jnp.where((local >= 0) & (local < per_home), local, slot)

    listed = fetch_ref.shape[1]
    return lax.fori_loop(0, listed, look, jnp.int32(0), unroll=listed <= 8)


def steps_kernel(per_home, home_ref, fetch_ref, lengths_ref, out):
    me = lax.axis_index("rep")
    rows = lax.broadcasted_iota(jnp.int32, out.shape, 1)
    result = jnp.zeros(out.shape, jnp.int32)
    start = jnp.int32(0)
    for j in range(fetch_ref.shape[1]):
        step = lax.div(home_ref[fetch_ref[me, j]], jnp.int32(per_home)) ^ me
        result = jnp.where(rows >= start, step, result)
        start = start + lengths_ref[0, j]
    out[...] = result


def steps_of_rows(count, per_home, adapter_home, fetch_list, seg_len):
    return pl.pallas_call(
        functools.partial(steps_kernel, per_home),
        out_shape=jax.ShapeDtypeStruct((8, count), jnp.int32),
        in_specs=[pl.BlockSpec(memory_space=pltpu.SMEM)] * 3,
        out_specs=pl.BlockSpec(memory_space=pltpu.VMEM),
        compiler_params=pltpu.CompilerParams(vmem_limit_bytes=2 << 20),
        cost_estimate=pl.CostEstimate(flops=0, bytes_accessed=0, transcendentals=0),
    )(adapter_home, fetch_list, seg_len)


def pack_kernel(groups, home_ref, fetch_ref, shrink_ref, expand_ref, *refs):
    outs, (held, in_sems, out_sems) = refs[:-3], refs[-3:]
    me = lax.axis_index("rep")
    other = 1 - upper(fetch_ref.shape[0])
    per_home, _, depth = shrink_ref.shape
    columns = expand_ref.shape[2] // lax.axis_size("tp")
    left = pl.multiple_of(lax.axis_index("tp") * columns, 128)
    cuts = in_sems.shape[1] - 1
    width = depth // cuts
    arriving = []
    for at, group in enumerate(groups):
        slot = slot_for(me ^ step_of(group, other), me, per_home, home_ref, fetch_ref)
        pieces = [(shrink_ref.at[slot, :, pl.ds(n * width, width)], n * width, width) for n in range(cuts)]
        pieces.append((expand_ref.at[slot, :, pl.ds(left, columns)], depth, columns))
        for n, (source, start, size) in enumerate(pieces):
            target = held.at[at, :, pl.ds(start, size)]
            copy = pltpu.make_async_copy(source, target, in_sems.at[at, n])
            copy.start()
            leave = pltpu.make_async_copy(target, outs[at].at[:, pl.ds(start, size)], out_sems.at[at, n])
            arriving.append((copy, leave))
    for copy, leave in arriving:
        copy.wait()
        leave.start()
    for _, leave in arriving:
        leave.wait()


def pack(groups, columns, adapter_home, fetch_list, panels, expand_panels):
    rank, depth = panels.shape[1:]
    shape = (rank, depth + columns)
    cuts = 2
    return list(
        pl.pallas_call(
            functools.partial(pack_kernel, groups),
            out_shape=[jax.ShapeDtypeStruct(shape, panels.dtype)] * len(groups),
            in_specs=[pl.BlockSpec(memory_space=pltpu.SMEM)] * 2 + [pl.BlockSpec(memory_space=pl.ANY)] * 2,
            out_specs=[pl.BlockSpec(memory_space=pl.ANY)] * len(groups),
            scratch_shapes=[pltpu.VMEM((len(groups),) + shape, panels.dtype)]
            + [pltpu.SemaphoreType.DMA((len(groups), cuts + 1))] * 2,
            compiler_params=pltpu.CompilerParams(vmem_limit_bytes=56 << 20),
            cost_estimate=pl.CostEstimate(flops=0, bytes_accessed=0, transcendentals=0),
        )(adapter_home, fetch_list, panels, expand_panels)
    )


def score_kernel(plan, groups, kept, chunks, has_prior, replicas, *refs):
    sets, many = len(plan), len(groups)
    row_steps, refs = refs[:sets], refs[sets:]
    prior, refs = (refs[0], refs[1:]) if has_prior else (None, refs)
    tokens, panels = refs[:sets], refs[sets : sets + many]
    out, out_expand = refs[sets + many :]
    rank, (count, depth) = out.shape[0], tokens[0].shape
    for i, n in enumerate(kept):
        out_expand[pl.ds(i * rank, rank), :] = panels[n][:, pl.ds(depth, out_expand.shape[1])]
    high = upper(replicas)
    width = depth // chunks
    sums = [None] * sets
    for c in range(chunks):
        cols = pl.ds(c * width, width)
        for t, used in enumerate(plan):
            product = lax.dot_general(
                jnp.concatenate([panels[n][:, cols] for n in used], axis=0),
                tokens[t][:, cols],
                (((1,), (1,)), ((), ())),
                preferred_element_type=jnp.float32,
            )
            sums[t] = product if c == 0 else sums[t] + product
    for t, used in enumerate(plan):
        mine = row_steps[t][pl.ds(0, 1), :]
        total = prior[...] if has_prior and t == 0 else jnp.zeros((rank, count), jnp.float32)
        for n, panel in enumerate(used):
            term = sums[t][n * rank : (n + 1) * rank]
            total = total + jnp.where(mine == step_of(groups[panel], high), term, 0.0)
        out[:, pl.ds(t * count, count)] = total


def score(plan, groups, kept, columns, row_steps, tokens_of, panels, prior=None):
    count, depth = tokens_of[0].shape
    rank = panels[0].shape[0]
    chunks = 2
    prior = [] if prior is None else [prior]
    vmem = pl.BlockSpec(memory_space=pltpu.VMEM)
    outs = [(rank, len(plan) * count), (len(kept) * rank, columns)]
    arrays = list(row_steps) + prior + list(tokens_of) + list(panels)
    need = 4 * len(plan) * count * (rank * len(panels) + depth) + 4 * len(panels) * rank * (depth + columns)
    return pl.pallas_call(
        functools.partial(
            score_kernel, plan, groups, kept, chunks, bool(prior), lax.axis_size("rep")
        ),
        out_shape=[
            jax.ShapeDtypeStruct(shape, panels[0].dtype if n else jnp.float32)
            for n, shape in enumerate(outs)
        ],
        in_specs=[vmem] * len(arrays),
        out_specs=[vmem] * len(outs),
        compiler_params=pltpu.CompilerParams(vmem_limit_bytes=need + (2 << 20)),
        cost_estimate=pl.CostEstimate(flops=0, bytes_accessed=0, transcendentals=0),
    )(*arrays)


def base_kernel(chunks, tokens_ref, weight_ref, *refs):
    outs, (held_tokens, held_weight, sems) = refs[:-3], refs[-3:]
    cores, half = len(outs), lax.axis_index("tp")
    columns = outs[0].shape[1]
    height = tokens_ref.shape[1] // chunks
    copies = []
    for c in range(chunks):
        rows = pl.ds(c * height, height)
        pairs = [(tokens_ref.at[:, rows], held_tokens.at[:, rows])]
        for shift in range(cores):
            left = pl.multiple_of(lax.rem(half + shift, cores) * columns, 128)
            pairs.append((weight_ref.at[rows, pl.ds(left, columns)], held_weight.at[shift, rows, :]))
        copies.append([])
        for n, (source, target) in enumerate(pairs):
            copies[-1].append(pltpu.make_async_copy(source, target, sems.at[c, n]))
            copies[-1][-1].start()
    for c in range(chunks):
        for copy in copies[c]:
            copy.wait()
        rows = pl.ds(c * height, height)
        for shift, out in enumerate(outs):
            product = jnp.dot(
                held_tokens[:, rows], held_weight[shift, rows, :], preferred_element_type=jnp.float32
            )
            if c == 0:
                out[...] = product
            else:
                out[...] += product


def base_terms(tokens, weight, cores):
    count, depth = tokens.shape
    columns = weight.shape[1] // cores
    chunks = 4
    return list(
        pl.pallas_call(
            functools.partial(base_kernel, chunks),
            out_shape=[jax.ShapeDtypeStruct((count, columns), jnp.float32)] * cores,
            in_specs=[pl.BlockSpec(memory_space=pl.ANY)] * 2,
            out_specs=[pl.BlockSpec(memory_space=pltpu.VMEM)] * cores,
            scratch_shapes=[
                pltpu.VMEM((count, depth), tokens.dtype),
                pltpu.VMEM((cores, depth, columns), weight.dtype),
                pltpu.SemaphoreType.DMA((chunks, 1 + cores)),
            ],
            compiler_params=pltpu.CompilerParams(vmem_limit_bytes=20 << 20),
            cost_estimate=pl.CostEstimate(flops=0, bytes_accessed=0, transcendentals=0),
        )(tokens, weight)
    )


def end_kernel(pieces, added, bases, replicas, row_steps, *refs):
    scores, base, refs = refs[:added], refs[added : added + bases], refs[added + bases :]
    arrays, out = refs[:-1], refs[-1]
    count, columns = out.shape
    rank = scores[0].shape[0]
    expand = jnp.concatenate(
        [
            arrays[at][pl.ds(row, rank), pl.ds(arrays[at].shape[1] - columns, columns)]
            for at, row, _ in pieces
        ],
        axis=0,
    )
    shrink = scores[0][:, pl.ds(0, count)]
    for x in scores[1:]:
        shrink = shrink + x[:, pl.ds(0, count)]
    shrink = adapter_scale * shrink
    high = shrink.astype(jnp.bfloat16).astype(jnp.float32)
    place = upper(replicas)
    masks = [row_steps[pl.ds(0, 1), :] == step_of(group, place) for _, _, group in pieces]
    total = base[0][...]
    for x in base[1:]:
        total = total + x[...]
    for term in (high, shrink - high):
        wide = jnp.concatenate([jnp.where(mask, term, 0.0) for mask in masks], axis=0)
        total = total + lax.dot_general(
            wide.astype(jnp.bfloat16),
            expand,
            (((0,), (0,)), ((), ())),
            preferred_element_type=jnp.float32,
        )
    out[...] = total.astype(out.dtype)


def end(pieces, row_steps, scores, base, arrays, kind, cost):
    count, columns = base[0].shape
    vmem = pl.BlockSpec(memory_space=pltpu.VMEM)
    return pl.pallas_call(
        functools.partial(end_kernel, pieces, len(scores), len(base), lax.axis_size("rep")),
        out_shape=jax.ShapeDtypeStruct((count, columns), kind),
        in_specs=[vmem] * (1 + len(scores) + len(base) + len(arrays)),
        out_specs=vmem,
        compiler_params=pltpu.CompilerParams(vmem_limit_bytes=16 << 20),
        cost_estimate=pl.CostEstimate(flops=0, bytes_accessed=cost, transcendentals=0),
    )(row_steps, *scores, *base, *arrays)


def on_device(tokens, base_weight, shrink_panels, expand_panels, adapter_home, fetch_list, seg_len):
    replicas, parts, cores = lax.axis_size("rep"), lax.axis_size("parts"), lax.axis_size("tp")
    tok_count = tokens.shape[0]
    columns = expand_panels.shape[2] // cores
    panels = jnp.swapaxes(shrink_panels, 1, 2)
    rank = panels.shape[1]
    tie = lax.optimization_barrier

    half = replicas // 2
    far = [(tuple(range(step, step + parts))[::-1], True) for step in range(half, replicas, parts)]
    size = half // parts - 1
    near = [(tuple(parts + p * size + g for p in reversed(range(parts))), False) for g in range(size)]
    near.append((tuple(range(parts)), False))

    def hop(x, group):
        steps, moves = group
        pairs = []
        for p in range(parts):
            for i in range(replicas):
                step = steps[(p + (moves and i >= half)) % parts]
                pairs.append((p * replicas + (i ^ step), p * replicas + i))
        return lax.ppermute(x, ("parts", "rep"), pairs)

    def shift_parts(x, shift):
        return lax.ppermute(x, "parts", [(i, (i + shift) % parts) for i in range(parts)])

    def shift_cores(x, shift):
        return lax.ppermute(x, "tp", [(i, (i + shift) % cores) for i in range(cores)])

    tables = (adapter_home, fetch_list, panels, expand_panels)
    groups = far + near
    send = pack(groups, columns, *tables)
    tokens, send = tie((tokens, send))
    recv = [hop(x, group) for x, group in zip(send, groups)]
    tokens_of = [tokens] + [shift_parts(tokens, shift) for shift in range(1, parts)]
    base = base_terms(tokens, base_weight, cores)
    base, recv[: len(far) - 1] = tie((base, recv[: len(far) - 1]))
    base = base[:1] + [shift_cores(x, shift + 1) for shift, x in enumerate(base[1:])]
    row_steps = steps_of_rows(tok_count, panels.shape[0], adapter_home, fetch_list, seg_len)
    steps_of = [row_steps] + [shift_parts(row_steps, shift) for shift in range(1, parts)]
    early, early_groups = recv[len(far) :] + recv[: len(far) - 1], near + far[:-1]
    last, last_group = recv[len(far) - 1], far[-1]

    count = len(early)
    first, sent = score(
        [tuple(range(count))],
        early_groups,
        tuple(range(count)),
        columns,
        steps_of[:1],
        [tokens],
        early,
    )
    passed = [shift_parts(sent, shift) for shift in range(1, parts)]
    base, first, passed, tokens_of[1:], last = tie((base, first, passed, tokens_of[1:], last))
    scores, sent = score(
        [(0,)] + [tuple(range(count + 1))] * (parts - 1),
        [last_group] + early_groups,
        (0,),
        columns,
        steps_of,
        tokens_of,
        [last] + early,
        first,
    )
    last_passed = [shift_parts(sent, shift) for shift in range(1, parts)]
    halves = [scores] + [shift_cores(scores, shift) for shift in range(1, cores)]
    whole = halves[0]
    for x in halves[1:]:
        whole = whole + x
    came = [
        shift_parts(whole[:, shift * tok_count : (shift + 1) * tok_count], -shift)
        for shift in range(1, parts)
    ]
    pieces = [(n, 0, group) for n, group in enumerate(early_groups + [last_group])]
    result = end(pieces, row_steps, halves, base, early + [last], jnp.float32, 1 << 24)
    pieces = []
    for shift in range(1, parts):
        at = shift - 1
        pieces += [(at, n * rank, turned(group, shift)) for n, group in enumerate(early_groups)]
        pieces.append((at + parts - 1, 0, turned(last_group, shift)))
    return end(pieces, row_steps, came, [result], passed + last_passed, jnp.bfloat16, 0)


def solution(mesh):
    return jax.shard_map(
        on_device,
        mesh=mesh,
        in_specs=(
            P(("parts", "rep"), "tp"),
            P("tp", None),
            P("rep", "tp", None),
            P("rep", None, None),
            P(),
            P(),
            P(("parts", "rep"), None),
        ),
        out_specs=P(("parts", "rep"), "tp"),
        check_vma=False,
    )
```

```python
import functools
import jax
import jax.numpy as jnp
from jax import lax
from jax.experimental import pallas as pl
from jax.experimental.pallas import tpu as pltpu
from jax.sharding import PartitionSpec as P

adapter_scale = 2.0


def upper(replicas):
    return (lax.axis_index("rep") >= replicas // 2).astype(jnp.int32)


def step_of(group, high):
    steps, moves = group
    part = lax.axis_index("parts")
    if moves:
        part = lax.rem(part + high, jnp.int32(len(steps)))
    chosen = jnp.int32(steps[0])
    for p, step in enumerate(steps):
        chosen = jnp.where(part == p, step, chosen)
    return chosen


def turned(group, shift):
    steps, moves = group
    return (tuple(steps[(p - shift) % len(steps)] for p in range(len(steps))), moves)


def slot_for(peer, me, per_home, home_ref, fetch_ref):
    first = me * per_home

    def look(j, slot):
        local = home_ref[fetch_ref[peer, j]] - first
        return jnp.where((local >= 0) & (local < per_home), local, slot)

    listed = fetch_ref.shape[1]
    return lax.fori_loop(0, listed, look, jnp.int32(0), unroll=listed <= 8)


def steps_kernel(per_home, home_ref, fetch_ref, lengths_ref, out):
    me = lax.axis_index("rep")
    rows = lax.broadcasted_iota(jnp.int32, out.shape, 1)
    result = jnp.zeros(out.shape, jnp.int32)
    start = jnp.int32(0)
    for j in range(fetch_ref.shape[1]):
        step = lax.div(home_ref[fetch_ref[me, j]], jnp.int32(per_home)) ^ me
        result = jnp.where(rows >= start, step, result)
        start = start + lengths_ref[0, j]
    out[...] = result


def steps_of_rows(count, per_home, adapter_home, fetch_list, seg_len):
    return pl.pallas_call(
        functools.partial(steps_kernel, per_home),
        out_shape=jax.ShapeDtypeStruct((8, count), jnp.int32),
        in_specs=[pl.BlockSpec(memory_space=pltpu.SMEM)] * 3,
        out_specs=pl.BlockSpec(memory_space=pltpu.VMEM),
        compiler_params=pltpu.CompilerParams(vmem_limit_bytes=2 << 20),
        cost_estimate=pl.CostEstimate(flops=0, bytes_accessed=0, transcendentals=0),
    )(adapter_home, fetch_list, seg_len)


def pack_kernel(groups, home_ref, fetch_ref, shrink_ref, expand_ref, *refs):
    outs, (held, in_sems, out_sems) = refs[:-3], refs[-3:]
    me = lax.axis_index("rep")
    other = 1 - upper(fetch_ref.shape[0])
    per_home, _, depth = shrink_ref.shape
    columns = expand_ref.shape[2] // lax.axis_size("tp")
    left = pl.multiple_of(lax.axis_index("tp") * columns, 128)
    cuts = in_sems.shape[1] - 1
    width = depth // cuts
    arriving = []
    for at, group in enumerate(groups):
        slot = slot_for(me ^ step_of(group, other), me, per_home, home_ref, fetch_ref)
        pieces = [(shrink_ref.at[slot, :, pl.ds(n * width, width)], n * width, width) for n in range(cuts)]
        pieces.append((expand_ref.at[slot, :, pl.ds(left, columns)], depth, columns))
        for n, (source, start, size) in enumerate(pieces):
            target = held.at[at, :, pl.ds(start, size)]
            copy = pltpu.make_async_copy(source, target, in_sems.at[at, n])
            copy.start()
            leave = pltpu.make_async_copy(target, outs[at].at[:, pl.ds(start, size)], out_sems.at[at, n])
            arriving.append((copy, leave))
    for copy, leave in arriving:
        copy.wait()
        leave.start()
    for _, leave in arriving:
        leave.wait()


def pack(groups, columns, adapter_home, fetch_list, panels, expand_panels):
    rank, depth = panels.shape[1:]
    shape = (rank, depth + columns)
    cuts = 2
    return list(
        pl.pallas_call(
            functools.partial(pack_kernel, groups),
            out_shape=[jax.ShapeDtypeStruct(shape, panels.dtype)] * len(groups),
            in_specs=[pl.BlockSpec(memory_space=pltpu.SMEM)] * 2 + [pl.BlockSpec(memory_space=pl.ANY)] * 2,
            out_specs=[pl.BlockSpec(memory_space=pl.ANY)] * len(groups),
            scratch_shapes=[pltpu.VMEM((len(groups),) + shape, panels.dtype)]
            + [pltpu.SemaphoreType.DMA((len(groups), cuts + 1))] * 2,
            compiler_params=pltpu.CompilerParams(vmem_limit_bytes=56 << 20),
            cost_estimate=pl.CostEstimate(flops=0, bytes_accessed=0, transcendentals=0),
        )(adapter_home, fetch_list, panels, expand_panels)
    )


def score_kernel(plan, groups, kept, chunks, has_prior, replicas, *refs):
    sets, many = len(plan), len(groups)
    row_steps, refs = refs[:sets], refs[sets:]
    prior, refs = (refs[0], refs[1:]) if has_prior else (None, refs)
    tokens, panels = refs[:sets], refs[sets : sets + many]
    out, out_expand = refs[sets + many :]
    rank, (count, depth) = out.shape[0], tokens[0].shape
    for i, n in enumerate(kept):
        out_expand[pl.ds(i * rank, rank), :] = panels[n][:, pl.ds(depth, out_expand.shape[1])]
    high = upper(replicas)
    width = depth // chunks
    sums = [None] * sets
    for c in range(chunks):
        cols = pl.ds(c * width, width)
        for t, used in enumerate(plan):
            product = lax.dot_general(
                jnp.concatenate([panels[n][:, cols] for n in used], axis=0),
                tokens[t][:, cols],
                (((1,), (1,)), ((), ())),
                preferred_element_type=jnp.float32,
            )
            sums[t] = product if c == 0 else sums[t] + product
    for t, used in enumerate(plan):
        mine = row_steps[t][pl.ds(0, 1), :]
        total = prior[...] if has_prior and t == 0 else jnp.zeros((rank, count), jnp.float32)
        for n, panel in enumerate(used):
            term = sums[t][n * rank : (n + 1) * rank]
            total = total + jnp.where(mine == step_of(groups[panel], high), term, 0.0)
        out[:, pl.ds(t * count, count)] = total


def score(plan, groups, kept, columns, row_steps, tokens_of, panels, prior=None):
    count, depth = tokens_of[0].shape
    rank = panels[0].shape[0]
    chunks = 1
    prior = [] if prior is None else [prior]
    vmem = pl.BlockSpec(memory_space=pltpu.VMEM)
    outs = [(rank, len(plan) * count), (len(kept) * rank, columns)]
    arrays = list(row_steps) + prior + list(tokens_of) + list(panels)
    need = 4 * len(plan) * count * (rank * len(panels) + depth) + 4 * len(panels) * rank * (depth + columns)
    return pl.pallas_call(
        functools.partial(
            score_kernel, plan, groups, kept, chunks, bool(prior), lax.axis_size("rep")
        ),
        out_shape=[
            jax.ShapeDtypeStruct(shape, panels[0].dtype if n else jnp.float32)
            for n, shape in enumerate(outs)
        ],
        in_specs=[vmem] * len(arrays),
        out_specs=[vmem] * len(outs),
        compiler_params=pltpu.CompilerParams(vmem_limit_bytes=need + (2 << 20)),
        cost_estimate=pl.CostEstimate(flops=0, bytes_accessed=0, transcendentals=0),
    )(*arrays)


def base_kernel(chunks, tokens_ref, weight_ref, *refs):
    outs, (held_tokens, held_weight, sems) = refs[:-3], refs[-3:]
    cores, half = len(outs), lax.axis_index("tp")
    columns = outs[0].shape[1]
    height = tokens_ref.shape[1] // chunks
    copies = []
    for c in range(chunks):
        rows = pl.ds(c * height, height)
        pairs = [(tokens_ref.at[:, rows], held_tokens.at[:, rows])]
        for shift in range(cores):
            left = pl.multiple_of(lax.rem(half + shift, cores) * columns, 128)
            pairs.append((weight_ref.at[rows, pl.ds(left, columns)], held_weight.at[shift, rows, :]))
        copies.append([])
        for n, (source, target) in enumerate(pairs):
            copies[-1].append(pltpu.make_async_copy(source, target, sems.at[c, n]))
            copies[-1][-1].start()
    for c in range(chunks):
        for copy in copies[c]:
            copy.wait()
        rows = pl.ds(c * height, height)
        for shift, out in enumerate(outs):
            product = jnp.dot(
                held_tokens[:, rows], held_weight[shift, rows, :], preferred_element_type=jnp.float32
            )
            if c == 0:
                out[...] = product
            else:
                out[...] += product


def base_terms(tokens, weight, cores):
    count, depth = tokens.shape
    columns = weight.shape[1] // cores
    chunks = 4
    return list(
        pl.pallas_call(
            functools.partial(base_kernel, chunks),
            out_shape=[jax.ShapeDtypeStruct((count, columns), jnp.float32)] * cores,
            in_specs=[pl.BlockSpec(memory_space=pl.ANY)] * 2,
            out_specs=[pl.BlockSpec(memory_space=pltpu.VMEM)] * cores,
            scratch_shapes=[
                pltpu.VMEM((count, depth), tokens.dtype),
                pltpu.VMEM((cores, depth, columns), weight.dtype),
                pltpu.SemaphoreType.DMA((chunks, 1 + cores)),
            ],
            compiler_params=pltpu.CompilerParams(vmem_limit_bytes=20 << 20),
            cost_estimate=pl.CostEstimate(flops=0, bytes_accessed=0, transcendentals=0),
        )(tokens, weight)
    )


def end_kernel(pieces, added, bases, replicas, row_steps, *refs):
    scores, base, refs = refs[:added], refs[added : added + bases], refs[added + bases :]
    arrays, out = refs[:-1], refs[-1]
    count, columns = out.shape
    rank = scores[0].shape[0]
    expand = jnp.concatenate(
        [
            arrays[at][pl.ds(row, rank), pl.ds(arrays[at].shape[1] - columns, columns)]
            for at, row, _ in pieces
        ],
        axis=0,
    )
    shrink = scores[0][:, pl.ds(0, count)]
    for x in scores[1:]:
        shrink = shrink + x[:, pl.ds(0, count)]
    shrink = adapter_scale * shrink
    high = shrink.astype(jnp.bfloat16).astype(jnp.float32)
    place = upper(replicas)
    masks = [row_steps[pl.ds(0, 1), :] == step_of(group, place) for _, _, group in pieces]
    total = base[0][...]
    for x in base[1:]:
        total = total + x[...]
    for term in (high, shrink - high):
        wide = jnp.concatenate([jnp.where(mask, term, 0.0) for mask in masks], axis=0)
        total = total + lax.dot_general(
            wide.astype(jnp.bfloat16),
            expand,
            (((0,), (0,)), ((), ())),
            preferred_element_type=jnp.float32,
        )
    out[...] = total.astype(out.dtype)


def end(pieces, row_steps, scores, base, arrays, kind, cost):
    count, columns = base[0].shape
    vmem = pl.BlockSpec(memory_space=pltpu.VMEM)
    return pl.pallas_call(
        functools.partial(end_kernel, pieces, len(scores), len(base), lax.axis_size("rep")),
        out_shape=jax.ShapeDtypeStruct((count, columns), kind),
        in_specs=[vmem] * (1 + len(scores) + len(base) + len(arrays)),
        out_specs=vmem,
        compiler_params=pltpu.CompilerParams(vmem_limit_bytes=16 << 20),
        cost_estimate=pl.CostEstimate(flops=0, bytes_accessed=cost, transcendentals=0),
    )(row_steps, *scores, *base, *arrays)


def on_device(tokens, base_weight, shrink_panels, expand_panels, adapter_home, fetch_list, seg_len):
    replicas, parts, cores = lax.axis_size("rep"), lax.axis_size("parts"), lax.axis_size("tp")
    tok_count = tokens.shape[0]
    columns = expand_panels.shape[2] // cores
    panels = jnp.swapaxes(shrink_panels, 1, 2)
    rank = panels.shape[1]
    tie = lax.optimization_barrier

    half = replicas // 2
    far = [(tuple(range(step, step + parts))[::-1], True) for step in range(half, replicas, parts)]
    size = half // parts - 1
    near = [(tuple(parts + p * size + g for p in reversed(range(parts))), False) for g in range(size)]
    near.append((tuple(range(parts)), False))

    def hop(x, group):
        steps, moves = group
        pairs = []
        for p in range(parts):
            for i in range(replicas):
                step = steps[(p + (moves and i >= half)) % parts]
                pairs.append((p * replicas + (i ^ step), p * replicas + i))
        return lax.ppermute(x, ("parts", "rep"), pairs)

    def shift_parts(x, shift):
        return lax.ppermute(x, "parts", [(i, (i + shift) % parts) for i in range(parts)])

    def shift_cores(x, shift):
        return lax.ppermute(x, "tp", [(i, (i + shift) % cores) for i in range(cores)])

    tables = (adapter_home, fetch_list, panels, expand_panels)
    groups = far + near
    send = pack(groups, columns, *tables)
    tokens, send = tie((tokens, send))
    recv = [hop(x, group) for x, group in zip(send, groups)]
    tokens_of = [tokens] + [shift_parts(tokens, shift) for shift in range(1, parts)]
    base = base_terms(tokens, base_weight, cores)
    base, recv[: len(far) - 1] = tie((base, recv[: len(far) - 1]))
    base = base[:1] + [shift_cores(x, shift + 1) for shift, x in enumerate(base[1:])]
    row_steps = steps_of_rows(tok_count, panels.shape[0], adapter_home, fetch_list, seg_len)
    steps_of = [row_steps] + [shift_parts(row_steps, shift) for shift in range(1, parts)]
    early, early_groups = recv[len(far) :] + recv[: len(far) - 1], near + far[:-1]
    last, last_group = recv[len(far) - 1], far[-1]

    count = len(early)
    first, sent = score(
        [tuple(range(count))],
        early_groups,
        tuple(range(count)),
        columns,
        steps_of[:1],
        [tokens],
        early,
    )
    passed = [shift_parts(sent, shift) for shift in range(1, parts)]
    base, first, passed, tokens_of[1:], last = tie((base, first, passed, tokens_of[1:], last))
    scores, sent = score(
        [(0,)] + [tuple(range(count + 1))] * (parts - 1),
        [last_group] + early_groups,
        (0,),
        columns,
        steps_of,
        tokens_of,
        [last] + early,
        first,
    )
    last_passed = [shift_parts(sent, shift) for shift in range(1, parts)]
    halves = [scores] + [shift_cores(scores, shift) for shift in range(1, cores)]
    whole = halves[0]
    for x in halves[1:]:
        whole = whole + x
    came = [
        shift_parts(whole[:, shift * tok_count : (shift + 1) * tok_count], -shift)
        for shift in range(1, parts)
    ]
    pieces = [(n, 0, group) for n, group in enumerate(early_groups + [last_group])]
    result = end(pieces, row_steps, halves, base, early + [last], jnp.float32, 1 << 24)
    pieces = []
    for shift in range(1, parts):
        at = shift - 1
        pieces += [(at, n * rank, turned(group, shift)) for n, group in enumerate(early_groups)]
        pieces.append((at + parts - 1, 0, turned(last_group, shift)))
    return end(pieces, row_steps, came, [result], passed + last_passed, jnp.bfloat16, 0)


def solution(mesh):
    return jax.shard_map(
        on_device,
        mesh=mesh,
        in_specs=(
            P(("parts", "rep"), "tp"),
            P("tp", None),
            P("rep", "tp", None),
            P("rep", None, None),
            P(),
            P(),
            P(("parts", "rep"), None),
        ),
        out_specs=P(("parts", "rep"), "tp"),
        check_vma=False,
    )
```
